32 devices in a mesh: energy: 8 (over z, y), slab: 4 (over x, core).
Axes of the slice: x: 2, y: 2, z: 4, core: 2. Of those that a mesh axis runs over, the one named last changes fastest.
Arguments:
- lesser: bfloat16 [8, 4, 2, 1024, 1024], P('energy', 'slab'), may hold values from -6 to 6
- greater_diag: float32 [8, 4, 1024], P('energy', 'slab'), may hold values from -6 to 6
- dipole: bfloat16 [4, 1024, 1024], P('slab'), may hold values from -0.1875 to 0.1875
- photon_weights: float32 [8, 3], P('energy'), may hold values from 0.2 to 1
- sidebands: int32 [8], P('energy'), may hold values from 1 to 2
- phonon_lags: int32 [6], replicated, may hold values from 1 to 3
- phonon_strengths: float32 [2, 6], replicated, may hold values from 0.3 to 1.5
- slab_coupling: float32 [4, 1024], P('slab'), may hold values from 0.3 to 1
Outputs:
- lesser_self: bfloat16 [8, 4, 2, 1024, 1024], P('energy', 'slab')
- greater_phonon: float32 [8, 4, 1024], P('energy', 'slab')
The draws below stay inside these ranges and needn't reach their ends.
All inputs are finite; a program needn't handle non-finite values.
Results may differ from the reference program's by a relative error of at most 0.0057.
Values may be sent and summed in bfloat16 or wider, within the bound.
No kernel may reach another device: no remote copies, remote signals or barrier semaphores. Data moves between devices by JAX's collectives and lax.ppermute only.
A program may use at most 64 MiB of HBM per device.

```python
import math
import jax
import jax.numpy as jnp
from jax import lax

NORB = 1024
MODES = 6
NE = 8
PHOT = 3
SLABS = 4


def plant(result, key, low, top_value):
    longest = result.shape.index(max(result.shape))
    spots = []
    for shift in (0, 1):
        where = [jax.random.randint(jax.random.fold_in(key, axis), (), 0, length) for axis, length in enumerate(result.shape)]
        where[longest] = (where[longest] + shift) % result.shape[longest]
        spots.append(tuple(where))
    return result.at[spots[0]].set(low).at[spots[1]].set(top_value)


def levels(key, extent, pieces, least, largest):
    def one(position, blocks):
        draws = jax.random.uniform(jax.random.fold_in(jax.random.fold_in(key, 6), position), (blocks,), jnp.float32, least / len(pieces), largest / len(pieces))
        return jnp.repeat(jnp.exp(draws), extent[position] // blocks).reshape((-1,) + (1,) * (len(extent) - position - 1))

    loudness = one(*pieces[0])
    for cut in pieces[1:]:
        loudness = loudness * one(*cut)
    return loudness


def normal_values(own_key, extent, deviation, bound, split=(), kind=jnp.bfloat16):
    drawn = deviation * jax.random.normal(own_key, extent, jnp.float32)
    if split:
        drawn = drawn * levels(own_key, extent, split, -0.22, 0.18)
    return jnp.clip(drawn, -bound, bound).astype(kind)


def setup_inputs(seed: int = 0) -> dict:
    splits = jax.random.split(jax.random.key(seed), 9)
    lesser = normal_values(splits[0], (NE, SLABS, 2, NORB, NORB), 1.0, 6.0, ((0, 8), (1, 4)))
    greater_diag = normal_values(splits[1], (NE, SLABS, NORB), 1.0, 6.0, ((0, 8), (1, 4)), jnp.float32)
    dipole = normal_values(splits[2], (SLABS, NORB, NORB), NORB ** -0.5, 0.1875, ((0, 4),))
    photon_weights = jnp.clip(jnp.exp(math.log(1.0) - 1.609438 * jax.random.uniform(splits[3], (NE, 3), jnp.float32) ** levels(splits[3], (NE, 3), ((0, 8),), -0.2, 0.2)), 0.2, 1.0)
    sidebands = plant(jax.random.randint(splits[4], (NE,), 1, 3), jax.random.fold_in(splits[4], 1), 1, 2).astype(jnp.int32)
    phonon_lags = plant(jax.random.randint(splits[5], (MODES,), 1, NE // 2), jax.random.fold_in(splits[5], 1), 1, (NE // 2) - 1).astype(jnp.int32)
    phonon_strengths = jnp.clip(jnp.exp(jax.random.uniform(splits[6], (2, MODES), jnp.float32, math.log(0.3), math.log(1.5))), 0.3, 1.5)
    slab_coupling = jnp.clip(jnp.exp(math.log(1.0) - 1.2039728 * jax.random.uniform(splits[7], (SLABS, NORB), jnp.float32) ** levels(splits[7], (SLABS, NORB), ((0, 4),), -0.2, 0.2)), 0.3, 1.0)
    return {"lesser": lesser, "greater_diag": greater_diag, "dipole": dipole, "photon_weights": photon_weights, "sidebands": sidebands, "phonon_lags": phonon_lags, "phonon_strengths": phonon_strengths, "slab_coupling": slab_coupling}


def kernel(rows, cols, phonon_lags, first, second):
    offset = cols[None, :] - rows[:, None]
    upward = (offset[None, :, :] == phonon_lags[:, None, None]).astype(jnp.float32)
    downward = (offset[None, :, :] == -phonon_lags[:, None, None]).astype(jnp.float32)
    return jnp.sum(first[:, None, None] * upward + second[:, None, None] * downward, axis=0)


def couple(values, slab_coupling):
    scaled = slab_coupling[None] * values
    zeros = jnp.zeros_like(values[:, :1])
    below = jnp.concatenate([zeros, scaled[:, :-1]], axis=1)
    above = jnp.concatenate([values[:, 1:], zeros], axis=1)
    return values + below + slab_coupling[None] * above


def reference(lesser, greater_diag, dipole, photon_weights, sidebands, phonon_lags, phonon_strengths, slab_coupling):
    dip_wide = dipole.astype(jnp.float32)
    energies = jnp.arange(NE, dtype=jnp.int32)
    diag_less = jnp.diagonal(lesser[:, :, 1], axis1=-2, axis2=-1).astype(jnp.float32)
    k_less = kernel(energies, energies, phonon_lags, phonon_strengths[0], phonon_strengths[1])
    k_great = kernel(energies, energies, phonon_lags, phonon_strengths[1], phonon_strengths[0])
    corr_less = jnp.einsum('ef,fsn->esn', k_less, diag_less, precision=lax.Precision.HIGHEST)
    corr_great = jnp.einsum('ef,fsn->esn', k_great, greater_diag, precision=lax.Precision.HIGHEST)
    phon_less = couple(corr_less, slab_coupling)
    greater_phonon = couple(corr_great, slab_coupling)

    def left_product(block):
        return jnp.einsum('scij,skj->scik', block.astype(jnp.float32), dip_wide).astype(jnp.bfloat16)

    left = lax.map(left_product, lesser)
    masks = sidebands.astype(jnp.float32)
    eye_mask = (jnp.arange(NORB)[:, None] == jnp.arange(NORB)[None, :]).astype(jnp.float32)

    def per_energy(index):
        own_left = lax.dynamic_index_in_dim(left, index, 0, keepdims=False).astype(jnp.float32)
        lower = lax.dynamic_index_in_dim(left, jnp.maximum(index - PHOT, 0), 0, keepdims=False).astype(jnp.float32)
        upper = lax.dynamic_index_in_dim(left, jnp.minimum(index + PHOT, NE - 1), 0, keepdims=False).astype(jnp.float32)
        lower = jnp.where(index >= PHOT, lower, jnp.zeros_like(lower))
        upper = jnp.where(index + PHOT < NE, upper, jnp.zeros_like(upper))
        weights = lax.dynamic_index_in_dim(photon_weights, index, 0, keepdims=False)
        flag = lax.dynamic_index_in_dim(masks, index, 0, keepdims=False)
        mixed = (weights[0] * own_left + flag * (weights[1] * lower + weights[2] * upper)).astype(jnp.bfloat16)
        photon = jnp.einsum('sij,scjk->scik', dip_wide, mixed.astype(jnp.float32))
        diag_add = lax.dynamic_index_in_dim(phon_less, index, 0, keepdims=False)
        photon = photon.at[:, 1].add(eye_mask[None] * diag_add[:, :, None])
        return photon.astype(jnp.bfloat16)

    lesser_self = lax.map(per_energy, energies)
    return lesser_self, greater_phonon
```

```python
import functools

import jax
import jax.numpy as jnp
from jax import lax
from jax.experimental import pallas as pl
from jax.experimental.pallas import tpu as pltpu
from jax.sharding import PartitionSpec as P

PHOT_BLOCKS = 3
VMEM_BYTES = 48 * 1024 * 1024


def shifted(block, axis, distance):
    devices = range(lax.axis_size(axis))
    route = [(i - distance, i) for i in devices if i - distance in devices]
    return lax.ppermute(block, axis, route)


def lag_kernel(rows, cols, phonon_lags, first, second):
    offset = cols[None, :] - rows[:, None]
    upward = (offset[None, :, :] == phonon_lags[:, None, None]).astype(jnp.float32)
    downward = (offset[None, :, :] == -phonon_lags[:, None, None]).astype(jnp.float32)
    return jnp.sum(first[:, None, None] * upward + second[:, None, None] * downward, axis=0)


def left_body(blocks_ref, dipole_ref, left_ref):
    left_ref[...] = lax.dot_general(
        blocks_ref[...],
        dipole_ref[...],
        (((1,), (1,)), ((), ())),
        preferred_element_type=jnp.float32,
    ).astype(left_ref.dtype)


def left_of(lesser, dipole, part):
    width = lesser.shape[-1]
    rows = width // 4
    return pl.pallas_call(
        left_body,
        grid=(width // rows,),
        in_specs=[
            pl.BlockSpec((None, None, None, rows, width), lambda i: (0, 0, part, i, 0)),
            pl.BlockSpec((None, width, width), lambda i: (0, 0, 0)),
        ],
        out_specs=pl.BlockSpec((rows, width), lambda i: (i, 0)),
        out_shape=jax.ShapeDtypeStruct((width, width), lesser.dtype),
        compiler_params=pltpu.CompilerParams(vmem_limit_bytes=VMEM_BYTES),
        name="left",
    )(lesser, dipole)


def photon_body(part, factors_ref, dipole_ref, own_ref, lower_ref, upper_ref, phonon_ref, *rest):
    out_ref = rest[-1]
    side = factors_ref[1] * lower_ref[...].astype(jnp.float32)
    side += factors_ref[2] * upper_ref[...].astype(jnp.float32)
    mixed = factors_ref[0] * own_ref[...].astype(jnp.float32) + factors_ref[3] * side
    photon = jnp.dot(
        dipole_ref[...], mixed.astype(jnp.bfloat16), preferred_element_type=jnp.float32
    )
    if part == 1:
        height, cols = photon.shape
        row = lax.broadcasted_iota(jnp.int32, (height, cols), 0)
        col = lax.broadcasted_iota(jnp.int32, (height, cols), 1) + pl.program_id(0) * cols
        photon += jnp.where(row == col, phonon_ref[...], 0.0)
    out_ref[...] = photon.astype(out_ref.dtype)


def photon_of(part, factors, dipole, own, lower, upper, phonon, out):
    width = own.shape[-1]
    cols = width // 4
    piece = pl.BlockSpec((width, cols), lambda k: (0, k))
    operands = [factors, dipole, own, lower, upper, phonon]
    in_specs = [
        pl.BlockSpec(memory_space=pltpu.SMEM),
        pl.BlockSpec((None, width, width), lambda k: (0, 0, 0)),
        piece,
        piece,
        piece,
        pl.BlockSpec((1, cols), lambda k: (0, k)),
    ]
    aliases = {}
    if out is not None:
        aliases = {len(operands): 0}
        operands.append(out)
        in_specs.append(pl.BlockSpec(memory_space=pl.ANY))
    return pl.pallas_call(
        functools.partial(photon_body, part),
        grid=(width // cols,),
        in_specs=in_specs,
        out_specs=pl.BlockSpec((None, None, None, width, cols), lambda k: (0, 0, part, 0, k)),
        out_shape=jax.ShapeDtypeStruct((1, 1, 2, width, width), jnp.bfloat16),
        input_output_aliases=aliases,
        compiler_params=pltpu.CompilerParams(vmem_limit_bytes=VMEM_BYTES),
        name="photon",
    )(*operands)


def on_device(
    lesser,
    greater_diag,
    dipole,
    photon_weights,
    sidebands,
    phonon_lags,
    phonon_strengths,
    slab_coupling,
):
    e_count = lesser.shape[0]
    width = lesser.shape[-1]
    total_e = e_count * lax.axis_size("energy")
    own_rows = lax.axis_index("energy") * e_count + jnp.arange(e_count, dtype=jnp.int32)
    all_rows = jnp.arange(total_e, dtype=jnp.int32)

    eye = jnp.arange(width)[:, None] == jnp.arange(width)[None, :]
    diag_less = jnp.sum(jnp.where(eye, lesser[0, 0, 1], 0).astype(jnp.float32), axis=0)
    diags = jnp.stack([diag_less, greater_diag[0, 0]])
    below = shifted(slab_coupling * diags, "slab", 1)
    above = shifted(diags, "slab", -1)
    coupled = diags + below + slab_coupling * above
    everyone = lax.all_gather(coupled, "energy", axis=0)
    k_less = lag_kernel(own_rows, all_rows, phonon_lags, phonon_strengths[0], phonon_strengths[1])
    k_great = lag_kernel(own_rows, all_rows, phonon_lags, phonon_strengths[1], phonon_strengths[0])
    phon_less = jnp.sum(k_less[0][:, None] * everyone[:, 0], axis=0)
    phon_great = jnp.sum(k_great[0][:, None] * everyone[:, 1], axis=0)

    factors = jnp.concatenate([photon_weights[0], sidebands.astype(jnp.float32)])
    out = None
    left, lower, upper = {}, {}, {}
    for part in (0, 1):
        left[part] = left_of(lesser, dipole, part)
        if part == 0:
            left[part], phon_less = lax.optimization_barrier((left[part], phon_less))
        lower[part] = shifted(left[part], "energy", PHOT_BLOCKS)
        upper[part] = shifted(left[part], "energy", -PHOT_BLOCKS)
    for part in (0, 1):
        out = photon_of(
            part, factors, dipole, left[part], lower[part], upper[part], phon_less[None], out
        )
    return out, phon_great[None, None]


def solution(mesh):
    return jax.shard_map(
        on_device,
        mesh=mesh,
        in_specs=(
            P("energy", "slab", None, None, None),
            P("energy", "slab", None),
            P("slab", None, None),
            P("energy", None),
            P("energy"),
            P(),
            P(),
            P("slab", None),
        ),
        out_specs=(P("energy", "slab", None, None, None), P("energy", "slab", None)),
        check_vma=False,
    )
```

```python
import functools

import jax
import jax.numpy as jnp
from jax import lax
from jax.experimental import pallas as pl
from jax.experimental.pallas import tpu as pltpu
from jax.sharding import PartitionSpec as P

PHOT_BLOCKS = 3
CHUNKS = ((0, 0, 2), (1, 0, 1), (1, 1, 1))
VMEM_BYTES = 20 * 1024 * 1024

RELAYS = {8: ((1, 0, 4), (6, 7, 3))}


def pairs_of(count, distance):
    return [(i - distance, i) for i in range(count) if 0 <= i - distance < count]


def shifted(block, axis, distance, without=()):
    route = pairs_of(lax.axis_size(axis), distance)
    return lax.ppermute(block, axis, [pair for pair in route if pair not in without])


def gathered(block, axis):
    count = lax.axis_size(axis)
    if count & (count - 1):
        return lax.all_gather(block, axis, axis=0)
    block = block[None]
    index = lax.axis_index(axis)
    step = 1
    while step < count:
        other = lax.ppermute(block, axis, [(i, i ^ step) for i in range(count)])
        upper = (index & step) != 0
        block = jnp.concatenate(
            [jnp.where(upper, other, block), jnp.where(upper, block, other)], axis=0
        )
        step *= 2
    return block


def lag_kernel(rows, cols, phonon_lags, first, second):
    offset = cols[None, :] - rows[:, None]
    upward = (offset[None, :, :] == phonon_lags[:, None, None]).astype(jnp.float32)
    downward = (offset[None, :, :] == -phonon_lags[:, None, None]).astype(jnp.float32)
    return jnp.sum(first[:, None, None] * upward + second[:, None, None] * downward, axis=0)


def left_body(blocks_ref, dipole_ref, left_ref):
    left_ref[...] = lax.dot_general(
        blocks_ref[...],
        dipole_ref[...],
        (((1,), (1,)), ((), ())),
        preferred_element_type=jnp.float32,
    ).astype(left_ref.dtype)


def left_of(lesser, dipole, chunk):
    part, first, halves = chunk
    width = lesser.shape[-1]
    cols = width // 2 * halves
    rows = width // 4
    return pl.pallas_call(
        left_body,
        grid=(width // rows,),
        in_specs=[
            pl.BlockSpec((None, None, None, rows, width), lambda i: (0, 0, part, i, 0)),
            pl.BlockSpec((None, cols, width), lambda i: (0, first, 0)),
        ],
        out_specs=pl.BlockSpec((rows, cols), lambda i: (i, 0)),
        out_shape=jax.ShapeDtypeStruct((width, cols), lesser.dtype),
        compiler_params=pltpu.CompilerParams(vmem_limit_bytes=VMEM_BYTES),
        name="left",
    )(lesser, dipole)


def photon_body(part, first, n_sides, factors_ref, dipole_ref, phonon_ref, own_ref, *rest):
    out_ref = rest[-1]
    side = factors_ref[2] * rest[0][...].astype(jnp.float32)
    for n in range(1, n_sides):
        side += factors_ref[2 + n] * rest[n][...].astype(jnp.float32)
    mixed = factors_ref[0] * own_ref[...].astype(jnp.float32) + factors_ref[1] * side
    photon = jnp.dot(
        dipole_ref[...], mixed.astype(jnp.bfloat16), preferred_element_type=jnp.float32
    )
    if part == 1:
        height, cols = photon.shape
        row = lax.broadcasted_iota(jnp.int32, (height, cols), 0)
        col = lax.broadcasted_iota(jnp.int32, (height, cols), 1)
        col += (first + pl.program_id(0)) * cols
        photon += jnp.where(row == col, phonon_ref[...], 0.0)
    out_ref[...] = photon.astype(out_ref.dtype)


def photon_of(chunk, factors, dipole, phonon, own, sides, out):
    part, first, _ = chunk
    width = own.shape[0]
    cols = width // 4
    steps = own.shape[1] // cols
    first *= 2
    piece = pl.BlockSpec((width, cols), lambda k: (0, k))
    operands = [factors, dipole, phonon, own, *sides]
    in_specs = [
        pl.BlockSpec(memory_space=pltpu.SMEM),
        pl.BlockSpec((None, width, width), lambda k: (0, 0, 0)),
        pl.BlockSpec((1, cols), lambda k: (0, first + k)),
        piece,
        *(piece for _ in sides),
    ]
    aliases = {}
    if out is not None:
        aliases = {len(operands): 0}
        operands.append(out)
        in_specs.append(pl.BlockSpec(memory_space=pl.ANY))
    return pl.pallas_call(
        functools.partial(photon_body, part, first, len(sides)),
        grid=(steps,),
        in_specs=in_specs,
        out_specs=pl.BlockSpec(
            (None, None, None, width, cols), lambda k: (0, 0, part, 0, first + k)
        ),
        out_shape=jax.ShapeDtypeStruct((1, 1, 2, width, width), jnp.bfloat16),
        input_output_aliases=aliases,
        compiler_params=pltpu.CompilerParams(vmem_limit_bytes=VMEM_BYTES),
        name="photon",
    )(*operands)


def on_device(
    lesser,
    greater_diag,
    dipole,
    photon_weights,
    sidebands,
    phonon_lags,
    phonon_strengths,
    slab_coupling,
):
    e_count = lesser.shape[0]
    width = lesser.shape[-1]
    count = lax.axis_size("energy")
    own = lax.axis_index("energy")
    relays = RELAYS.get(count, ())

    left = [left_of(lesser, dipole, chunk) for chunk in CHUNKS]
    around = tuple((source, target) for source, _, target in relays)
    if relays:
        relay = lax.ppermute(left[0], "energy", [(source, by) for source, by, _ in relays])
    lower = [shifted(left[0], "energy", PHOT_BLOCKS, around)]
    upper = [shifted(left[0], "energy", -PHOT_BLOCKS, around)]
    lower.append(shifted(left[1], "energy", PHOT_BLOCKS))
    upper.append(shifted(left[1], "energy", -PHOT_BLOCKS))

    eye = jnp.arange(width)[:, None] == jnp.arange(width)[None, :]
    diag_less = jnp.sum(jnp.where(eye, lesser[0, 0, 1], 0).astype(jnp.float32), axis=0)
    diags = jnp.stack([diag_less, greater_diag[0, 0]])
    below = shifted(slab_coupling * diags, "slab", 1)
    above = shifted(diags, "slab", -1)
    coupled = diags + below + slab_coupling * above
    everyone = gathered(coupled, "energy")

    if relays:
        relay, left, everyone = lax.optimization_barrier((relay, left, everyone))
        relay = lax.ppermute(relay, "energy", [(by, target) for _, by, target in relays])
    left[2], lower[0], upper[0] = lax.optimization_barrier((left[2], lower[0], upper[0]))
    lower.append(shifted(left[2], "energy", PHOT_BLOCKS))
    upper.append(shifted(left[2], "energy", -PHOT_BLOCKS))

    own_rows = own * e_count + jnp.arange(e_count, dtype=jnp.int32)
    all_rows = jnp.arange(e_count * count, dtype=jnp.int32)
    k_less = lag_kernel(own_rows, all_rows, phonon_lags, phonon_strengths[0], phonon_strengths[1])
    k_great = lag_kernel(own_rows, all_rows, phonon_lags, phonon_strengths[1], phonon_strengths[0])
    phon_less = jnp.sum(k_less[0][:, None] * everyone[:, 0], axis=0)
    phon_great = jnp.sum(k_great[0][:, None] * everyone[:, 1], axis=0)

    own_weights = photon_weights[0]
    by_relay = jnp.zeros((), jnp.float32)
    for source, _, target in relays:
        weight = own_weights[1] if source < target else own_weights[2]
        by_relay = jnp.where(own == target, weight, by_relay)
    factors = jnp.stack(
        [
            own_weights[0],
            sidebands[0].astype(jnp.float32),
            own_weights[1],
            own_weights[2],
            by_relay,
        ]
    )
    out = None
    for n, chunk in enumerate(CHUNKS):
        sides = [lower[n], upper[n]] + ([relay] if relays and n == 0 else [])
        out = photon_of(chunk, factors, dipole, phon_less[None], left[n], sides, out)
    return out, phon_great[None, None]


def solution(mesh):
    return jax.shard_map(
        on_device,
        mesh=mesh,
        in_specs=(
            P("energy", "slab", None, None, None),
            P("energy", "slab", None),
            P("slab", None, None),
            P("energy", None),
            P("energy"),
            P(),
            P(),
            P("slab", None),
        ),
        out_specs=(P("energy", "slab", None, None, None), P("energy", "slab", None)),
        check_vma=False,
    )
```

```python
import functools

import jax
import jax.numpy as jnp
from jax import lax
from jax.experimental import pallas as pl
from jax.experimental.pallas import tpu as pltpu
from jax.sharding import PartitionSpec as P

PHOT_BLOCKS = 3
CHUNKS = ((0, 0, 2), (1, 0, 2))
VMEM_BYTES = 20 * 1024 * 1024

RELAYS = {8: ((1, 0, 4), (6, 7, 3))}


def shifted(block, axis, distance, relays=()):
    devices = range(lax.axis_size(axis))
    route = {i - distance: i for i in devices if i - distance in devices}
    for source, by, target in relays:
        if route.get(source) == target:
            route[source] = by
    return lax.ppermute(block, axis, sorted(route.items()))


def gathered(block, axis):
    count = lax.axis_size(axis)
    if count & (count - 1):
        return lax.all_gather(block, axis, axis=0)
    block = block[None]
    index = lax.axis_index(axis)
    step = 1
    while step < count:
        other = lax.ppermute(block, axis, [(i, i ^ step) for i in range(count)])
        upper = (index & step) != 0
        block = jnp.concatenate(
            [jnp.where(upper, other, block), jnp.where(upper, block, other)], axis=0
        )
        step *= 2
    return block


def lag_kernel(rows, cols, phonon_lags, first, second):
    offset = cols[None, :] - rows[:, None]
    upward = (offset[None, :, :] == phonon_lags[:, None, None]).astype(jnp.float32)
    downward = (offset[None, :, :] == -phonon_lags[:, None, None]).astype(jnp.float32)
    return jnp.sum(first[:, None, None] * upward + second[:, None, None] * downward, axis=0)


def left_body(blocks_ref, dipole_ref, left_ref):
    left_ref[...] = lax.dot_general(
        blocks_ref[...],
        dipole_ref[...],
        (((1,), (1,)), ((), ())),
        preferred_element_type=jnp.float32,
    ).astype(left_ref.dtype)


def left_of(lesser, dipole, chunk):
    part, first, halves = chunk
    width = lesser.shape[-1]
    cols = width // 2 * halves
    rows = width // 4
    return pl.pallas_call(
        left_body,
        grid=(width // rows,),
        in_specs=[
            pl.BlockSpec((None, None, None, rows, width), lambda i: (0, 0, part, i, 0)),
            pl.BlockSpec((None, cols, width), lambda i: (0, first, 0)),
        ],
        out_specs=pl.BlockSpec((rows, cols), lambda i: (i, 0)),
        out_shape=jax.ShapeDtypeStruct((width, cols), lesser.dtype),
        compiler_params=pltpu.CompilerParams(vmem_limit_bytes=VMEM_BYTES),
        name="left",
    )(lesser, dipole)


def photon_body(part, first, n_sides, factors_ref, dipole_ref, phonon_ref, own_ref, *rest):
    out_ref = rest[-1]
    side = factors_ref[2] * rest[0][...].astype(jnp.float32)
    for n in range(1, n_sides):
        side += factors_ref[2 + n] * rest[n][...].astype(jnp.float32)
    mixed = factors_ref[0] * own_ref[...].astype(jnp.float32) + factors_ref[1] * side
    photon = jnp.dot(
        dipole_ref[...], mixed.astype(jnp.bfloat16), preferred_element_type=jnp.float32
    )
    if part == 1:
        height, cols = photon.shape
        row = lax.broadcasted_iota(jnp.int32, (height, cols), 0)
        col = lax.broadcasted_iota(jnp.int32, (height, cols), 1)
        col += (first + pl.program_id(0)) * cols
        photon += jnp.where(row == col, phonon_ref[...], 0.0)
    out_ref[...] = photon.astype(out_ref.dtype)


def photon_of(chunk, factors, dipole, phonon, own, sides, out):
    part, first, _ = chunk
    width = own.shape[0]
    cols = width // 4
    steps = own.shape[1] // cols
    first *= 2
    piece = pl.BlockSpec((width, cols), lambda k: (0, k))
    operands = [factors, dipole, phonon, own, *sides]
    in_specs = [
        pl.BlockSpec(memory_space=pltpu.SMEM),
        pl.BlockSpec((None, width, width), lambda k: (0, 0, 0)),
        pl.BlockSpec((1, cols), lambda k: (0, first + k)),
        piece,
        *(piece for _ in sides),
    ]
    aliases = {}
    if out is not None:
        aliases = {len(operands): 0}
        operands.append(out)
        in_specs.append(pl.BlockSpec(memory_space=pl.ANY))
    return pl.pallas_call(
        functools.partial(photon_body, part, first, len(sides)),
        grid=(steps,),
        in_specs=in_specs,
        out_specs=pl.BlockSpec(
            (None, None, None, width, cols), lambda k: (0, 0, part, 0, first + k)
        ),
        out_shape=jax.ShapeDtypeStruct((1, 1, 2, width, width), jnp.bfloat16),
        input_output_aliases=aliases,
        compiler_params=pltpu.CompilerParams(vmem_limit_bytes=VMEM_BYTES),
        name="photon",
    )(*operands)


def on_device(
    lesser,
    greater_diag,
    dipole,
    photon_weights,
    sidebands,
    phonon_lags,
    phonon_strengths,
    slab_coupling,
):
    e_count = lesser.shape[0]
    width = lesser.shape[-1]
    count = lax.axis_size("energy")
    own = lax.axis_index("energy")
    relays = RELAYS.get(count, ())

    eye = jnp.arange(width)[:, None] == jnp.arange(width)[None, :]
    diag_less = jnp.sum(jnp.where(eye, lesser[0, 0, 1], 0).astype(jnp.float32), axis=0)
    everyone = gathered(jnp.stack([diag_less, greater_diag[0, 0]]), "energy")

    left = [left_of(lesser, dipole, chunk) for chunk in CHUNKS]
    everyone, *left = lax.optimization_barrier((everyone, *left))
    lower, upper = [], []
    for n, block in enumerate(left):
        hops = relays if n == 0 else ()
        lower.append(shifted(block, "energy", PHOT_BLOCKS, hops))
        upper.append(shifted(block, "energy", -PHOT_BLOCKS, hops))
    relayed = []
    for source, by, target in relays:
        block = lower[0] if source < target else upper[0]
        relayed.append(lax.ppermute(block, "energy", [(by, target)]))

    own_rows = own * e_count + jnp.arange(e_count, dtype=jnp.int32)
    all_rows = jnp.arange(e_count * count, dtype=jnp.int32)
    k_less = lag_kernel(own_rows, all_rows, phonon_lags, phonon_strengths[0], phonon_strengths[1])
    k_great = lag_kernel(own_rows, all_rows, phonon_lags, phonon_strengths[1], phonon_strengths[0])
    corr_less = jnp.sum(k_less[0][:, None] * everyone[:, 0], axis=0)
    corr_great = jnp.sum(k_great[0][:, None] * everyone[:, 1], axis=0)
    correlated = jnp.stack([corr_less, corr_great])
    below = shifted(slab_coupling * correlated, "slab", 1)
    above = shifted(correlated, "slab", -1)
    phon_less, phon_great = correlated + below + slab_coupling * above

    weight_0, weight_low, weight_high = photon_weights[0]
    flag = sidebands[0].astype(jnp.float32)
    first_low, first_high, by_relay = weight_low, weight_high, []
    for source, by, target in relays:
        if source < target:
            first_low = jnp.where(own == by, 0.0, first_low)
            by_relay.append(weight_low)
        else:
            first_high = jnp.where(own == by, 0.0, first_high)
            by_relay.append(weight_high)
    first_factors = jnp.stack([weight_0, flag, first_low, first_high, *by_relay])
    factors = jnp.stack([weight_0, flag, weight_low, weight_high])
    out = None
    for n in (1, 0):
        sides = [lower[n], upper[n]] + (relayed if n == 0 else [])
        weights = first_factors if n == 0 else factors
        out = photon_of(CHUNKS[n], weights, dipole, phon_less[None], left[n], sides, out)
    return out, phon_great[None, None]


def solution(mesh):
    return jax.shard_map(
        on_device,
        mesh=mesh,
        in_specs=(
            P("energy", "slab", None, None, None),
            P("energy", "slab", None),
            P("slab", None, None),
            P("energy", None),
            P("energy"),
            P(),
            P(),
            P("slab", None),
        ),
        out_specs=(P("energy", "slab", None, None, None), P("energy", "slab", None)),
        check_vma=False,
    )
```

```python
import functools

import jax
import jax.numpy as jnp
from jax import lax
from jax.experimental import pallas as pl
from jax.experimental.pallas import tpu as pltpu
from jax.sharding import PartitionSpec as P

PHOT_BLOCKS = 3
CHUNKS = ((0, 0, 2), (1, 0, 2))
VMEM_BYTES = 20 * 1024 * 1024
LEFT_VMEM_BYTES = 56 * 1024 * 1024

DETOURS = {8: ((1, 0, 4), (6, 7, 3))}
LATE = {8: ((3, 0), (4, 7))}


def shifted(block, axis, distance, detours=(), late=()):
    devices = range(lax.axis_size(axis))
    route = {i - distance: i for i in devices if i - distance in devices}
    route = {source: target for source, target in route.items() if (source, target) not in late}
    for source, by, target in detours:
        if route.get(source) == target:
            route[source] = by
    return lax.ppermute(block, axis, sorted(route.items()))


def doubled(block, axis, step):
    other = lax.ppermute(block, axis, [(i, i ^ step) for i in range(lax.axis_size(axis))])
    upper = (lax.axis_index(axis) & step) != 0
    return jnp.concatenate(
        [jnp.where(upper, other, block), jnp.where(upper, block, other)], axis=0
    )


def any_of(own, energies):
    return functools.reduce(jnp.logical_or, [own == energy for energy in energies])


def diagonals_body(tile, lesser_ref, greater_ref, out_ref, tiles, arrived):
    count = tiles.shape[0]
    copies = [
        pltpu.make_async_copy(
            lesser_ref.at[0, 0, 1, pl.ds(n * tile, tile), pl.ds(n * tile, tile)],
            tiles.at[n],
            arrived.at[n],
        )
        for n in range(count)
    ]
    for copy in copies:
        copy.start()
    row = lax.broadcasted_iota(jnp.int32, (tile, tile), 0)
    col = lax.broadcasted_iota(jnp.int32, (tile, tile), 1)
    out_ref[0, 1:2] = greater_ref[0]
    for n, copy in enumerate(copies):
        copy.wait()
        block = jnp.where(row == col, tiles[n].astype(jnp.float32), 0.0)
        out_ref[0, 0:1, n * tile : (n + 1) * tile] = jnp.sum(block, axis=0, keepdims=True)


def diagonals_of(lesser, greater_diag):
    width = lesser.shape[-1]
    tile = 128
    return pl.pallas_call(
        functools.partial(diagonals_body, tile),
        in_specs=[
            pl.BlockSpec(memory_space=pltpu.HBM),
            pl.BlockSpec(memory_space=pltpu.VMEM),
        ],
        out_specs=pl.BlockSpec(memory_space=pltpu.VMEM),
        out_shape=jax.ShapeDtypeStruct((1, 2, width), jnp.float32),
        scratch_shapes=[
            pltpu.VMEM((width // tile, tile, tile), lesser.dtype),
            pltpu.SemaphoreType.DMA((width // tile,)),
        ],
        compiler_params=pltpu.CompilerParams(vmem_limit_bytes=LEFT_VMEM_BYTES),
        name="diagonals",
    )(lesser, greater_diag)


def lag_kernel(rows, cols, phonon_lags, first, second):
    offset = cols[None, :] - rows[:, None]
    upward = (offset[None, :, :] == phonon_lags[:, None, None]).astype(jnp.float32)
    downward = (offset[None, :, :] == -phonon_lags[:, None, None]).astype(jnp.float32)
    return jnp.sum(first[:, None, None] * upward + second[:, None, None] * downward, axis=0)


def left_body(blocks_ref, dipole_ref, left_ref):
    left_ref[...] = lax.dot_general(
        blocks_ref[...],
        dipole_ref[...],
        (((1,), (1,)), ((), ())),
        preferred_element_type=jnp.float32,
    ).astype(left_ref.dtype)


def left_of(lesser, dipole, chunk):
    part, first, halves = chunk
    width = lesser.shape[-1]
    cols = width // 2 * halves
    rows = width // 4
    return pl.pallas_call(
        left_body,
        grid=(width // rows,),
        in_specs=[
            pl.BlockSpec((None, None, None, rows, width), lambda i: (0, 0, part, i, 0)),
            pl.BlockSpec((None, cols, width), lambda i: (0, first, 0)),
        ],
        out_specs=pl.BlockSpec((rows, cols), lambda i: (i, 0)),
        out_shape=jax.ShapeDtypeStruct((width, cols), lesser.dtype),
        compiler_params=pltpu.CompilerParams(vmem_limit_bytes=LEFT_VMEM_BYTES),
        name="left",
    )(lesser, dipole)


def photon_body(part, first, n_sides, factors_ref, dipole_ref, phonon_ref, own_ref, *rest):
    out_ref = rest[-1]
    side = factors_ref[2] * rest[0][...].astype(jnp.float32)
    for n in range(1, n_sides):
        side += factors_ref[2 + n] * rest[n][...].astype(jnp.float32)
    mixed = factors_ref[0] * own_ref[...].astype(jnp.float32) + factors_ref[1] * side
    photon = jnp.dot(
        dipole_ref[...], mixed.astype(jnp.bfloat16), preferred_element_type=jnp.float32
    )
    if part == 1:
        height, cols = photon.shape
        row = lax.broadcasted_iota(jnp.int32, (height, cols), 0)
        col = lax.broadcasted_iota(jnp.int32, (height, cols), 1)
        col += (first + pl.program_id(0)) * cols
        photon += jnp.where(row == col, phonon_ref[...], 0.0)
    out_ref[...] = photon.astype(out_ref.dtype)


def photon_of(chunk, factors, dipole, phonon, own, sides, out):
    part, first, _ = chunk
    width = own.shape[0]
    cols = width // 4
    steps = own.shape[1] // cols
    first *= 2
    piece = pl.BlockSpec((width, cols), lambda k: (0, k))
    operands = [factors, dipole, phonon, own, *sides]
    in_specs = [
        pl.BlockSpec(memory_space=pltpu.SMEM),
        pl.BlockSpec((None, width, width), lambda k: (0, 0, 0)),
        pl.BlockSpec((1, cols), lambda k: (0, first + k)),
        piece,
        *(piece for _ in sides),
    ]
    aliases = {}
    if out is not None:
        aliases = {len(operands): 0}
        operands.append(out)
        in_specs.append(pl.BlockSpec(memory_space=pl.ANY))
    return pl.pallas_call(
        functools.partial(photon_body, part, first, len(sides)),
        grid=(steps,),
        in_specs=in_specs,
        out_specs=pl.BlockSpec(
            (None, None, None, width, cols), lambda k: (0, 0, part, 0, first + k)
        ),
        out_shape=jax.ShapeDtypeStruct((1, 1, 2, width, width), jnp.bfloat16),
        input_output_aliases=aliases,
        compiler_params=pltpu.CompilerParams(vmem_limit_bytes=VMEM_BYTES),
        name="photon",
    )(*operands)


def on_device(
    lesser,
    greater_diag,
    dipole,
    photon_weights,
    sidebands,
    phonon_lags,
    phonon_strengths,
    slab_coupling,
):
    e_count = lesser.shape[0]
    width = lesser.shape[-1]
    count = lax.axis_size("energy")
    own = lax.axis_index("energy")
    detours, late = DETOURS.get(count, ()), LATE.get(count, ())

    left = [left_of(lesser, dipole, chunk) for chunk in CHUNKS]
    everyone = diagonals_of(lesser, greater_diag)
    step = 1
    while step < count:
        everyone = doubled(everyone, "energy", step)
        everyone, left[0] = lax.optimization_barrier((everyone, left[0]))
        step *= 2

    lower = [shifted(left[0], "energy", PHOT_BLOCKS, detours, late)]
    upper = [shifted(left[0], "energy", -PHOT_BLOCKS, detours, late)]
    lower.append(shifted(left[1], "energy", PHOT_BLOCKS))
    upper.append(shifted(left[1], "energy", -PHOT_BLOCKS))
    last_hops = list(late)
    block = left[0]
    for source, by, target in detours:
        block = jnp.where(own == by, lower[0] if source < target else upper[0], block)
        last_hops.append((by, target))
    if last_hops:
        last = lax.ppermute(block, "energy", last_hops)

    own_rows = own * e_count + jnp.arange(e_count, dtype=jnp.int32)
    all_rows = jnp.arange(e_count * count, dtype=jnp.int32)
    k_less = lag_kernel(own_rows, all_rows, phonon_lags, phonon_strengths[0], phonon_strengths[1])
    k_great = lag_kernel(own_rows, all_rows, phonon_lags, phonon_strengths[1], phonon_strengths[0])
    corr_less = jnp.sum(k_less[0][:, None] * everyone[:, 0], axis=0)
    corr_great = jnp.sum(k_great[0][:, None] * everyone[:, 1], axis=0)
    correlated = jnp.stack([corr_less, corr_great])
    below = shifted(slab_coupling * correlated, "slab", 1)
    above = shifted(correlated, "slab", -1)
    phon_less, phon_great = correlated + below + slab_coupling * above

    weight_0, weight_low, weight_high = photon_weights[0]
    flag = sidebands[0].astype(jnp.float32)
    factors = jnp.stack([weight_0, flag, weight_low, weight_high])
    first_factors, first_sides = factors, [lower[0], upper[0]]
    if last_hops:
        ends = late + tuple((source, target) for source, _, target in detours)
        from_low = any_of(own, [target for source, target in ends if source < target])
        from_high = any_of(own, [target for source, target in ends if source > target])
        first_low = any_of(own, [by for source, by, target in detours if source < target])
        first_high = any_of(own, [by for source, by, target in detours if source > target])
        first_factors = jnp.stack(
            [
                weight_0,
                flag,
                jnp.where(first_low, 0.0, weight_low),
                jnp.where(first_high, 0.0, weight_high),
                jnp.where(from_low, weight_low, jnp.where(from_high, weight_high, 0.0)),
            ]
        )
        first_sides.append(last)
    out = photon_of(
        CHUNKS[1], factors, dipole, phon_less[None], left[1], [lower[1], upper[1]], None
    )
    out = photon_of(
        CHUNKS[0], first_factors, dipole, phon_less[None], left[0], first_sides, out
    )
    return out, phon_great[None, None]


def solution(mesh):
    return jax.shard_map(
        on_device,
        mesh=mesh,
        in_specs=(
            P("energy", "slab", None, None, None),
            P("energy", "slab", None),
            P("slab", None, None),
            P("energy", None),
            P("energy"),
            P(),
            P(),
            P("slab", None),
        ),
        out_specs=(P("energy", "slab", None, None, None), P("energy", "slab", None)),
        check_vma=False,
    )
```

```python
import functools

import jax
import jax.numpy as jnp
from jax import lax
from jax.experimental import pallas as pl
from jax.experimental.pallas import tpu as pltpu
from jax.sharding import PartitionSpec as P

PHOT_BLOCKS = 3
CHUNKS = ((0, 0, 2), (1, 0, 2))
VMEM_BYTES = 20 * 1024 * 1024
LEFT_VMEM_BYTES = 48 * 1024 * 1024
DIAGONALS_VMEM_BYTES = 56 * 1024 * 1024

DETOURS = {8: ((1, 0, 4), (6, 7, 3))}
LATE = {8: ((3, 0), (4, 7))}


def shifted(block, axis, distance, detours=(), late=()):
    devices = range(lax.axis_size(axis))
    route = {i - distance: i for i in devices if i - distance in devices}
    route = {source: target for source, target in route.items() if (source, target) not in late}
    for source, by, target in detours:
        if route.get(source) == target:
            route[source] = by
    return lax.ppermute(block, axis, sorted(route.items()))


def doubled(block, axis, step):
    other = lax.ppermute(block, axis, [(i, i ^ step) for i in range(lax.axis_size(axis))])
    upper = (lax.axis_index(axis) & step) != 0
    return jnp.concatenate(
        [jnp.where(upper, other, block), jnp.where(upper, block, other)], axis=0
    )


def any_of(own, energies):
    return functools.reduce(jnp.logical_or, [own == energy for energy in energies])


def diagonals_body(tile, lesser_ref, greater_ref, out_ref, tiles, arrived):
    count = tiles.shape[0]
    copies = [
        pltpu.make_async_copy(
            lesser_ref.at[0, 0, 1, pl.ds(n * tile, tile), pl.ds(n * tile, tile)],
            tiles.at[n],
            arrived.at[n],
        )
        for n in range(count)
    ]
    for copy in copies:
        copy.start()
    row = lax.broadcasted_iota(jnp.int32, (tile, tile), 0)
    col = lax.broadcasted_iota(jnp.int32, (tile, tile), 1)
    out_ref[0, 1:2] = greater_ref[0]
    for n, copy in enumerate(copies):
        copy.wait()
        block = jnp.where(row == col, tiles[n].astype(jnp.float32), 0.0)
        out_ref[0, 0:1, n * tile : (n + 1) * tile] = jnp.sum(block, axis=0, keepdims=True)


def diagonals_of(lesser, greater_diag):
    width = lesser.shape[-1]
    tile = 128
    return pl.pallas_call(
        functools.partial(diagonals_body, tile),
        in_specs=[
            pl.BlockSpec(memory_space=pltpu.HBM),
            pl.BlockSpec(memory_space=pltpu.VMEM),
        ],
        out_specs=pl.BlockSpec(memory_space=pltpu.VMEM),
        out_shape=jax.ShapeDtypeStruct((1, 2, width), jnp.float32),
        scratch_shapes=[
            pltpu.VMEM((width // tile, tile, tile), lesser.dtype),
            pltpu.SemaphoreType.DMA((width // tile,)),
        ],
        compiler_params=pltpu.CompilerParams(vmem_limit_bytes=DIAGONALS_VMEM_BYTES),
        name="diagonals",
    )(lesser, greater_diag)


def lag_kernel(rows, cols, phonon_lags, first, second):
    offset = cols[None, :] - rows[:, None]
    upward = (offset[None, :, :] == phonon_lags[:, None, None]).astype(jnp.float32)
    downward = (offset[None, :, :] == -phonon_lags[:, None, None]).astype(jnp.float32)
    return jnp.sum(first[:, None, None] * upward + second[:, None, None] * downward, axis=0)


def left_body(blocks_ref, dipole_ref, left_ref):
    left_ref[...] = lax.dot_general(
        blocks_ref[...],
        dipole_ref[...],
        (((1,), (1,)), ((), ())),
        preferred_element_type=jnp.float32,
    ).astype(left_ref.dtype)


def left_of(lesser, dipole, chunk):
    part, first, halves = chunk
    width = lesser.shape[-1]
    cols = width // 2 * halves
    rows = width // 4
    return pl.pallas_call(
        left_body,
        grid=(width // rows,),
        in_specs=[
            pl.BlockSpec((None, None, None, rows, width), lambda i: (0, 0, part, i, 0)),
            pl.BlockSpec((None, cols, width), lambda i: (0, first, 0)),
        ],
        out_specs=pl.BlockSpec((rows, cols), lambda i: (i, 0)),
        out_shape=jax.ShapeDtypeStruct((width, cols), lesser.dtype),
        compiler_params=pltpu.CompilerParams(vmem_limit_bytes=LEFT_VMEM_BYTES),
        name="left",
    )(lesser, dipole)


def photon_body(part, first, n_sides, factors_ref, dipole_ref, phonon_ref, own_ref, *rest):
    out_ref = rest[-1]
    side = factors_ref[2] * rest[0][...].astype(jnp.float32)
    for n in range(1, n_sides):
        side += factors_ref[2 + n] * rest[n][...].astype(jnp.float32)
    mixed = factors_ref[0] * own_ref[...].astype(jnp.float32) + factors_ref[1] * side
    photon = jnp.dot(
        dipole_ref[...], mixed.astype(jnp.bfloat16), preferred_element_type=jnp.float32
    )
    if part == 1:
        height, cols = photon.shape
        row = lax.broadcasted_iota(jnp.int32, (height, cols), 0)
        col = lax.broadcasted_iota(jnp.int32, (height, cols), 1)
        col += (first + pl.program_id(0)) * cols
        photon += jnp.where(row == col, phonon_ref[...], 0.0)
    out_ref[...] = photon.astype(out_ref.dtype)


def photon_of(chunk, factors, dipole, phonon, own, sides, out):
    part, first, _ = chunk
    width = own.shape[0]
    cols = width // 4
    steps = own.shape[1] // cols
    first *= 2
    piece = pl.BlockSpec((width, cols), lambda k: (0, k))
    operands = [factors, dipole, phonon, own, *sides]
    in_specs = [
        pl.BlockSpec(memory_space=pltpu.SMEM),
        pl.BlockSpec((None, width, width), lambda k: (0, 0, 0)),
        pl.BlockSpec((1, cols), lambda k: (0, first + k)),
        piece,
        *(piece for _ in sides),
    ]
    aliases = {}
    if out is not None:
        aliases = {len(operands): 0}
        operands.append(out)
        in_specs.append(pl.BlockSpec(memory_space=pl.ANY))
    return pl.pallas_call(
        functools.partial(photon_body, part, first, len(sides)),
        grid=(steps,),
        in_specs=in_specs,
        out_specs=pl.BlockSpec(
            (None, None, None, width, cols), lambda k: (0, 0, part, 0, first + k)
        ),
        out_shape=jax.ShapeDtypeStruct((1, 1, 2, width, width), jnp.bfloat16),
        input_output_aliases=aliases,
        compiler_params=pltpu.CompilerParams(vmem_limit_bytes=VMEM_BYTES),
        name="photon",
    )(*operands)


def on_device(
    lesser,
    greater_diag,
    dipole,
    photon_weights,
    sidebands,
    phonon_lags,
    phonon_strengths,
    slab_coupling,
):
    e_count = lesser.shape[0]
    width = lesser.shape[-1]
    count = lax.axis_size("energy")
    own = lax.axis_index("energy")
    detours, late = DETOURS.get(count, ()), LATE.get(count, ())

    left = [left_of(lesser, dipole, chunk) for chunk in CHUNKS]
    everyone = diagonals_of(lesser, greater_diag)
    step = 1
    while step < count:
        everyone = doubled(everyone, "energy", step)
        everyone, left[0] = lax.optimization_barrier((everyone, left[0]))
        step *= 2

    lower = [shifted(left[0], "energy", PHOT_BLOCKS, detours, late)]
    upper = [shifted(left[0], "energy", -PHOT_BLOCKS, detours, late)]
    last_hops = list(late)
    block = left[0]
    for source, by, target in detours:
        block = jnp.where(own == by, lower[0] if source < target else upper[0], block)
        last_hops.append((by, target))
    if last_hops:
        block, left[1] = lax.optimization_barrier((block, left[1]))
        last = lax.ppermute(block, "energy", last_hops)
    lower.append(shifted(left[1], "energy", PHOT_BLOCKS))
    upper.append(shifted(left[1], "energy", -PHOT_BLOCKS))

    own_rows = own * e_count + jnp.arange(e_count, dtype=jnp.int32)
    all_rows = jnp.arange(e_count * count, dtype=jnp.int32)
    k_less = lag_kernel(own_rows, all_rows, phonon_lags, phonon_strengths[0], phonon_strengths[1])
    k_great = lag_kernel(own_rows, all_rows, phonon_lags, phonon_strengths[1], phonon_strengths[0])
    corr_less = jnp.sum(k_less[0][:, None] * everyone[:, 0], axis=0)
    corr_great = jnp.sum(k_great[0][:, None] * everyone[:, 1], axis=0)
    correlated = jnp.stack([corr_less, corr_great])
    below = shifted(slab_coupling * correlated, "slab", 1)
    above = shifted(correlated, "slab", -1)
    phon_less, phon_great = correlated + below + slab_coupling * above

    weight_0, weight_low, weight_high = photon_weights[0]
    flag = sidebands[0].astype(jnp.float32)
    factors = jnp.stack([weight_0, flag, weight_low, weight_high])
    first_factors, first_sides = factors, [lower[0], upper[0]]
    if last_hops:
        ends = late + tuple((source, target) for source, _, target in detours)
        from_low = any_of(own, [target for source, target in ends if source < target])
        from_high = any_of(own, [target for source, target in ends if source > target])
        first_low = any_of(own, [by for source, by, target in detours if source < target])
        first_high = any_of(own, [by for source, by, target in detours if source > target])
        first_factors = jnp.stack(
            [
                weight_0,
                flag,
                jnp.where(first_low, 0.0, weight_low),
                jnp.where(first_high, 0.0, weight_high),
                jnp.where(from_low, weight_low, jnp.where(from_high, weight_high, 0.0)),
            ]
        )
        first_sides.append(last)
    out = photon_of(
        CHUNKS[0], first_factors, dipole, phon_less[None], left[0], first_sides, None
    )
    out = photon_of(
        CHUNKS[1], factors, dipole, phon_less[None], left[1], [lower[1], upper[1]], out
    )
    return out, phon_great[None, None]


def solution(mesh):
    return jax.shard_map(
        on_device,
        mesh=mesh,
        in_specs=(
            P("energy", "slab", None, None, None),
            P("energy", "slab", None),
            P("slab", None, None),
            P("energy", None),
            P("energy"),
            P(),
            P(),
            P("slab", None),
        ),
        out_specs=(P("energy", "slab", None, None, None), P("energy", "slab", None)),
        check_vma=False,
    )
```

```python
import functools

import jax
import jax.numpy as jnp
from jax import lax
from jax.experimental import pallas as pl
from jax.experimental.pallas import tpu as pltpu
from jax.sharding import PartitionSpec as P

PHOT_BLOCKS = 3
CHUNKS = ((0, 0, 4), (1, 0, 1), (1, 1, 3))
IMAGINARY = (1, 0, 4)
QUARTERS = 4
VMEM_BYTES = 20 * 1024 * 1024
LEFT_VMEM_BYTES = 48 * 1024 * 1024
DIAGONALS_VMEM_BYTES = 56 * 1024 * 1024

STRAIGHT = ((0, 3), (2, 5), (3, 6), (4, 1), (5, 2), (7, 4))
CROSS = ((1, 4), (3, 0), (4, 7), (6, 3))
DETOURS = ((1, 0, 4), (6, 7, 3))
EDGES = ((3, 0), (4, 7))


def shifted(block, axis, distance):
    devices = range(lax.axis_size(axis))
    return lax.ppermute(
        block, axis, [(i - distance, i) for i in devices if i - distance in devices]
    )


def any_of(own, energies):
    return functools.reduce(jnp.logical_or, [own == energy for energy in energies])


def side_weight(own, route, low, high):
    from_low = any_of(own, [target for source, target in route if source < target])
    from_high = any_of(own, [target for source, target in route if source > target])
    return jnp.where(from_low, low, jnp.where(from_high, high, 0.0))


def doubled(block, axis, step):
    other = lax.ppermute(block, axis, [(i, i ^ step) for i in range(lax.axis_size(axis))])
    upper = (lax.axis_index(axis) & step) != 0
    return jnp.concatenate(
        [jnp.where(upper, other, block), jnp.where(upper, block, other)], axis=0
    )


def diagonals_body(tile, lesser_ref, greater_ref, out_ref, tiles, arrived):
    count = tiles.shape[0]
    copies = [
        pltpu.make_async_copy(
            lesser_ref.at[0, 0, 1, pl.ds(n * tile, tile), pl.ds(n * tile, tile)],
            tiles.at[n],
            arrived.at[n],
        )
        for n in range(count)
    ]
    for copy in copies:
        copy.start()
    row = lax.broadcasted_iota(jnp.int32, (tile, tile), 0)
    col = lax.broadcasted_iota(jnp.int32, (tile, tile), 1)
    out_ref[0, 1:2] = greater_ref[0]
    for n, copy in enumerate(copies):
        copy.wait()
        block = jnp.where(row == col, tiles[n].astype(jnp.float32), 0.0)
        out_ref[0, 0:1, n * tile : (n + 1) * tile] = jnp.sum(block, axis=0, keepdims=True)


def diagonals_of(lesser, greater_diag):
    width = lesser.shape[-1]
    tile = 128
    return pl.pallas_call(
        functools.partial(diagonals_body, tile),
        in_specs=[
            pl.BlockSpec(memory_space=pltpu.HBM),
            pl.BlockSpec(memory_space=pltpu.VMEM),
        ],
        out_specs=pl.BlockSpec(memory_space=pltpu.VMEM),
        out_shape=jax.ShapeDtypeStruct((1, 2, width), jnp.float32),
        scratch_shapes=[
            pltpu.VMEM((width // tile, tile, tile), lesser.dtype),
            pltpu.SemaphoreType.DMA((width // tile,)),
        ],
        compiler_params=pltpu.CompilerParams(vmem_limit_bytes=DIAGONALS_VMEM_BYTES),
        name="diagonals",
    )(lesser, greater_diag)


def lag_kernel(rows, cols, phonon_lags, first, second):
    offset = cols[None, :] - rows[:, None]
    upward = (offset[None, :, :] == phonon_lags[:, None, None]).astype(jnp.float32)
    downward = (offset[None, :, :] == -phonon_lags[:, None, None]).astype(jnp.float32)
    return jnp.sum(first[:, None, None] * upward + second[:, None, None] * downward, axis=0)


def left_body(blocks_ref, dipole_ref, left_ref):
    left_ref[...] = lax.dot_general(
        blocks_ref[...],
        dipole_ref[...],
        (((1,), (1,)), ((), ())),
        preferred_element_type=jnp.float32,
    ).astype(left_ref.dtype)


def left_of(lesser, dipole, chunk):
    part, first, quarters = chunk
    width = lesser.shape[-1]
    cols = width // QUARTERS
    return pl.pallas_call(
        left_body,
        grid=(quarters,),
        in_specs=[
            pl.BlockSpec((None, None, None, width, width), lambda k: (0, 0, part, 0, 0)),
            pl.BlockSpec((None, cols, width), lambda k: (0, first + k, 0)),
        ],
        out_specs=pl.BlockSpec((width, cols), lambda k: (0, k)),
        out_shape=jax.ShapeDtypeStruct((width, cols * quarters), lesser.dtype),
        compiler_params=pltpu.CompilerParams(vmem_limit_bytes=LEFT_VMEM_BYTES),
        name="left",
    )(lesser, dipole)


def photon_body(part, first, n_sides, factors_ref, dipole_ref, phonon_ref, own_ref, *rest):
    out_ref = rest[-1]
    side = factors_ref[2] * rest[0][...].astype(jnp.float32)
    for n in range(1, n_sides):
        side += factors_ref[2 + n] * rest[n][...].astype(jnp.float32)
    mixed = factors_ref[0] * own_ref[...].astype(jnp.float32) + factors_ref[1] * side
    photon = jnp.dot(
        dipole_ref[...], mixed.astype(jnp.bfloat16), preferred_element_type=jnp.float32
    )
    if part == 1:
        height, cols = photon.shape
        row = lax.broadcasted_iota(jnp.int32, (height, cols), 0)
        col = lax.broadcasted_iota(jnp.int32, (height, cols), 1)
        col += (first + pl.program_id(0)) * cols
        photon += jnp.where(row == col, phonon_ref[...], 0.0)
    out_ref[...] = photon.astype(out_ref.dtype)


def photon_of(chunk, factors, dipole, phonon, own, sides, out):
    part, first, quarters = chunk
    width = own.shape[0]
    cols = width // QUARTERS
    operands = [factors, dipole, phonon, own, *sides]
    in_specs = [
        pl.BlockSpec(memory_space=pltpu.SMEM),
        pl.BlockSpec((None, width, width), lambda k: (0, 0, 0)),
        pl.BlockSpec((1, cols), lambda k: (0, first + k)),
    ]
    for block in (own, *sides):
        skip = first if block.shape[1] > cols * quarters else 0
        in_specs.append(pl.BlockSpec((width, cols), lambda k, skip=skip: (0, skip + k)))
    aliases = {}
    if out is not None:
        aliases = {len(operands): 0}
        operands.append(out)
        in_specs.append(pl.BlockSpec(memory_space=pl.ANY))
    return pl.pallas_call(
        functools.partial(photon_body, part, first, len(sides)),
        grid=(quarters,),
        in_specs=in_specs,
        out_specs=pl.BlockSpec(
            (None, None, None, width, cols), lambda k: (0, 0, part, 0, first + k)
        ),
        out_shape=jax.ShapeDtypeStruct((1, 1, 2, width, width), jnp.bfloat16),
        input_output_aliases=aliases,
        compiler_params=pltpu.CompilerParams(vmem_limit_bytes=VMEM_BYTES),
        name="photon",
    )(*operands)


def on_device(
    lesser,
    greater_diag,
    dipole,
    photon_weights,
    sidebands,
    phonon_lags,
    phonon_strengths,
    slab_coupling,
):
    e_count = lesser.shape[0]
    width = lesser.shape[-1]
    count = lax.axis_size("energy")
    own = lax.axis_index("energy")
    everyone = doubled(diagonals_of(lesser, greater_diag), "energy", 1)
    everyone, lesser = lax.optimization_barrier((everyone, lesser))
    held = jnp.arange(2, dtype=jnp.int32)
    if count == 8:
        others = [
            lax.ppermute(everyone, "energy", [(i, i ^ step) for i in range(count)])
            for step in range(2, count, 2)
        ]
        everyone = jnp.concatenate([everyone, *others], axis=0)
        pairs = (own // 2) ^ jnp.arange(count // 2, dtype=jnp.int32)
        all_rows = (2 * pairs[:, None] + held[None, :]).reshape(-1)
    else:
        step = 2
        while step < count:
            everyone = doubled(everyone, "energy", step)
            step *= 2
        all_rows = jnp.arange(count, dtype=jnp.int32)

    left = [left_of(lesser, dipole, chunk) for chunk in CHUNKS]
    everyone, left[0] = lax.optimization_barrier((everyone, left[0]))
    weight_0, weight_low, weight_high = photon_weights[0]
    flag = sidebands[0].astype(jnp.float32)
    if count == 8:
        first, second = {}, {}
        hops = tuple((source, by) for source, by, _ in DETOURS)
        second_hops = tuple((by, target) for _, by, target in DETOURS)
        first[0] = lax.ppermute(left[0], "energy", STRAIGHT + hops)
        first[1] = lax.ppermute(left[1], "energy", STRAIGHT)
        first[0], left[0], left[1] = lax.optimization_barrier((first[0], left[0], left[1]))
        edge = lax.ppermute(left[0], "energy", EDGES)
        second[0] = edge + lax.ppermute(first[0], "energy", second_hops)
        first[0], first[1], left[2], whole = lax.optimization_barrier(
            (first[0], first[1], left[2], left_of(lesser, dipole, IMAGINARY))
        )
        second[1] = second[2] = lax.ppermute(whole, "energy", CROSS)
        first[2] = lax.ppermute(left[2], "energy", STRAIGHT)
        weights = [
            side_weight(own, STRAIGHT, weight_low, weight_high),
            side_weight(own, CROSS, weight_low, weight_high),
        ]
    else:
        first = [shifted(block, "energy", PHOT_BLOCKS) for block in left]
        second = [shifted(block, "energy", -PHOT_BLOCKS) for block in left]
        weights = [weight_low, weight_high]
    factors = jnp.stack([weight_0, flag, *weights])

    own_rows = own * e_count + jnp.arange(e_count, dtype=jnp.int32)
    k_less = lag_kernel(own_rows, all_rows, phonon_lags, phonon_strengths[0], phonon_strengths[1])
    k_great = lag_kernel(own_rows, all_rows, phonon_lags, phonon_strengths[1], phonon_strengths[0])
    corr_less = jnp.sum(k_less[0][:, None] * everyone[:, 0], axis=0)
    corr_great = jnp.sum(k_great[0][:, None] * everyone[:, 1], axis=0)
    correlated = jnp.stack([corr_less, corr_great])
    below = shifted(slab_coupling * correlated, "slab", 1)
    above = shifted(correlated, "slab", -1)
    phon_less, phon_great = correlated + below + slab_coupling * above

    out = None
    for n in (0, 1, 2):
        sides = [first[n], second[n]]
        out = photon_of(CHUNKS[n], factors, dipole, phon_less[None], left[n], sides, out)
    return out, phon_great[None, None]


def solution(mesh):
    return jax.shard_map(
        on_device,
        mesh=mesh,
        in_specs=(
            P("energy", "slab", None, None, None),
            P("energy", "slab", None),
            P("slab", None, None),
            P("energy", None),
            P("energy"),
            P(),
            P(),
            P("slab", None),
        ),
        out_specs=(P("energy", "slab", None, None, None), P("energy", "slab", None)),
        check_vma=False,
    )
```

```python
import functools

import jax
import jax.numpy as jnp
from jax import lax
from jax.experimental import pallas as pl
from jax.experimental.pallas import tpu as pltpu
from jax.sharding import PartitionSpec as P

PHOT_BLOCKS = 3
CHUNKS = ((0, 0, 4), (1, 0, 1), (1, 2, 2), (1, 1, 1))
IMAGINARY = (1, 0, 4)
QUARTERS = 4
VMEM_BYTES = 20 * 1024 * 1024
LEFT_VMEM_BYTES = 48 * 1024 * 1024
DIAGONALS_VMEM_BYTES = 56 * 1024 * 1024

STRAIGHT = ((0, 3), (2, 5), (3, 6), (4, 1), (5, 2), (7, 4))
CROSS = ((1, 4), (3, 0), (4, 7), (6, 3))
DETOURS = ((1, 0, 4), (6, 7, 3))
EDGES = ((3, 0), (4, 7))

TO_HUBS = ((3, 1), (4, 6))
BETWEEN_HUBS = ((1, 6), (6, 1))
FROM_HUBS = (((1, 3), (6, 4)), ((1, 5), (6, 2)), ((1, 7), (6, 0)))


def shifted(block, axis, distance):
    devices = range(lax.axis_size(axis))
    return lax.ppermute(
        block, axis, [(i - distance, i) for i in devices if i - distance in devices]
    )


def any_of(own, energies):
    return functools.reduce(jnp.logical_or, [own == energy for energy in energies])


def side_weight(own, route, low, high):
    from_low = any_of(own, [target for source, target in route if source < target])
    from_high = any_of(own, [target for source, target in route if source > target])
    return jnp.where(from_low, low, jnp.where(from_high, high, 0.0))


def doubled(block, axis, step):
    other = lax.ppermute(block, axis, [(i, i ^ step) for i in range(lax.axis_size(axis))])
    upper = (lax.axis_index(axis) & step) != 0
    return jnp.concatenate(
        [jnp.where(upper, other, block), jnp.where(upper, block, other)], axis=0
    )


def diagonals_body(tile, lesser_ref, greater_ref, out_ref, tiles, arrived):
    count = tiles.shape[0]
    copies = [
        pltpu.make_async_copy(
            lesser_ref.at[0, 0, 1, pl.ds(n * tile, tile), pl.ds(n * tile, tile)],
            tiles.at[n],
            arrived.at[n],
        )
        for n in range(count)
    ]
    for copy in copies:
        copy.start()
    row = lax.broadcasted_iota(jnp.int32, (tile, tile), 0)
    col = lax.broadcasted_iota(jnp.int32, (tile, tile), 1)
    out_ref[0, 1:2] = greater_ref[0]
    for n, copy in enumerate(copies):
        copy.wait()
        block = jnp.where(row == col, tiles[n].astype(jnp.float32), 0.0)
        out_ref[0, 0:1, n * tile : (n + 1) * tile] = jnp.sum(block, axis=0, keepdims=True)


def diagonals_of(lesser, greater_diag):
    width = lesser.shape[-1]
    tile = 128
    return pl.pallas_call(
        functools.partial(diagonals_body, tile),
        in_specs=[
            pl.BlockSpec(memory_space=pltpu.HBM),
            pl.BlockSpec(memory_space=pltpu.VMEM),
        ],
        out_specs=pl.BlockSpec(memory_space=pltpu.VMEM),
        out_shape=jax.ShapeDtypeStruct((1, 2, width), jnp.float32),
        scratch_shapes=[
            pltpu.VMEM((width // tile, tile, tile), lesser.dtype),
            pltpu.SemaphoreType.DMA((width // tile,)),
        ],
        compiler_params=pltpu.CompilerParams(vmem_limit_bytes=DIAGONALS_VMEM_BYTES),
        name="diagonals",
    )(lesser, greater_diag)


def lag_kernel(rows, cols, phonon_lags, first, second):
    offset = cols[None, :] - rows[:, None]
    upward = (offset[None, :, :] == phonon_lags[:, None, None]).astype(jnp.float32)
    downward = (offset[None, :, :] == -phonon_lags[:, None, None]).astype(jnp.float32)
    return jnp.sum(first[:, None, None] * upward + second[:, None, None] * downward, axis=0)


def left_body(blocks_ref, dipole_ref, left_ref):
    left_ref[...] = lax.dot_general(
        blocks_ref[...],
        dipole_ref[...],
        (((1,), (1,)), ((), ())),
        preferred_element_type=jnp.float32,
    ).astype(left_ref.dtype)


def left_of(lesser, dipole, chunk):
    part, first, quarters = chunk
    width = lesser.shape[-1]
    rows, cols = width // 4, width // QUARTERS * quarters
    return pl.pallas_call(
        left_body,
        grid=(width // rows,),
        in_specs=[
            pl.BlockSpec((None, None, None, rows, width), lambda i: (0, 0, part, i, 0)),
            pl.BlockSpec((None, cols, width), lambda i: (0, first // quarters, 0)),
        ],
        out_specs=pl.BlockSpec((rows, cols), lambda i: (i, 0)),
        out_shape=jax.ShapeDtypeStruct((width, cols), lesser.dtype),
        compiler_params=pltpu.CompilerParams(vmem_limit_bytes=LEFT_VMEM_BYTES),
        name="left",
    )(lesser, dipole)


def photon_body(chunk, factors_ref, dipole_ref, phonon_ref, own_ref, first_ref, second_ref, *rest):
    out_ref, pieces, sent = rest[-3:]
    part, start, quarters = chunk
    width = own_ref.shape[0]
    cols = width // QUARTERS
    weights = [factors_ref[n] for n in range(4)]
    copies = []
    for k in range(quarters):
        at = (start + k) * cols

        def piece(ref):
            skip = at if ref.shape[1] > cols * quarters else k * cols
            return ref[:, skip : skip + cols].astype(jnp.float32)

        side = weights[2] * piece(first_ref) + weights[3] * piece(second_ref)
        mixed = (weights[0] * piece(own_ref) + weights[1] * side).astype(jnp.bfloat16)
        photon = jnp.dot(dipole_ref[0], mixed, preferred_element_type=jnp.float32)
        if part == 1:
            row = lax.broadcasted_iota(jnp.int32, photon.shape, 0)
            col = lax.broadcasted_iota(jnp.int32, photon.shape, 1) + at
            photon += jnp.where(row == col, phonon_ref[:, at : at + cols], 0.0)
        pieces[k] = photon.astype(pieces.dtype)
        copies.append(
            pltpu.make_async_copy(
                pieces.at[k], out_ref.at[0, 0, part, :, pl.ds(at, cols)], sent.at[k]
            )
        )
        copies[-1].start()
    for copy in copies:
        copy.wait()


def photon_of(chunk, factors, dipole, phonon, own, first, second, out):
    width = own.shape[0]
    quarters = chunk[2]
    operands = [factors, dipole, phonon, own, first, second]
    in_specs = [pl.BlockSpec(memory_space=pltpu.SMEM)]
    in_specs += [pl.BlockSpec(memory_space=pltpu.VMEM)] * 5
    aliases = {}
    if out is not None:
        aliases = {len(operands): 0}
        operands.append(out)
        in_specs.append(pl.BlockSpec(memory_space=pl.ANY))
    return pl.pallas_call(
        functools.partial(photon_body, chunk),
        in_specs=in_specs,
        out_specs=pl.BlockSpec(memory_space=pl.ANY),
        out_shape=jax.ShapeDtypeStruct((1, 1, 2, width, width), jnp.bfloat16),
        scratch_shapes=[
            pltpu.VMEM((quarters, width, width // QUARTERS), jnp.bfloat16),
            pltpu.SemaphoreType.DMA((quarters,)),
        ],
        input_output_aliases=aliases,
        compiler_params=pltpu.CompilerParams(vmem_limit_bytes=VMEM_BYTES),
        name="photon",
    )(*operands)


def on_device(
    lesser,
    greater_diag,
    dipole,
    photon_weights,
    sidebands,
    phonon_lags,
    phonon_strengths,
    slab_coupling,
):
    e_count = lesser.shape[0]
    width = lesser.shape[-1]
    count = lax.axis_size("energy")
    own = lax.axis_index("energy")
    everyone = doubled(diagonals_of(lesser, greater_diag), "energy", 1)
    left = [left_of(lesser, dipole, chunk) for chunk in CHUNKS]
    everyone, left[0] = lax.optimization_barrier((everyone, left[0]))
    weight_0, weight_low, weight_high = photon_weights[0]
    flag = sidebands[0].astype(jnp.float32)
    if count == 8:
        first, second = {}, {}
        hops = tuple((source, by) for source, by, _ in DETOURS)
        second_hops = tuple((by, target) for _, by, target in DETOURS)
        first[0] = lax.ppermute(left[0], "energy", STRAIGHT + hops)
        first[1] = lax.ppermute(left[1], "energy", STRAIGHT)

        is_low = own < count // 2
        for route in (TO_HUBS, BETWEEN_HUBS):
            other = lax.ppermute(everyone, "energy", route)
            everyone = jnp.concatenate(
                [jnp.where(is_low, everyone, other), jnp.where(is_low, other, everyone)], axis=0
            )
        held = jnp.where(any_of(own, [hub for hub, _ in BETWEEN_HUBS]), everyone, 0.0)
        for route in FROM_HUBS:
            held += lax.ppermute(everyone, "energy", route)
        everyone = held

        whole = left_of(lesser, dipole, IMAGINARY)
        first[0], everyone, *left[:3], whole = lax.optimization_barrier(
            (first[0], everyone, *left[:3], whole)
        )
        edge = lax.ppermute(left[0], "energy", EDGES)
        second[0] = edge + lax.ppermute(first[0], "energy", second_hops)
        first[0], first[1], *left[2:], whole = lax.optimization_barrier(
            (first[0], first[1], *left[2:], whole)
        )
        second[1] = second[2] = second[3] = lax.ppermute(whole, "energy", CROSS)
        first[2] = lax.ppermute(left[2], "energy", STRAIGHT)
        first[3] = lax.ppermute(left[3], "energy", STRAIGHT)
        weights = [
            side_weight(own, STRAIGHT, weight_low, weight_high),
            side_weight(own, CROSS, weight_low, weight_high),
        ]
    else:
        step = 2
        while step < count:
            everyone = doubled(everyone, "energy", step)
            step *= 2
        first = [shifted(block, "energy", PHOT_BLOCKS) for block in left]
        second = [shifted(block, "energy", -PHOT_BLOCKS) for block in left]
        weights = [weight_low, weight_high]
    factors = jnp.stack([weight_0, flag, *weights])

    own_rows = own * e_count + jnp.arange(e_count, dtype=jnp.int32)
    all_rows = jnp.arange(e_count * count, dtype=jnp.int32)
    k_less = lag_kernel(own_rows, all_rows, phonon_lags, phonon_strengths[0], phonon_strengths[1])
    k_great = lag_kernel(own_rows, all_rows, phonon_lags, phonon_strengths[1], phonon_strengths[0])
    corr_less = jnp.sum(k_less[0][:, None] * everyone[:, 0], axis=0)
    corr_great = jnp.sum(k_great[0][:, None] * everyone[:, 1], axis=0)
    correlated = jnp.stack([corr_less, corr_great])
    below = shifted(slab_coupling * correlated, "slab", 1)
    above = shifted(correlated, "slab", -1)
    phon_less, phon_great = correlated + below + slab_coupling * above

    out = None
    for n, chunk in enumerate(CHUNKS):
        out = photon_of(
            chunk, factors, dipole, phon_less[None], left[n], first[n], second[n], out
        )
    return out, phon_great[None, None]


def solution(mesh):
    return jax.shard_map(
        on_device,
        mesh=mesh,
        in_specs=(
            P("energy", "slab", None, None, None),
            P("energy", "slab", None),
            P("slab", None, None),
            P("energy", None),
            P("energy"),
            P(),
            P(),
            P("slab", None),
        ),
        out_specs=(P("energy", "slab", None, None, None), P("energy", "slab", None)),
        check_vma=False,
    )
```

```python
import functools

import jax
import jax.numpy as jnp
from jax import lax
from jax.experimental import pallas as pl
from jax.experimental.pallas import tpu as pltpu
from jax.sharding import PartitionSpec as P

PHOT_BLOCKS = 3
CHUNKS = ((0, 0, 7), (1, 0, 2), (1, 2, 6), (0, 7, 1))
IMAGINARY = (1, 0, 8)
EIGHTHS = 8
VMEM_BYTES = 20 * 1024 * 1024
DIAGONALS_VMEM_BYTES = 56 * 1024 * 1024

STRAIGHT = ((0, 3), (2, 5), (3, 6), (4, 1), (5, 2), (7, 4))
CROSS = ((1, 4), (3, 0), (4, 7), (6, 3))
DETOURS = ((1, 0, 4), (6, 7, 3))
EDGES = ((3, 0), (4, 7))

TO_HUBS = ((3, 1), (4, 6))
BETWEEN_HUBS = ((1, 6), (6, 1))
FROM_HUBS = (((1, 3), (6, 4)), ((1, 5), (6, 2)), ((1, 7), (6, 0)))


def shifted(block, axis, distance):
    devices = range(lax.axis_size(axis))
    return lax.ppermute(
        block, axis, [(i - distance, i) for i in devices if i - distance in devices]
    )


def any_of(own, energies):
    return functools.reduce(jnp.logical_or, [own == energy for energy in energies])


def side_weight(own, route, low, high):
    from_low = any_of(own, [target for source, target in route if source < target])
    from_high = any_of(own, [target for source, target in route if source > target])
    return jnp.where(from_low, low, jnp.where(from_high, high, 0.0))


def doubled(block, axis, step):
    other = lax.ppermute(block, axis, [(i, i ^ step) for i in range(lax.axis_size(axis))])
    upper = (lax.axis_index(axis) & step) != 0
    return jnp.concatenate(
        [jnp.where(upper, other, block), jnp.where(upper, block, other)], axis=0
    )


def diagonals_body(tile, lesser_ref, greater_ref, out_ref, tiles, arrived):
    count = tiles.shape[0]
    copies = [
        pltpu.make_async_copy(
            lesser_ref.at[0, 0, 1, pl.ds(n * tile, tile), pl.ds(n * tile, tile)],
            tiles.at[n],
            arrived.at[n],
        )
        for n in range(count)
    ]
    for copy in copies:
        copy.start()
    row = lax.broadcasted_iota(jnp.int32, (tile, tile), 0)
    col = lax.broadcasted_iota(jnp.int32, (tile, tile), 1)
    out_ref[0, 1:2] = greater_ref[0]
    for n, copy in enumerate(copies):
        copy.wait()
        block = jnp.where(row == col, tiles[n].astype(jnp.float32), 0.0)
        out_ref[0, 0:1, n * tile : (n + 1) * tile] = jnp.sum(block, axis=0, keepdims=True)


def diagonals_of(lesser, greater_diag):
    width = lesser.shape[-1]
    tile = 128
    return pl.pallas_call(
        functools.partial(diagonals_body, tile),
        in_specs=[
            pl.BlockSpec(memory_space=pltpu.HBM),
            pl.BlockSpec(memory_space=pltpu.VMEM),
        ],
        out_specs=pl.BlockSpec(memory_space=pltpu.VMEM),
        out_shape=jax.ShapeDtypeStruct((1, 2, width), jnp.float32),
        scratch_shapes=[
            pltpu.VMEM((width // tile, tile, tile), lesser.dtype),
            pltpu.SemaphoreType.DMA((width // tile,)),
        ],
        compiler_params=pltpu.CompilerParams(vmem_limit_bytes=DIAGONALS_VMEM_BYTES),
        name="diagonals",
    )(lesser, greater_diag)


def lag_kernel(rows, cols, phonon_lags, first, second):
    offset = cols[None, :] - rows[:, None]
    upward = (offset[None, :, :] == phonon_lags[:, None, None]).astype(jnp.float32)
    downward = (offset[None, :, :] == -phonon_lags[:, None, None]).astype(jnp.float32)
    return jnp.sum(first[:, None, None] * upward + second[:, None, None] * downward, axis=0)


def left_body(chunk, lesser_ref, dipole_ref, left_ref):
    part, first, _ = chunk
    width, cols = left_ref.shape
    rows = width // 4
    start = first * (width // EIGHTHS)
    for i in range(0, width, rows):
        left_ref[i : i + rows] = lax.dot_general(
            lesser_ref[0, 0, part, i : i + rows],
            dipole_ref[0, start : start + cols],
            (((1,), (1,)), ((), ())),
            preferred_element_type=jnp.float32,
        ).astype(left_ref.dtype)


def left_of(lesser, dipole, chunk):
    width = lesser.shape[-1]
    cols = width // EIGHTHS * chunk[2]
    return pl.pallas_call(
        functools.partial(left_body, chunk),
        in_specs=[pl.BlockSpec(memory_space=pltpu.VMEM)] * 2,
        out_specs=pl.BlockSpec(memory_space=pltpu.VMEM),
        out_shape=jax.ShapeDtypeStruct((width, cols), lesser.dtype),
        compiler_params=pltpu.CompilerParams(vmem_limit_bytes=VMEM_BYTES),
        name="left",
    )(lesser, dipole)


def photon_body(chunk, n_sides, factors_ref, dipole_ref, phonon_ref, own_ref, *rest):
    sides, (out_ref, pieces, sent) = rest[:n_sides], rest[-3:]
    part, first, eighths = chunk
    width = own_ref.shape[0]
    unit, most = width // EIGHTHS, pieces.shape[2]
    begin, end = first * unit, (first + eighths) * unit
    factors = [factors_ref[n] for n in range(2 + n_sides)]
    copies = []
    for k, at in enumerate(range(begin, end, most)):
        cols = min(most, end - at)

        def piece(ref):
            skip = at if ref.shape[1] > end - begin else at - begin
            return ref[:, skip : skip + cols].astype(jnp.float32)

        side = factors[2] * piece(sides[0])
        for factor, ref in zip(factors[3:], sides[1:]):
            side += factor * piece(ref)
        mixed = (factors[0] * piece(own_ref) + factors[1] * side).astype(jnp.bfloat16)
        photon = jnp.dot(dipole_ref[0], mixed, preferred_element_type=jnp.float32)
        if part == 1:
            row = lax.broadcasted_iota(jnp.int32, photon.shape, 0)
            col = lax.broadcasted_iota(jnp.int32, photon.shape, 1) + at
            photon += jnp.where(row == col, phonon_ref[:, at : at + cols], 0.0)
        pieces[k, :, :cols] = photon.astype(pieces.dtype)
        copies.append(
            pltpu.make_async_copy(
                pieces.at[k, :, pl.ds(0, cols)],
                out_ref.at[0, 0, part, :, pl.ds(at, cols)],
                sent.at[k],
            )
        )
        copies[-1].start()
    for copy in copies:
        copy.wait()


def photon_of(chunk, factors, dipole, phonon, own, sides, out):
    width, cols = own.shape
    most = min(cols, 2 * width // EIGHTHS)
    n_pieces = pl.cdiv(cols, most)
    operands = [factors, dipole, phonon, own, *sides]
    in_specs = [pl.BlockSpec(memory_space=pltpu.SMEM)]
    in_specs += [pl.BlockSpec(memory_space=pltpu.VMEM)] * (len(operands) - 1)
    aliases = {}
    if out is not None:
        aliases = {len(operands): 0}
        operands.append(out)
        in_specs.append(pl.BlockSpec(memory_space=pl.ANY))
    return pl.pallas_call(
        functools.partial(photon_body, chunk, len(sides)),
        in_specs=in_specs,
        out_specs=pl.BlockSpec(memory_space=pl.ANY),
        out_shape=jax.ShapeDtypeStruct((1, 1, 2, width, width), jnp.bfloat16),
        scratch_shapes=[
            pltpu.VMEM((n_pieces, width, most), jnp.bfloat16),
            pltpu.SemaphoreType.DMA((n_pieces,)),
        ],
        input_output_aliases=aliases,
        cost_estimate=pl.CostEstimate(
            flops=4 * width * width * cols,
            bytes_accessed=2 * width * (width + (2 + len(sides)) * cols),
            transcendentals=0,
        ),
        compiler_params=pltpu.CompilerParams(vmem_limit_bytes=VMEM_BYTES),
        name="photon",
    )(*operands)


def on_device(
    lesser,
    greater_diag,
    dipole,
    photon_weights,
    sidebands,
    phonon_lags,
    phonon_strengths,
    slab_coupling,
):
    e_count = lesser.shape[0]
    width = lesser.shape[-1]
    count = lax.axis_size("energy")
    own = lax.axis_index("energy")
    everyone = doubled(diagonals_of(lesser, greater_diag), "energy", 1)
    left = [left_of(lesser, dipole, chunk) for chunk in CHUNKS]
    everyone, left[0] = lax.optimization_barrier((everyone, left[0]))
    weight_0, weight_low, weight_high = photon_weights[0]
    flag = sidebands[0].astype(jnp.float32)
    if count == 8:
        first, second = {}, {}
        hops = tuple((source, by) for source, by, _ in DETOURS)
        second_hops = tuple((by, target) for _, by, target in DETOURS)
        first[0] = lax.ppermute(left[0], "energy", STRAIGHT + hops)
        first[1] = lax.ppermute(left[1], "energy", STRAIGHT)

        is_low = own < count // 2
        for route in (TO_HUBS, BETWEEN_HUBS):
            other = lax.ppermute(everyone, "energy", route)
            everyone = jnp.concatenate(
                [jnp.where(is_low, everyone, other), jnp.where(is_low, other, everyone)], axis=0
            )
        held = jnp.where(any_of(own, [hub for hub, _ in BETWEEN_HUBS]), everyone, 0.0)
        for route in FROM_HUBS:
            held += lax.ppermute(everyone, "energy", route)
        everyone = held

        whole = left_of(lesser, dipole, IMAGINARY)
        first[0], everyone, *left, whole = lax.optimization_barrier(
            (first[0], everyone, *left, whole)
        )
        edge = lax.ppermute(left[0], "energy", EDGES)
        second[0] = lax.ppermute(first[0], "energy", second_hops)
        first[1], left[2], left[3], whole = lax.optimization_barrier(
            (first[1], left[2], left[3], whole)
        )
        second[1] = second[2] = lax.ppermute(whole, "energy", CROSS)
        first[2] = lax.ppermute(left[2], "energy", STRAIGHT)
        second[3] = lax.ppermute(left[3], "energy", CROSS)
        first[3] = lax.ppermute(left[3], "energy", STRAIGHT)
        weights = [
            side_weight(own, STRAIGHT, weight_low, weight_high),
            side_weight(own, CROSS, weight_low, weight_high),
        ]
    else:
        step = 2
        while step < count:
            everyone = doubled(everyone, "energy", step)
            step *= 2
        first = [shifted(block, "energy", PHOT_BLOCKS) for block in left]
        second = [shifted(block, "energy", -PHOT_BLOCKS) for block in left]
        weights = [weight_low, weight_high]
    sides = {n: [first[n], second[n]] for n in range(len(CHUNKS))}
    factors = {n: jnp.stack([weight_0, flag, *weights]) for n in sides}
    if count == 8:
        sides[0].append(edge)
        factors[0] = jnp.stack([weight_0, flag, *weights, weights[1]])

    own_rows = own * e_count + jnp.arange(e_count, dtype=jnp.int32)
    all_rows = jnp.arange(e_count * count, dtype=jnp.int32)
    k_less = lag_kernel(own_rows, all_rows, phonon_lags, phonon_strengths[0], phonon_strengths[1])
    k_great = lag_kernel(own_rows, all_rows, phonon_lags, phonon_strengths[1], phonon_strengths[0])
    corr_less = jnp.sum(k_less[0][:, None] * everyone[:, 0], axis=0)
    corr_great = jnp.sum(k_great[0][:, None] * everyone[:, 1], axis=0)
    correlated = jnp.stack([corr_less, corr_great])
    below = shifted(slab_coupling * correlated, "slab", 1)
    above = shifted(correlated, "slab", -1)
    phon_less, phon_great = correlated + below + slab_coupling * above

    out = None
    for n, chunk in enumerate(CHUNKS):
        out = photon_of(chunk, factors[n], dipole, phon_less[None], left[n], sides[n], out)
    return out, phon_great[None, None]


def solution(mesh):
    return jax.shard_map(
        on_device,
        mesh=mesh,
        in_specs=(
            P("energy", "slab", None, None, None),
            P("energy", "slab", None),
            P("slab", None, None),
            P("energy", None),
            P("energy"),
            P(),
            P(),
            P("slab", None),
        ),
        out_specs=(P("energy", "slab", None, None, None), P("energy", "slab", None)),
        check_vma=False,
    )
```

```python
import functools

import jax
import jax.numpy as jnp
from jax import lax
from jax.experimental import pallas as pl
from jax.experimental.pallas import tpu as pltpu
from jax.sharding import PartitionSpec as P

PHOT_BLOCKS = 3
CHUNKS = (((0, 0, 7),), ((1, 0, 2),), ((1, 2, 4),), ((1, 6, 2), (0, 7, 1)))
MIDDLE = ((1, 0, 6),)
EIGHTHS = 8
VMEM_BYTES = 20 * 1024 * 1024
DIAGONALS_VMEM_BYTES = 56 * 1024 * 1024

STRAIGHT = ((0, 3), (2, 5), (3, 6), (4, 1), (5, 2), (7, 4))
CROSS = ((1, 4), (3, 0), (4, 7), (6, 3))
DETOURS = ((1, 0, 4), (6, 7, 3))
EDGES = ((3, 0), (4, 7))

TO_HUBS = ((3, 1), (4, 6))
BETWEEN_HUBS = ((1, 6), (6, 1))
FROM_HUBS = (((1, 3), (6, 4)), ((1, 5), (6, 2)), ((1, 7), (6, 0)))


def shifted(block, axis, distance):
    devices = range(lax.axis_size(axis))
    return lax.ppermute(
        block, axis, [(i - distance, i) for i in devices if i - distance in devices]
    )


def any_of(own, energies):
    return functools.reduce(jnp.logical_or, [own == energy for energy in energies])


def side_weight(own, route, low, high):
    from_low = any_of(own, [target for source, target in route if source < target])
    from_high = any_of(own, [target for source, target in route if source > target])
    return jnp.where(from_low, low, jnp.where(from_high, high, 0.0))


def doubled(block, axis, step):
    other = lax.ppermute(block, axis, [(i, i ^ step) for i in range(lax.axis_size(axis))])
    upper = (lax.axis_index(axis) & step) != 0
    return jnp.concatenate(
        [jnp.where(upper, other, block), jnp.where(upper, block, other)], axis=0
    )


def diagonals_body(tile, lesser_ref, greater_ref, out_ref, tiles, arrived):
    count = tiles.shape[0]
    copies = [
        pltpu.make_async_copy(
            lesser_ref.at[0, 0, 1, pl.ds(n * tile, tile), pl.ds(n * tile, tile)],
            tiles.at[n],
            arrived.at[n],
        )
        for n in range(count)
    ]
    for copy in copies:
        copy.start()
    row = lax.broadcasted_iota(jnp.int32, (tile, tile), 0)
    col = lax.broadcasted_iota(jnp.int32, (tile, tile), 1)
    out_ref[0, 1:2] = greater_ref[0]
    for n, copy in enumerate(copies):
        copy.wait()
        block = jnp.where(row == col, tiles[n].astype(jnp.float32), 0.0)
        out_ref[0, 0:1, n * tile : (n + 1) * tile] = jnp.sum(block, axis=0, keepdims=True)


def diagonals_of(lesser, greater_diag):
    width = lesser.shape[-1]
    tile = 128
    return pl.pallas_call(
        functools.partial(diagonals_body, tile),
        in_specs=[
            pl.BlockSpec(memory_space=pltpu.HBM),
            pl.BlockSpec(memory_space=pltpu.VMEM),
        ],
        out_specs=pl.BlockSpec(memory_space=pltpu.VMEM),
        out_shape=jax.ShapeDtypeStruct((1, 2, width), jnp.float32),
        scratch_shapes=[
            pltpu.VMEM((width // tile, tile, tile), lesser.dtype),
            pltpu.SemaphoreType.DMA((width // tile,)),
        ],
        compiler_params=pltpu.CompilerParams(vmem_limit_bytes=DIAGONALS_VMEM_BYTES),
        name="diagonals",
    )(lesser, greater_diag)


def lag_kernel(rows, cols, phonon_lags, first, second):
    offset = cols[None, :] - rows[:, None]
    upward = (offset[None, :, :] == phonon_lags[:, None, None]).astype(jnp.float32)
    downward = (offset[None, :, :] == -phonon_lags[:, None, None]).astype(jnp.float32)
    return jnp.sum(first[:, None, None] * upward + second[:, None, None] * downward, axis=0)


def left_body(chunk, lesser_ref, dipole_ref, left_ref):
    width = left_ref.shape[0]
    unit, rows = width // EIGHTHS, width // 4
    at = 0
    for part, first, eighths in chunk:
        cols = eighths * unit
        for i in range(0, width, rows):
            left_ref[i : i + rows, at : at + cols] = lax.dot_general(
                lesser_ref[0, 0, part, i : i + rows],
                dipole_ref[0, first * unit : first * unit + cols],
                (((1,), (1,)), ((), ())),
                preferred_element_type=jnp.float32,
            ).astype(left_ref.dtype)
        at += cols


def left_of(lesser, dipole, chunk):
    width = lesser.shape[-1]
    cols = width // EIGHTHS * sum(eighths for _, _, eighths in chunk)
    return pl.pallas_call(
        functools.partial(left_body, chunk),
        in_specs=[pl.BlockSpec(memory_space=pltpu.VMEM)] * 2,
        out_specs=pl.BlockSpec(memory_space=pltpu.VMEM),
        out_shape=jax.ShapeDtypeStruct((width, cols), lesser.dtype),
        compiler_params=pltpu.CompilerParams(vmem_limit_bytes=VMEM_BYTES),
        name="left",
    )(lesser, dipole)


def pieces_of(chunk):
    pieces, place = [], 0
    for part, first, eighths in chunk:
        for at in range(first, first + eighths, 2):
            size = min(2, first + eighths - at)
            pieces.append((part, at, place, size))
            place += size
    return pieces


def photon_body(chunk, skips, factors_ref, dipole_ref, phonon_ref, own_ref, *rest):
    sides, (out_ref, results, sent) = rest[: len(skips)], rest[-3:]
    width = own_ref.shape[0]
    unit = width // EIGHTHS
    factors = [factors_ref[n] for n in range(2 + len(skips))]
    copies = []
    for k, (part, at, place, size) in enumerate(pieces_of(chunk)):
        at, place, cols = at * unit, place * unit, size * unit

        def piece(ref, skip=0):
            return ref[:, skip * unit + place : skip * unit + place + cols].astype(jnp.float32)

        side = factors[2] * piece(sides[0], skips[0])
        for factor, ref, skip in zip(factors[3:], sides[1:], skips[1:]):
            side += factor * piece(ref, skip)
        mixed = (factors[0] * piece(own_ref) + factors[1] * side).astype(jnp.bfloat16)
        photon = jnp.dot(dipole_ref[0], mixed, preferred_element_type=jnp.float32)
        if part == 1:
            row = lax.broadcasted_iota(jnp.int32, photon.shape, 0)
            col = lax.broadcasted_iota(jnp.int32, photon.shape, 1) + at
            photon += jnp.where(row == col, phonon_ref[:, at : at + cols], 0.0)
        results[k, :, :cols] = photon.astype(results.dtype)
        copies.append(
            pltpu.make_async_copy(
                results.at[k, :, pl.ds(0, cols)],
                out_ref.at[0, 0, part, :, pl.ds(at, cols)],
                sent.at[k],
            )
        )
        copies[-1].start()
    for copy in copies:
        copy.wait()


def photon_of(chunk, factors, dipole, phonon, own, sides, out):
    width = own.shape[0]
    sides, skips = zip(*sides)
    n_pieces = len(pieces_of(chunk))
    operands = [factors, dipole, phonon, own, *sides]
    in_specs = [pl.BlockSpec(memory_space=pltpu.SMEM)]
    in_specs += [pl.BlockSpec(memory_space=pltpu.VMEM)] * (len(operands) - 1)
    aliases = {}
    if out is not None:
        aliases = {len(operands): 0}
        operands.append(out)
        in_specs.append(pl.BlockSpec(memory_space=pl.ANY))
    return pl.pallas_call(
        functools.partial(photon_body, chunk, skips),
        in_specs=in_specs,
        out_specs=pl.BlockSpec(memory_space=pl.ANY),
        out_shape=jax.ShapeDtypeStruct((1, 1, 2, width, width), jnp.bfloat16),
        scratch_shapes=[
            pltpu.VMEM((n_pieces, width, 2 * width // EIGHTHS), jnp.bfloat16),
            pltpu.SemaphoreType.DMA((n_pieces,)),
        ],
        input_output_aliases=aliases,
        compiler_params=pltpu.CompilerParams(vmem_limit_bytes=VMEM_BYTES),
        name="photon",
    )(*operands)


def on_device(
    lesser,
    greater_diag,
    dipole,
    photon_weights,
    sidebands,
    phonon_lags,
    phonon_strengths,
    slab_coupling,
):
    e_count = lesser.shape[0]
    width = lesser.shape[-1]
    count = lax.axis_size("energy")
    own = lax.axis_index("energy")
    everyone = doubled(diagonals_of(lesser, greater_diag), "energy", 1)
    left = [left_of(lesser, dipole, chunk) for chunk in CHUNKS]
    everyone, left[0] = lax.optimization_barrier((everyone, left[0]))
    weight_0, weight_low, weight_high = photon_weights[0]
    flag = sidebands[0].astype(jnp.float32)
    if count == 8:
        first, second = {}, {}
        hops = tuple((source, by) for source, by, _ in DETOURS)
        second_hops = tuple((by, target) for _, by, target in DETOURS)
        first[0] = lax.ppermute(left[0], "energy", STRAIGHT + hops)
        first[1] = lax.ppermute(left[1], "energy", STRAIGHT)

        is_low = own < count // 2
        for route in (TO_HUBS, BETWEEN_HUBS):
            other = lax.ppermute(everyone, "energy", route)
            everyone = jnp.concatenate(
                [jnp.where(is_low, everyone, other), jnp.where(is_low, other, everyone)], axis=0
            )
        held = jnp.where(any_of(own, [hub for hub, _ in BETWEEN_HUBS]), everyone, 0.0)
        for route in FROM_HUBS:
            held += lax.ppermute(everyone, "energy", route)
        everyone = held

        middle = left_of(lesser, dipole, MIDDLE)
        first[0], everyone, *left, middle = lax.optimization_barrier(
            (first[0], everyone, *left, middle)
        )
        relays = any_of(own, [by for by, _ in second_hops])
        onward = jnp.where(relays, first[0], left[0])
        second[0] = lax.ppermute(onward, "energy", EDGES + second_hops)
        first[1], left[2], left[3], middle = lax.optimization_barrier(
            (first[1], left[2], left[3], middle)
        )
        crossed = lax.ppermute(middle, "energy", CROSS)
        first[2] = lax.ppermute(left[2], "energy", STRAIGHT)
        second[3] = lax.ppermute(left[3], "energy", CROSS)
        first[3] = lax.ppermute(left[3], "energy", STRAIGHT)
        weights = [
            side_weight(own, STRAIGHT, weight_low, weight_high),
            side_weight(own, CROSS, weight_low, weight_high),
        ]
    else:
        step = 2
        while step < count:
            everyone = doubled(everyone, "energy", step)
            step *= 2
        first = [shifted(block, "energy", PHOT_BLOCKS) for block in left]
        second = [shifted(block, "energy", -PHOT_BLOCKS) for block in left]
        weights = [weight_low, weight_high]
    factors = jnp.stack([weight_0, flag, *weights])
    if count == 8:
        sides = [
            [(first[0], 0), (second[0], 0)],
            [(first[1], 0), (crossed, 0)],
            [(first[2], 0), (crossed, 2)],
            [(first[3], 0), (second[3], 0)],
        ]
    else:
        sides = [[(low, 0), (high, 0)] for low, high in zip(first, second)]

    own_rows = own * e_count + jnp.arange(e_count, dtype=jnp.int32)
    all_rows = jnp.arange(e_count * count, dtype=jnp.int32)
    k_less = lag_kernel(own_rows, all_rows, phonon_lags, phonon_strengths[0], phonon_strengths[1])
    k_great = lag_kernel(own_rows, all_rows, phonon_lags, phonon_strengths[1], phonon_strengths[0])
    corr_less = jnp.sum(k_less[0][:, None] * everyone[:, 0], axis=0)
    corr_great = jnp.sum(k_great[0][:, None] * everyone[:, 1], axis=0)
    correlated = jnp.stack([corr_less, corr_great])
    below = shifted(slab_coupling * correlated, "slab", 1)
    above = shifted(correlated, "slab", -1)
    phon_less, phon_great = correlated + below + slab_coupling * above

    out = None
    for n, chunk in enumerate(CHUNKS):
        out = photon_of(chunk, factors, dipole, phon_less[None], left[n], sides[n], out)
    return out, phon_great[None, None]


def solution(mesh):
    return jax.shard_map(
        on_device,
        mesh=mesh,
        in_specs=(
            P("energy", "slab", None, None, None),
            P("energy", "slab", None),
            P("slab", None, None),
            P("energy", None),
            P("energy"),
            P(),
            P(),
            P("slab", None),
        ),
        out_specs=(P("energy", "slab", None, None, None), P("energy", "slab", None)),
        check_vma=False,
    )
```

```python
import functools

import jax
import jax.numpy as jnp
from jax import lax
from jax.experimental import pallas as pl
from jax.experimental.pallas import tpu as pltpu
from jax.sharding import PartitionSpec as P

PHOT_BLOCKS = 3
CHUNKS = (((0, 0, 7),), ((1, 0, 2),), ((1, 2, 5),), ((1, 7, 1), (0, 7, 1)))
MIDDLE = ((1, 0, 7),)
EIGHTHS = 8
VMEM_BYTES = 20 * 1024 * 1024
EARLY_VMEM_BYTES = 56 * 1024 * 1024
FIRST_VMEM_BYTES = 48 * 1024 * 1024

STRAIGHT = ((0, 3), (2, 5), (3, 6), (4, 1), (5, 2), (7, 4))
CROSS = ((1, 4), (3, 0), (4, 7), (6, 3))
DETOURS = ((1, 0, 4), (6, 7, 3))
EDGES = ((3, 0), (4, 7))

TO_HUBS = ((3, 1), (4, 6))
BETWEEN_HUBS = ((1, 6), (6, 1))
FROM_HUBS = (((1, 3), (6, 4)), ((1, 5), (6, 2)), ((1, 7), (6, 0)))


def shifted(block, axis, distance):
    devices = range(lax.axis_size(axis))
    return lax.ppermute(
        block, axis, [(i - distance, i) for i in devices if i - distance in devices]
    )


def any_of(own, energies):
    return functools.reduce(jnp.logical_or, [own == energy for energy in energies])


def side_weight(own, route, low, high):
    from_low = any_of(own, [target for source, target in route if source < target])
    from_high = any_of(own, [target for source, target in route if source > target])
    return jnp.where(from_low, low, jnp.where(from_high, high, 0.0))


def doubled(block, axis, step):
    other = lax.ppermute(block, axis, [(i, i ^ step) for i in range(lax.axis_size(axis))])
    upper = (lax.axis_index(axis) & step) != 0
    return jnp.concatenate(
        [jnp.where(upper, other, block), jnp.where(upper, block, other)], axis=0
    )


def diagonals_body(tile, lesser_ref, greater_ref, out_ref, tiles, arrived):
    count = tiles.shape[0]
    copies = [
        pltpu.make_async_copy(
            lesser_ref.at[0, 0, 1, pl.ds(n * tile, tile), pl.ds(n * tile, tile)],
            tiles.at[n],
            arrived.at[n],
        )
        for n in range(count)
    ]
    for copy in copies:
        copy.start()
    row = lax.broadcasted_iota(jnp.int32, (tile, tile), 0)
    col = lax.broadcasted_iota(jnp.int32, (tile, tile), 1)
    out_ref[0, 1:2] = greater_ref[0]
    for n, copy in enumerate(copies):
        copy.wait()
        block = jnp.where(row == col, tiles[n].astype(jnp.float32), 0.0)
        out_ref[0, 0:1, n * tile : (n + 1) * tile] = jnp.sum(block, axis=0, keepdims=True)


def diagonals_of(lesser, greater_diag):
    width = lesser.shape[-1]
    tile = 128
    return pl.pallas_call(
        functools.partial(diagonals_body, tile),
        in_specs=[
            pl.BlockSpec(memory_space=pltpu.HBM),
            pl.BlockSpec(memory_space=pltpu.VMEM),
        ],
        out_specs=pl.BlockSpec(memory_space=pltpu.VMEM),
        out_shape=jax.ShapeDtypeStruct((1, 2, width), jnp.float32),
        scratch_shapes=[
            pltpu.VMEM((width // tile, tile, tile), lesser.dtype),
            pltpu.SemaphoreType.DMA((width // tile,)),
        ],
        compiler_params=pltpu.CompilerParams(vmem_limit_bytes=EARLY_VMEM_BYTES),
        name="diagonals",
    )(lesser, greater_diag)


def lag_kernel(rows, cols, phonon_lags, first, second):
    offset = cols[None, :] - rows[:, None]
    upward = (offset[None, :, :] == phonon_lags[:, None, None]).astype(jnp.float32)
    downward = (offset[None, :, :] == -phonon_lags[:, None, None]).astype(jnp.float32)
    return jnp.sum(first[:, None, None] * upward + second[:, None, None] * downward, axis=0)


def left_body(chunk, lesser_ref, dipole_ref, left_ref, blocks, arrived):
    width = left_ref.shape[0]
    unit, rows = width // EIGHTHS, width // 4
    copies = [
        [
            pltpu.make_async_copy(
                lesser_ref.at[0, 0, part, pl.ds(i, rows)],
                blocks.at[n, pl.ds(i, rows)],
                arrived.at[n, i // rows],
            )
            for i in range(0, width, rows)
        ]
        for n, (part, _, _) in enumerate(chunk)
    ]
    for copy in sum(copies, []):
        copy.start()
    at = 0
    for n, (_, first, eighths) in enumerate(chunk):
        cols = eighths * unit
        for i in range(0, width, rows):
            copies[n][i // rows].wait()
            left_ref[i : i + rows, at : at + cols] = lax.dot_general(
                blocks[n, i : i + rows],
                dipole_ref[0, first * unit : first * unit + cols],
                (((1,), (1,)), ((), ())),
                preferred_element_type=jnp.float32,
            ).astype(left_ref.dtype)
        at += cols


def left_of(lesser, dipole, chunk, vmem_bytes=VMEM_BYTES):
    width = lesser.shape[-1]
    cols = width // EIGHTHS * sum(eighths for _, _, eighths in chunk)
    return pl.pallas_call(
        functools.partial(left_body, chunk),
        in_specs=[
            pl.BlockSpec(memory_space=pl.ANY),
            pl.BlockSpec(memory_space=pltpu.VMEM),
        ],
        out_specs=pl.BlockSpec(memory_space=pltpu.VMEM),
        out_shape=jax.ShapeDtypeStruct((width, cols), lesser.dtype),
        scratch_shapes=[
            pltpu.VMEM((len(chunk), width, width), lesser.dtype),
            pltpu.SemaphoreType.DMA((len(chunk), 4)),
        ],
        compiler_params=pltpu.CompilerParams(vmem_limit_bytes=vmem_bytes),
        name="left",
    )(lesser, dipole)


def either_body(flag_ref, yes_ref, no_ref, out_ref):
    @pl.when(flag_ref[0] != 0)
    def _():
        out_ref[...] = yes_ref[...]

    @pl.when(flag_ref[0] == 0)
    def _():
        out_ref[...] = no_ref[...]


def either_of(flag, yes, no):
    return pl.pallas_call(
        either_body,
        in_specs=[
            pl.BlockSpec(memory_space=pltpu.SMEM),
            pl.BlockSpec(memory_space=pltpu.VMEM),
            pl.BlockSpec(memory_space=pltpu.VMEM),
        ],
        out_specs=pl.BlockSpec(memory_space=pltpu.VMEM),
        out_shape=jax.ShapeDtypeStruct(yes.shape, yes.dtype),
        compiler_params=pltpu.CompilerParams(vmem_limit_bytes=VMEM_BYTES),
        name="either",
    )(flag.astype(jnp.int32).reshape(1), yes, no)


def pieces_of(chunk):
    pieces, place = [], 0
    for part, first, eighths in chunk:
        for at in range(first, first + eighths, 2):
            size = min(2, first + eighths - at)
            pieces.append((part, at, place, size))
            place += size
    return pieces


def photon_body(chunk, skips, factors_ref, dipole_ref, phonon_ref, own_ref, *rest):
    sides, (out_ref, results, sent) = rest[: len(skips)], rest[-3:]
    width = own_ref.shape[0]
    unit = width // EIGHTHS
    factors = [factors_ref[n] for n in range(2 + len(skips))]
    copies = []
    for k, (part, at, place, size) in enumerate(pieces_of(chunk)):
        at, place, cols = at * unit, place * unit, size * unit

        def piece(ref, skip=0):
            return ref[:, skip * unit + place : skip * unit + place + cols].astype(jnp.float32)

        side = factors[2] * piece(sides[0], skips[0])
        for factor, ref, skip in zip(factors[3:], sides[1:], skips[1:]):
            side += factor * piece(ref, skip)
        mixed = (factors[0] * piece(own_ref) + factors[1] * side).astype(jnp.bfloat16)
        photon = jnp.dot(dipole_ref[0], mixed, preferred_element_type=jnp.float32)
        if part == 1:
            row = lax.broadcasted_iota(jnp.int32, photon.shape, 0)
            col = lax.broadcasted_iota(jnp.int32, photon.shape, 1) + at
            photon += jnp.where(row == col, phonon_ref[:, at : at + cols], 0.0)
        results[k, :, :cols] = photon.astype(results.dtype)
        copies.append(
            pltpu.make_async_copy(
                results.at[k, :, pl.ds(0, cols)],
                out_ref.at[0, 0, part, :, pl.ds(at, cols)],
                sent.at[k],
            )
        )
        copies[-1].start()
    for copy in copies:
        copy.wait()


def photon_of(chunk, factors, dipole, phonon, own, sides, out):
    width = own.shape[0]
    sides, skips = zip(*sides)
    n_pieces = len(pieces_of(chunk))
    operands = [factors, dipole, phonon, own, *sides]
    in_specs = [pl.BlockSpec(memory_space=pltpu.SMEM)]
    in_specs += [pl.BlockSpec(memory_space=pltpu.VMEM)] * (len(operands) - 1)
    aliases = {}
    if out is not None:
        aliases = {len(operands): 0}
        operands.append(out)
        in_specs.append(pl.BlockSpec(memory_space=pl.ANY))
    return pl.pallas_call(
        functools.partial(photon_body, chunk, skips),
        in_specs=in_specs,
        out_specs=pl.BlockSpec(memory_space=pl.ANY),
        out_shape=jax.ShapeDtypeStruct((1, 1, 2, width, width), jnp.bfloat16),
        scratch_shapes=[
            pltpu.VMEM((n_pieces, width, 2 * width // EIGHTHS), jnp.bfloat16),
            pltpu.SemaphoreType.DMA((n_pieces,)),
        ],
        input_output_aliases=aliases,
        compiler_params=pltpu.CompilerParams(vmem_limit_bytes=VMEM_BYTES),
        name="photon",
    )(*operands)


def on_device(
    lesser,
    greater_diag,
    dipole,
    photon_weights,
    sidebands,
    phonon_lags,
    phonon_strengths,
    slab_coupling,
):
    e_count = lesser.shape[0]
    width = lesser.shape[-1]
    count = lax.axis_size("energy")
    own = lax.axis_index("energy")
    everyone = doubled(diagonals_of(lesser, greater_diag), "energy", 1)
    left = [left_of(lesser, dipole, CHUNKS[0], FIRST_VMEM_BYTES)]
    left += [left_of(lesser, dipole, chunk) for chunk in CHUNKS[1:]]
    everyone, left[0] = lax.optimization_barrier((everyone, left[0]))
    weight_0, weight_low, weight_high = photon_weights[0]
    flag = sidebands[0].astype(jnp.float32)
    if count == 8:
        first, second = {}, {}
        hops = tuple((source, by) for source, by, _ in DETOURS)
        second_hops = tuple((by, target) for _, by, target in DETOURS)
        first[0] = lax.ppermute(left[0], "energy", STRAIGHT + hops)
        first[1] = lax.ppermute(left[1], "energy", STRAIGHT)

        is_low = own < count // 2
        for route in (TO_HUBS, BETWEEN_HUBS):
            other = lax.ppermute(everyone, "energy", route)
            everyone = jnp.concatenate(
                [jnp.where(is_low, everyone, other), jnp.where(is_low, other, everyone)], axis=0
            )
        held = jnp.where(any_of(own, [hub for hub, _ in BETWEEN_HUBS]), everyone, 0.0)
        for route in FROM_HUBS:
            held += lax.ppermute(everyone, "energy", route)
        everyone = held

        middle = left_of(lesser, dipole, MIDDLE)
        first[0], everyone, *left, middle = lax.optimization_barrier(
            (first[0], everyone, *left, middle)
        )
        relays = any_of(own, [by for by, _ in second_hops])
        onward = either_of(relays, first[0], left[0])
        second[0] = lax.ppermute(onward, "energy", EDGES + second_hops)
        crossed = lax.ppermute(middle, "energy", CROSS)
        first[1], left[2], left[3] = lax.optimization_barrier((first[1], left[2], left[3]))
        first[2] = lax.ppermute(left[2], "energy", STRAIGHT)
        second[3] = lax.ppermute(left[3], "energy", CROSS)
        first[3] = lax.ppermute(left[3], "energy", STRAIGHT)
        weights = [
            side_weight(own, STRAIGHT, weight_low, weight_high),
            side_weight(own, CROSS, weight_low, weight_high),
        ]
    else:
        step = 2
        while step < count:
            everyone = doubled(everyone, "energy", step)
            step *= 2
        first = [shifted(block, "energy", PHOT_BLOCKS) for block in left]
        second = [shifted(block, "energy", -PHOT_BLOCKS) for block in left]
        weights = [weight_low, weight_high]
    factors = jnp.stack([weight_0, flag, *weights])
    if count == 8:
        sides = [
            [(first[0], 0), (second[0], 0)],
            [(first[1], 0), (crossed, 0)],
            [(first[2], 0), (crossed, 2)],
            [(first[3], 0), (second[3], 0)],
        ]
    else:
        sides = [[(low, 0), (high, 0)] for low, high in zip(first, second)]

    own_rows = own * e_count + jnp.arange(e_count, dtype=jnp.int32)
    all_rows = jnp.arange(e_count * count, dtype=jnp.int32)
    k_less = lag_kernel(own_rows, all_rows, phonon_lags, phonon_strengths[0], phonon_strengths[1])
    k_great = lag_kernel(own_rows, all_rows, phonon_lags, phonon_strengths[1], phonon_strengths[0])
    corr_less = jnp.sum(k_less[0][:, None] * everyone[:, 0], axis=0)
    corr_great = jnp.sum(k_great[0][:, None] * everyone[:, 1], axis=0)
    correlated = jnp.stack([corr_less, corr_great])
    below = shifted(slab_coupling * correlated, "slab", 1)
    above = shifted(correlated, "slab", -1)
    phon_less, phon_great = correlated + below + slab_coupling * above

    out = None
    for n, chunk in enumerate(CHUNKS):
        out = photon_of(chunk, factors, dipole, phon_less[None], left[n], sides[n], out)
    return out, phon_great[None, None]


def solution(mesh):
    return jax.shard_map(
        on_device,
        mesh=mesh,
        in_specs=(
            P("energy", "slab", None, None, None),
            P("energy", "slab", None),
            P("slab", None, None),
            P("energy", None),
            P("energy"),
            P(),
            P(),
            P("slab", None),
        ),
        out_specs=(P("energy", "slab", None, None, None), P("energy", "slab", None)),
        check_vma=False,
    )
```

```python
import functools

import jax
import jax.numpy as jnp
from jax import lax
from jax.experimental import pallas as pl
from jax.experimental.pallas import tpu as pltpu
from jax.sharding import PartitionSpec as P

PHOT_BLOCKS = 3
CHUNKS = (((0, 0, 7),), ((1, 0, 2),), ((1, 2, 5),), ((1, 7, 1), (0, 7, 1)))
MIDDLE = ((1, 0, 7),)
EIGHTHS = 8
VMEM_BYTES = 20 * 1024 * 1024
EARLY_VMEM_BYTES = 53 * 1024 * 1024
FIRST_VMEM_BYTES = 48 * 1024 * 1024

STRAIGHT = ((0, 3), (2, 5), (3, 6), (4, 1), (5, 2), (7, 4))
CROSS = ((1, 4), (3, 0), (4, 7), (6, 3))
DETOURS = ((1, 0, 4), (6, 7, 3))
EDGES = ((3, 0), (4, 7))

TO_HUBS = ((3, 1), (4, 6))
BETWEEN_HUBS = ((1, 6), (6, 1))
FROM_HUBS = (((1, 3), (6, 4)), ((1, 5), (6, 2)), ((1, 7), (6, 0)))


def shifted(block, axis, distance):
    devices = range(lax.axis_size(axis))
    return lax.ppermute(
        block, axis, [(i - distance, i) for i in devices if i - distance in devices]
    )


def any_of(own, energies):
    return functools.reduce(jnp.logical_or, [own == energy for energy in energies])


def side_weight(own, route, low, high):
    from_low = any_of(own, [target for source, target in route if source < target])
    from_high = any_of(own, [target for source, target in route if source > target])
    return jnp.where(from_low, low, jnp.where(from_high, high, 0.0))


def doubled(block, axis, step):
    other = lax.ppermute(block, axis, [(i, i ^ step) for i in range(lax.axis_size(axis))])
    upper = (lax.axis_index(axis) & step) != 0
    return jnp.concatenate(
        [jnp.where(upper, other, block), jnp.where(upper, block, other)], axis=0
    )


def diagonals_body(tile, lesser_ref, greater_ref, out_ref, tiles, arrived):
    count = tiles.shape[0]
    copies = [
        pltpu.make_async_copy(
            lesser_ref.at[0, 0, 1, pl.ds(n * tile, tile), pl.ds(n * tile, tile)],
            tiles.at[n],
            arrived.at[n],
        )
        for n in range(count)
    ]
    for copy in copies:
        copy.start()
    row = lax.broadcasted_iota(jnp.int32, (tile, tile), 0)
    col = lax.broadcasted_iota(jnp.int32, (tile, tile), 1)
    out_ref[0, 1:2] = greater_ref[0]
    for n, copy in enumerate(copies):
        copy.wait()
        block = jnp.where(row == col, tiles[n].astype(jnp.float32), 0.0)
        out_ref[0, 0:1, n * tile : (n + 1) * tile] = jnp.sum(block, axis=0, keepdims=True)


def diagonals_of(lesser, greater_diag):
    width = lesser.shape[-1]
    tile = 128
    return pl.pallas_call(
        functools.partial(diagonals_body, tile),
        in_specs=[
            pl.BlockSpec(memory_space=pltpu.HBM),
            pl.BlockSpec(memory_space=pltpu.VMEM),
        ],
        out_specs=pl.BlockSpec(memory_space=pltpu.VMEM),
        out_shape=jax.ShapeDtypeStruct((1, 2, width), jnp.float32),
        scratch_shapes=[
            pltpu.VMEM((width // tile, tile, tile), lesser.dtype),
            pltpu.SemaphoreType.DMA((width // tile,)),
        ],
        compiler_params=pltpu.CompilerParams(vmem_limit_bytes=EARLY_VMEM_BYTES),
        name="diagonals",
    )(lesser, greater_diag)


def lag_kernel(rows, cols, phonon_lags, first, second):
    offset = cols[None, :] - rows[:, None]
    upward = (offset[None, :, :] == phonon_lags[:, None, None]).astype(jnp.float32)
    downward = (offset[None, :, :] == -phonon_lags[:, None, None]).astype(jnp.float32)
    return jnp.sum(first[:, None, None] * upward + second[:, None, None] * downward, axis=0)


def left_body(chunk, lesser_ref, dipole_ref, left_ref, blocks, arrived):
    width = left_ref.shape[0]
    unit, rows = width // EIGHTHS, width // 4
    copies = [
        [
            pltpu.make_async_copy(
                lesser_ref.at[0, 0, part, pl.ds(i, rows)],
                blocks.at[n, pl.ds(i, rows)],
                arrived.at[n, i // rows],
            )
            for i in range(0, width, rows)
        ]
        for n, (part, _, _) in enumerate(chunk)
    ]
    for copy in sum(copies, []):
        copy.start()
    at = 0
    for n, (_, first, eighths) in enumerate(chunk):
        cols = eighths * unit
        for i in range(0, width, rows):
            copies[n][i // rows].wait()
            left_ref[i : i + rows, at : at + cols] = lax.dot_general(
                blocks[n, i : i + rows],
                dipole_ref[0, first * unit : first * unit + cols],
                (((1,), (1,)), ((), ())),
                preferred_element_type=jnp.float32,
            ).astype(left_ref.dtype)
        at += cols


def left_of(lesser, dipole, chunk, vmem_bytes=VMEM_BYTES):
    width = lesser.shape[-1]
    cols = width // EIGHTHS * sum(eighths for _, _, eighths in chunk)
    return pl.pallas_call(
        functools.partial(left_body, chunk),
        in_specs=[
            pl.BlockSpec(memory_space=pl.ANY),
            pl.BlockSpec(memory_space=pltpu.VMEM),
        ],
        out_specs=pl.BlockSpec(memory_space=pltpu.VMEM),
        out_shape=jax.ShapeDtypeStruct((width, cols), lesser.dtype),
        scratch_shapes=[
            pltpu.VMEM((len(chunk), width, width), lesser.dtype),
            pltpu.SemaphoreType.DMA((len(chunk), 4)),
        ],
        compiler_params=pltpu.CompilerParams(vmem_limit_bytes=vmem_bytes),
        name="left",
    )(lesser, dipole)


def replaced_body(flag_ref, new_ref, old_ref, out_ref, sent):
    del old_ref

    @pl.when(flag_ref[0] != 0)
    def _():
        copy = pltpu.make_async_copy(new_ref, out_ref, sent)
        copy.start()
        copy.wait()


def replaced_of(flag, new, old):
    return pl.pallas_call(
        replaced_body,
        in_specs=[
            pl.BlockSpec(memory_space=pltpu.SMEM),
            pl.BlockSpec(memory_space=pl.ANY),
            pl.BlockSpec(memory_space=pl.ANY),
        ],
        out_specs=pl.BlockSpec(memory_space=pl.ANY),
        out_shape=jax.ShapeDtypeStruct(new.shape, new.dtype),
        scratch_shapes=[pltpu.SemaphoreType.DMA],
        input_output_aliases={2: 0},
        compiler_params=pltpu.CompilerParams(vmem_limit_bytes=VMEM_BYTES),
        name="replaced",
    )(flag.astype(jnp.int32).reshape(1), new, old)


def held_body(block_ref, out_ref):
    out_ref[...] = block_ref[...]


def held_of(block):
    return pl.pallas_call(
        held_body,
        in_specs=[pl.BlockSpec(memory_space=pltpu.VMEM)],
        out_specs=pl.BlockSpec(memory_space=pltpu.VMEM),
        out_shape=jax.ShapeDtypeStruct(block.shape, block.dtype),
        cost_estimate=pl.CostEstimate(flops=4000000000, bytes_accessed=0, transcendentals=0),
        compiler_params=pltpu.CompilerParams(vmem_limit_bytes=VMEM_BYTES),
        name="held",
    )(block)


def pieces_of(chunk):
    pieces, place = [], 0
    for part, first, eighths in chunk:
        for at in range(first, first + eighths, 2):
            size = min(2, first + eighths - at)
            pieces.append((part, at, place, size))
            place += size
    return pieces


def photon_body(chunk, skips, factors_ref, dipole_ref, phonon_ref, own_ref, *rest):
    sides, (out_ref, results, sent) = rest[: len(skips)], rest[-3:]
    width = own_ref.shape[0]
    unit = width // EIGHTHS
    factors = [factors_ref[n] for n in range(2 + len(skips))]
    copies = []
    for k, (part, at, place, size) in enumerate(pieces_of(chunk)):
        at, place, cols = at * unit, place * unit, size * unit

        def piece(ref, skip=0):
            return ref[:, skip * unit + place : skip * unit + place + cols].astype(jnp.float32)

        side = factors[2] * piece(sides[0], skips[0])
        for factor, ref, skip in zip(factors[3:], sides[1:], skips[1:]):
            side += factor * piece(ref, skip)
        mixed = (factors[0] * piece(own_ref) + factors[1] * side).astype(jnp.bfloat16)
        photon = jnp.dot(dipole_ref[0], mixed, preferred_element_type=jnp.float32)
        if part == 1:
            row = lax.broadcasted_iota(jnp.int32, photon.shape, 0)
            col = lax.broadcasted_iota(jnp.int32, photon.shape, 1) + at
            photon += jnp.where(row == col, phonon_ref[:, at : at + cols], 0.0)
        results[k, :, :cols] = photon.astype(results.dtype)
        copies.append(
            pltpu.make_async_copy(
                results.at[k, :, pl.ds(0, cols)],
                out_ref.at[0, 0, part, :, pl.ds(at, cols)],
                sent.at[k],
            )
        )
        copies[-1].start()
    for copy in copies:
        copy.wait()


def photon_of(chunk, factors, dipole, phonon, own, sides, out):
    width = own.shape[0]
    sides, skips = zip(*sides)
    n_pieces = len(pieces_of(chunk))
    operands = [factors, dipole, phonon, own, *sides]
    in_specs = [pl.BlockSpec(memory_space=pltpu.SMEM)]
    in_specs += [pl.BlockSpec(memory_space=pltpu.VMEM)] * (len(operands) - 1)
    aliases = {}
    if out is not None:
        aliases = {len(operands): 0}
        operands.append(out)
        in_specs.append(pl.BlockSpec(memory_space=pl.ANY))
    return pl.pallas_call(
        functools.partial(photon_body, chunk, skips),
        in_specs=in_specs,
        out_specs=pl.BlockSpec(memory_space=pl.ANY),
        out_shape=jax.ShapeDtypeStruct((1, 1, 2, width, width), jnp.bfloat16),
        scratch_shapes=[
            pltpu.VMEM((n_pieces, width, 2 * width // EIGHTHS), jnp.bfloat16),
            pltpu.SemaphoreType.DMA((n_pieces,)),
        ],
        input_output_aliases=aliases,
        compiler_params=pltpu.CompilerParams(vmem_limit_bytes=VMEM_BYTES),
        name="photon",
    )(*operands)


def on_device(
    lesser,
    greater_diag,
    dipole,
    photon_weights,
    sidebands,
    phonon_lags,
    phonon_strengths,
    slab_coupling,
):
    e_count = lesser.shape[0]
    width = lesser.shape[-1]
    count = lax.axis_size("energy")
    own = lax.axis_index("energy")
    everyone = doubled(diagonals_of(lesser, greater_diag), "energy", 1)
    left = [left_of(lesser, dipole, CHUNKS[0], FIRST_VMEM_BYTES)]
    left += [left_of(lesser, dipole, chunk) for chunk in CHUNKS[1:]]
    everyone, left[0] = lax.optimization_barrier((everyone, left[0]))
    weight_0, weight_low, weight_high = photon_weights[0]
    flag = sidebands[0].astype(jnp.float32)
    if count == 8:
        first, second = {}, {}
        hops = tuple((source, by) for source, by, _ in DETOURS)
        second_hops = tuple((by, target) for _, by, target in DETOURS)
        first[0] = lax.ppermute(left[0], "energy", STRAIGHT + hops)
        first[1] = lax.ppermute(left[1], "energy", STRAIGHT)

        is_low = own < count // 2
        for route in (TO_HUBS, BETWEEN_HUBS):
            other = lax.ppermute(everyone, "energy", route)
            everyone = jnp.concatenate(
                [jnp.where(is_low, everyone, other), jnp.where(is_low, other, everyone)], axis=0
            )
        held = jnp.where(any_of(own, [hub for hub, _ in BETWEEN_HUBS]), everyone, 0.0)
        for route in FROM_HUBS:
            held += lax.ppermute(everyone, "energy", route)
        everyone = held

        middle = left_of(lesser, dipole, MIDDLE)
        again = left_of(lesser, dipole, CHUNKS[0])
        first[0], everyone, *left, middle, again = lax.optimization_barrier(
            (first[0], everyone, *left, middle, again)
        )
        relays = any_of(own, [by for by, _ in second_hops])
        onward = replaced_of(relays, first[0], again)
        second[0] = lax.ppermute(onward, "energy", EDGES + second_hops)
        crossed = lax.ppermute(middle, "energy", CROSS)
        first[2] = lax.ppermute(left[2], "energy", STRAIGHT)
        first[1] = held_of(first[1])
        first[1], left[3] = lax.optimization_barrier((first[1], left[3]))
        second[3] = lax.ppermute(left[3], "energy", CROSS)
        first[3] = lax.ppermute(left[3], "energy", STRAIGHT)
        weights = [
            side_weight(own, STRAIGHT, weight_low, weight_high),
            side_weight(own, CROSS, weight_low, weight_high),
        ]
    else:
        step = 2
        while step < count:
            everyone = doubled(everyone, "energy", step)
            step *= 2
        first = [shifted(block, "energy", PHOT_BLOCKS) for block in left]
        second = [shifted(block, "energy", -PHOT_BLOCKS) for block in left]
        weights = [weight_low, weight_high]
    factors = jnp.stack([weight_0, flag, *weights])
    if count == 8:
        sides = [
            [(first[0], 0), (second[0], 0)],
            [(first[1], 0), (crossed, 0)],
            [(first[2], 0), (crossed, 2)],
            [(first[3], 0), (second[3], 0)],
        ]
    else:
        sides = [[(low, 0), (high, 0)] for low, high in zip(first, second)]

    own_rows = own * e_count + jnp.arange(e_count, dtype=jnp.int32)
    all_rows = jnp.arange(e_count * count, dtype=jnp.int32)
    k_less = lag_kernel(own_rows, all_rows, phonon_lags, phonon_strengths[0], phonon_strengths[1])
    k_great = lag_kernel(own_rows, all_rows, phonon_lags, phonon_strengths[1], phonon_strengths[0])
    corr_less = jnp.sum(k_less[0][:, None] * everyone[:, 0], axis=0)
    corr_great = jnp.sum(k_great[0][:, None] * everyone[:, 1], axis=0)
    correlated = jnp.stack([corr_less, corr_great])
    below = shifted(slab_coupling * correlated, "slab", 1)
    above = shifted(correlated, "slab", -1)
    phon_less, phon_great = correlated + below + slab_coupling * above

    out = None
    for n, chunk in enumerate(CHUNKS):
        out = photon_of(chunk, factors, dipole, phon_less[None], left[n], sides[n], out)
    return out, phon_great[None, None]


def solution(mesh):
    return jax.shard_map(
        on_device,
        mesh=mesh,
        in_specs=(
            P("energy", "slab", None, None, None),
            P("energy", "slab", None),
            P("slab", None, None),
            P("energy", None),
            P("energy"),
            P(),
            P(),
            P("slab", None),
        ),
        out_specs=(P("energy", "slab", None, None, None), P("energy", "slab", None)),
        check_vma=False,
    )
```

```python
import functools

import jax
import jax.numpy as jnp
from jax import lax
from jax.experimental import pallas as pl
from jax.experimental.pallas import tpu as pltpu
from jax.sharding import PartitionSpec as P

PHOT_BLOCKS = 3
CHUNKS = (((0, 0, 7),), ((1, 0, 2),), ((1, 2, 5),), ((1, 7, 1), (0, 7, 1)))
MIDDLE = ((1, 0, 7),)
EIGHTHS = 8
VMEM_BYTES = 20 * 1024 * 1024
EARLY_VMEM_BYTES = 53 * 1024 * 1024
FIRST_VMEM_BYTES = 48 * 1024 * 1024

STRAIGHT = ((0, 3), (2, 5), (3, 6), (4, 1), (5, 2), (7, 4))
CROSS = ((1, 4), (3, 0), (4, 7), (6, 3))
DETOURS = ((1, 0, 4), (6, 7, 3))
EDGES = ((3, 0), (4, 7))

TO_HUBS = ((3, 1), (4, 6))
BETWEEN_HUBS = ((1, 6), (6, 1))
FROM_HUBS = (((1, 3), (6, 4)), ((1, 5), (6, 2)), ((1, 7), (6, 0)))


def shifted(block, axis, distance):
    devices = range(lax.axis_size(axis))
    return lax.ppermute(
        block, axis, [(i - distance, i) for i in devices if i - distance in devices]
    )


def any_of(own, energies):
    return functools.reduce(jnp.logical_or, [own == energy for energy in energies])


def side_weight(own, route, low, high):
    from_low = any_of(own, [target for source, target in route if source < target])
    from_high = any_of(own, [target for source, target in route if source > target])
    return jnp.where(from_low, low, jnp.where(from_high, high, 0.0))


def doubled(block, axis, step):
    other = lax.ppermute(block, axis, [(i, i ^ step) for i in range(lax.axis_size(axis))])
    upper = (lax.axis_index(axis) & step) != 0
    return jnp.concatenate(
        [jnp.where(upper, other, block), jnp.where(upper, block, other)], axis=0
    )


def diagonals_body(tile, lesser_ref, greater_ref, out_ref, tiles, arrived):
    count = tiles.shape[0]
    copies = [
        pltpu.make_async_copy(
            lesser_ref.at[0, 0, 1, pl.ds(n * tile, tile), pl.ds(n * tile, tile)],
            tiles.at[n],
            arrived.at[n],
        )
        for n in range(count)
    ]
    for copy in copies:
        copy.start()
    row = lax.broadcasted_iota(jnp.int32, (tile, tile), 0)
    col = lax.broadcasted_iota(jnp.int32, (tile, tile), 1)
    out_ref[0, 1:2] = greater_ref[0]
    for n, copy in enumerate(copies):
        copy.wait()
        block = jnp.where(row == col, tiles[n].astype(jnp.float32), 0.0)
        out_ref[0, 0:1, n * tile : (n + 1) * tile] = jnp.sum(block, axis=0, keepdims=True)


def diagonals_of(lesser, greater_diag):
    width = lesser.shape[-1]
    tile = 128
    return pl.pallas_call(
        functools.partial(diagonals_body, tile),
        in_specs=[
            pl.BlockSpec(memory_space=pltpu.HBM),
            pl.BlockSpec(memory_space=pltpu.VMEM),
        ],
        out_specs=pl.BlockSpec(memory_space=pltpu.VMEM),
        out_shape=jax.ShapeDtypeStruct((1, 2, width), jnp.float32),
        scratch_shapes=[
            pltpu.VMEM((width // tile, tile, tile), lesser.dtype),
            pltpu.SemaphoreType.DMA((width // tile,)),
        ],
        compiler_params=pltpu.CompilerParams(vmem_limit_bytes=EARLY_VMEM_BYTES),
        name="diagonals",
    )(lesser, greater_diag)


def lag_kernel(rows, cols, phonon_lags, first, second):
    offset = cols[None, :] - rows[:, None]
    upward = (offset[None, :, :] == phonon_lags[:, None, None]).astype(jnp.float32)
    downward = (offset[None, :, :] == -phonon_lags[:, None, None]).astype(jnp.float32)
    return jnp.sum(first[:, None, None] * upward + second[:, None, None] * downward, axis=0)


def left_body(chunk, streamed, lesser_ref, dipole_ref, left_ref, *scratch):
    width = left_ref.shape[0]
    unit, rows = width // EIGHTHS, width // 4
    starts = range(0, width, rows)
    if streamed:
        blocks, arrived = scratch
        copies = [
            pltpu.make_async_copy(
                lesser_ref.at[0, 0, chunk[0][0], pl.ds(i, rows)], blocks.at[pl.ds(i, rows)], sem
            )
            for i, sem in zip(starts, [arrived.at[n] for n in range(len(starts))])
        ]
        for copy in copies:
            copy.start()
    at = 0
    for part, first, eighths in chunk:
        cols = eighths * unit
        for n, i in enumerate(starts):
            if streamed:
                copies[n].wait()
                block = blocks[i : i + rows]
            else:
                block = lesser_ref[0, 0, part, i : i + rows]
            left_ref[i : i + rows, at : at + cols] = lax.dot_general(
                block,
                dipole_ref[0, first * unit : first * unit + cols],
                (((1,), (1,)), ((), ())),
                preferred_element_type=jnp.float32,
            ).astype(left_ref.dtype)
        at += cols


def left_of(lesser, dipole, chunk, streamed=False):
    width = lesser.shape[-1]
    cols = width // EIGHTHS * sum(eighths for _, _, eighths in chunk)
    scratch = [pltpu.VMEM((width, width), lesser.dtype), pltpu.SemaphoreType.DMA((4,))]
    return pl.pallas_call(
        functools.partial(left_body, chunk, streamed),
        in_specs=[
            pl.BlockSpec(memory_space=pl.ANY if streamed else pltpu.VMEM),
            pl.BlockSpec(memory_space=pltpu.VMEM),
        ],
        out_specs=pl.BlockSpec(memory_space=pltpu.VMEM),
        out_shape=jax.ShapeDtypeStruct((width, cols), lesser.dtype),
        scratch_shapes=scratch if streamed else [],
        compiler_params=pltpu.CompilerParams(
            vmem_limit_bytes=FIRST_VMEM_BYTES if streamed else VMEM_BYTES
        ),
        name="left",
    )(lesser, dipole)


def either_body(flag_ref, yes_ref, no_ref, out_ref):
    height = out_ref.shape[0]
    rows = height // 16

    def copied_from(ref):
        @pl.loop(0, height // rows)
        def _(i):
            at = pl.ds(pl.multiple_of(i * rows, rows), rows)
            out_ref[at] = ref[at]

    pl.when(flag_ref[0] != 0)(lambda: copied_from(yes_ref))
    pl.when(flag_ref[0] == 0)(lambda: copied_from(no_ref))


def either_of(flag, yes, no):
    return pl.pallas_call(
        either_body,
        in_specs=[
            pl.BlockSpec(memory_space=pltpu.SMEM),
            pl.BlockSpec(memory_space=pltpu.VMEM),
            pl.BlockSpec(memory_space=pltpu.VMEM),
        ],
        out_specs=pl.BlockSpec(memory_space=pltpu.VMEM),
        out_shape=jax.ShapeDtypeStruct(yes.shape, yes.dtype),
        compiler_params=pltpu.CompilerParams(vmem_limit_bytes=VMEM_BYTES),
        name="either",
    )(flag.astype(jnp.int32).reshape(1), yes, no)


def held_body(block_ref, out_ref):
    out_ref[...] = block_ref[...]


def held_of(block):
    return pl.pallas_call(
        held_body,
        in_specs=[pl.BlockSpec(memory_space=pltpu.VMEM)],
        out_specs=pl.BlockSpec(memory_space=pltpu.VMEM),
        out_shape=jax.ShapeDtypeStruct(block.shape, block.dtype),
        cost_estimate=pl.CostEstimate(flops=4000000000, bytes_accessed=0, transcendentals=0),
        compiler_params=pltpu.CompilerParams(vmem_limit_bytes=VMEM_BYTES),
        name="held",
    )(block)


def pieces_of(chunk):
    pieces, place = [], 0
    for part, first, eighths in chunk:
        for at in range(first, first + eighths, 2):
            size = min(2, first + eighths - at)
            pieces.append((part, at, place, size))
            place += size
    return pieces


def photon_body(chunk, skips, factors_ref, dipole_ref, phonon_ref, own_ref, *rest):
    sides, (out_ref, results, sent) = rest[: len(skips)], rest[-3:]
    width = own_ref.shape[0]
    unit = width // EIGHTHS
    factors = [factors_ref[n] for n in range(2 + len(skips))]
    copies = []
    for k, (part, at, place, size) in enumerate(pieces_of(chunk)):
        at, place, cols = at * unit, place * unit, size * unit

        def piece(ref, skip=0):
            return ref[:, skip * unit + place : skip * unit + place + cols].astype(jnp.float32)

        side = factors[2] * piece(sides[0], skips[0])
        for factor, ref, skip in zip(factors[3:], sides[1:], skips[1:]):
            side += factor * piece(ref, skip)
        mixed = (factors[0] * piece(own_ref) + factors[1] * side).astype(jnp.bfloat16)
        photon = jnp.dot(dipole_ref[0], mixed, preferred_element_type=jnp.float32)
        if part == 1:
            row = lax.broadcasted_iota(jnp.int32, photon.shape, 0)
            col = lax.broadcasted_iota(jnp.int32, photon.shape, 1) + at
            photon += jnp.where(row == col, phonon_ref[:, at : at + cols], 0.0)
        results[k, :, :cols] = photon.astype(results.dtype)
        copies.append(
            pltpu.make_async_copy(
                results.at[k, :, pl.ds(0, cols)],
                out_ref.at[0, 0, part, :, pl.ds(at, cols)],
                sent.at[k],
            )
        )
        copies[-1].start()
    for copy in copies:
        copy.wait()


def photon_of(chunk, factors, dipole, phonon, own, sides, out):
    width = own.shape[0]
    sides, skips = zip(*sides)
    n_pieces = len(pieces_of(chunk))
    operands = [factors, dipole, phonon, own, *sides]
    in_specs = [pl.BlockSpec(memory_space=pltpu.SMEM)]
    in_specs += [pl.BlockSpec(memory_space=pltpu.VMEM)] * (len(operands) - 1)
    aliases = {}
    if out is not None:
        aliases = {len(operands): 0}
        operands.append(out)
        in_specs.append(pl.BlockSpec(memory_space=pl.ANY))
    return pl.pallas_call(
        functools.partial(photon_body, chunk, skips),
        in_specs=in_specs,
        out_specs=pl.BlockSpec(memory_space=pl.ANY),
        out_shape=jax.ShapeDtypeStruct((1, 1, 2, width, width), jnp.bfloat16),
        scratch_shapes=[
            pltpu.VMEM((n_pieces, width, 2 * width // EIGHTHS), jnp.bfloat16),
            pltpu.SemaphoreType.DMA((n_pieces,)),
        ],
        input_output_aliases=aliases,
        compiler_params=pltpu.CompilerParams(vmem_limit_bytes=VMEM_BYTES),
        name="photon",
    )(*operands)


def on_device(
    lesser,
    greater_diag,
    dipole,
    photon_weights,
    sidebands,
    phonon_lags,
    phonon_strengths,
    slab_coupling,
):
    e_count = lesser.shape[0]
    width = lesser.shape[-1]
    count = lax.axis_size("energy")
    own = lax.axis_index("energy")
    everyone = doubled(diagonals_of(lesser, greater_diag), "energy", 1)
    left = [left_of(lesser, dipole, CHUNKS[0], streamed=True)]
    left += [left_of(lesser, dipole, chunk) for chunk in CHUNKS[1:]]
    everyone, left[0] = lax.optimization_barrier((everyone, left[0]))
    weight_0, weight_low, weight_high = photon_weights[0]
    flag = sidebands[0].astype(jnp.float32)
    if count == 8:
        first, second = {}, {}
        hops = tuple((source, by) for source, by, _ in DETOURS)
        second_hops = tuple((by, target) for _, by, target in DETOURS)
        first[0] = lax.ppermute(left[0], "energy", STRAIGHT + hops)
        first[1] = lax.ppermute(left[1], "energy", STRAIGHT)

        is_low = own < count // 2
        for route in (TO_HUBS, BETWEEN_HUBS):
            other = lax.ppermute(everyone, "energy", route)
            everyone = jnp.concatenate(
                [jnp.where(is_low, everyone, other), jnp.where(is_low, other, everyone)], axis=0
            )
        held = jnp.where(any_of(own, [hub for hub, _ in BETWEEN_HUBS]), everyone, 0.0)
        for route in FROM_HUBS:
            held += lax.ppermute(everyone, "energy", route)
        everyone = held

        middle = left_of(lesser, dipole, MIDDLE)
        first[0], everyone, *left, middle = lax.optimization_barrier(
            (first[0], everyone, *left, middle)
        )
        relays = any_of(own, [by for by, _ in second_hops])
        onward = either_of(relays, first[0], left[0])
        second[0] = lax.ppermute(onward, "energy", EDGES + second_hops)
        crossed = lax.ppermute(middle, "energy", CROSS)
        first[2] = lax.ppermute(left[2], "energy", STRAIGHT)
        first[1] = held_of(first[1])
        first[1], left[3] = lax.optimization_barrier((first[1], left[3]))
        second[3] = lax.ppermute(left[3], "energy", CROSS)
        first[3] = lax.ppermute(left[3], "energy", STRAIGHT)
        weights = [
            side_weight(own, STRAIGHT, weight_low, weight_high),
            side_weight(own, CROSS, weight_low, weight_high),
        ]
    else:
        step = 2
        while step < count:
            everyone = doubled(everyone, "energy", step)
            step *= 2
        first = [shifted(block, "energy", PHOT_BLOCKS) for block in left]
        second = [shifted(block, "energy", -PHOT_BLOCKS) for block in left]
        weights = [weight_low, weight_high]
    factors = jnp.stack([weight_0, flag, *weights])
    if count == 8:
        sides = [
            [(first[0], 0), (second[0], 0)],
            [(first[1], 0), (crossed, 0)],
            [(first[2], 0), (crossed, 2)],
            [(first[3], 0), (second[3], 0)],
        ]
    else:
        sides = [[(low, 0), (high, 0)] for low, high in zip(first, second)]

    own_rows = own * e_count + jnp.arange(e_count, dtype=jnp.int32)
    all_rows = jnp.arange(e_count * count, dtype=jnp.int32)
    k_less = lag_kernel(own_rows, all_rows, phonon_lags, phonon_strengths[0], phonon_strengths[1])
    k_great = lag_kernel(own_rows, all_rows, phonon_lags, phonon_strengths[1], phonon_strengths[0])
    corr_less = jnp.sum(k_less[0][:, None] * everyone[:, 0], axis=0)
    corr_great = jnp.sum(k_great[0][:, None] * everyone[:, 1], axis=0)
    correlated = jnp.stack([corr_less, corr_great])
    below = shifted(slab_coupling * correlated, "slab", 1)
    above = shifted(correlated, "slab", -1)
    phon_less, phon_great = correlated + below + slab_coupling * above

    out = None
    for n, chunk in enumerate(CHUNKS):
        out = photon_of(chunk, factors, dipole, phon_less[None], left[n], sides[n], out)
    return out, phon_great[None, None]


def solution(mesh):
    return jax.shard_map(
        on_device,
        mesh=mesh,
        in_specs=(
            P("energy", "slab", None, None, None),
            P("energy", "slab", None),
            P("slab", None, None),
            P("energy", None),
            P("energy"),
            P(),
            P(),
            P("slab", None),
        ),
        out_specs=(P("energy", "slab", None, None, None), P("energy", "slab", None)),
        check_vma=False,
    )
```

```python
import functools

import jax
import jax.numpy as jnp
from jax import lax
from jax.experimental import pallas as pl
from jax.experimental.pallas import tpu as pltpu
from jax.sharding import PartitionSpec as P

PHOT_BLOCKS = 3
CHUNKS = (((0, 0, 7),), ((1, 0, 1),), ((1, 1, 6),), ((1, 7, 1), (0, 7, 1)))
MIDDLE = ((1, 0, 7),)
EIGHTHS = 8
VMEM_BYTES = 20 * 1024 * 1024
EARLY_VMEM_BYTES = 53 * 1024 * 1024
FIRST_VMEM_BYTES = 48 * 1024 * 1024

STRAIGHT = ((0, 3), (2, 5), (3, 6), (4, 1), (5, 2), (7, 4))
CROSS = ((1, 4), (3, 0), (4, 7), (6, 3))
DETOURS = ((1, 0, 4), (6, 7, 3))
EDGES = ((3, 0), (4, 7))

TO_HUBS = ((3, 1), (4, 6))
BETWEEN_HUBS = ((1, 6), (6, 1))
FROM_HUBS = (((1, 3), (6, 4)), ((1, 5), (6, 2)), ((1, 7), (6, 0)))


def shifted(block, axis, distance):
    devices = range(lax.axis_size(axis))
    return lax.ppermute(
        block, axis, [(i - distance, i) for i in devices if i - distance in devices]
    )


def any_of(own, energies):
    return functools.reduce(jnp.logical_or, [own == energy for energy in energies])


def side_weight(own, route, low, high):
    from_low = any_of(own, [target for source, target in route if source < target])
    from_high = any_of(own, [target for source, target in route if source > target])
    return jnp.where(from_low, low, jnp.where(from_high, high, 0.0))


def doubled(block, axis, step):
    other = lax.ppermute(block, axis, [(i, i ^ step) for i in range(lax.axis_size(axis))])
    upper = (lax.axis_index(axis) & step) != 0
    return jnp.concatenate(
        [jnp.where(upper, other, block), jnp.where(upper, block, other)], axis=0
    )


def diagonals_body(tile, lesser_ref, greater_ref, out_ref, tiles, arrived):
    count = tiles.shape[0]
    copies = [
        pltpu.make_async_copy(
            lesser_ref.at[0, 0, 1, pl.ds(n * tile, tile), pl.ds(n * tile, tile)],
            tiles.at[n],
            arrived.at[n],
        )
        for n in range(count)
    ]
    for copy in copies:
        copy.start()
    row = lax.broadcasted_iota(jnp.int32, (tile, tile), 0)
    col = lax.broadcasted_iota(jnp.int32, (tile, tile), 1)
    out_ref[0, 1:2] = greater_ref[0]
    for n, copy in enumerate(copies):
        copy.wait()
        block = jnp.where(row == col, tiles[n].astype(jnp.float32), 0.0)
        out_ref[0, 0:1, n * tile : (n + 1) * tile] = jnp.sum(block, axis=0, keepdims=True)


def diagonals_of(lesser, greater_diag):
    width = lesser.shape[-1]
    tile = 128
    return pl.pallas_call(
        functools.partial(diagonals_body, tile),
        in_specs=[
            pl.BlockSpec(memory_space=pltpu.HBM),
            pl.BlockSpec(memory_space=pltpu.VMEM),
        ],
        out_specs=pl.BlockSpec(memory_space=pltpu.VMEM),
        out_shape=jax.ShapeDtypeStruct((1, 2, width), jnp.float32),
        scratch_shapes=[
            pltpu.VMEM((width // tile, tile, tile), lesser.dtype),
            pltpu.SemaphoreType.DMA((width // tile,)),
        ],
        compiler_params=pltpu.CompilerParams(vmem_limit_bytes=EARLY_VMEM_BYTES),
        name="diagonals",
    )(lesser, greater_diag)


def lag_kernel(rows, cols, phonon_lags, first, second):
    offset = cols[None, :] - rows[:, None]
    upward = (offset[None, :, :] == phonon_lags[:, None, None]).astype(jnp.float32)
    downward = (offset[None, :, :] == -phonon_lags[:, None, None]).astype(jnp.float32)
    return jnp.sum(first[:, None, None] * upward + second[:, None, None] * downward, axis=0)


def left_body(chunk, streamed, lesser_ref, dipole_ref, left_ref, *scratch):
    width = left_ref.shape[0]
    unit, rows = width // EIGHTHS, width // 4
    starts = range(0, width, rows)
    if streamed:
        blocks, arrived = scratch
        copies = [
            pltpu.make_async_copy(
                lesser_ref.at[0, 0, chunk[0][0], pl.ds(i, rows)], blocks.at[pl.ds(i, rows)], sem
            )
            for i, sem in zip(starts, [arrived.at[n] for n in range(len(starts))])
        ]
        for copy in copies:
            copy.start()
    at = 0
    for part, first, eighths in chunk:
        cols = eighths * unit
        for n, i in enumerate(starts):
            if streamed:
                copies[n].wait()
                block = blocks[i : i + rows]
            else:
                block = lesser_ref[0, 0, part, i : i + rows]
            left_ref[i : i + rows, at : at + cols] = lax.dot_general(
                block,
                dipole_ref[0, first * unit : first * unit + cols],
                (((1,), (1,)), ((), ())),
                preferred_element_type=jnp.float32,
            ).astype(left_ref.dtype)
        at += cols


def left_of(lesser, dipole, chunk, streamed=False):
    width = lesser.shape[-1]
    cols = width // EIGHTHS * sum(eighths for _, _, eighths in chunk)
    scratch = [pltpu.VMEM((width, width), lesser.dtype), pltpu.SemaphoreType.DMA((4,))]
    return pl.pallas_call(
        functools.partial(left_body, chunk, streamed),
        in_specs=[
            pl.BlockSpec(memory_space=pl.ANY if streamed else pltpu.VMEM),
            pl.BlockSpec(memory_space=pltpu.VMEM),
        ],
        out_specs=pl.BlockSpec(memory_space=pltpu.VMEM),
        out_shape=jax.ShapeDtypeStruct((width, cols), lesser.dtype),
        scratch_shapes=scratch if streamed else [],
        compiler_params=pltpu.CompilerParams(
            vmem_limit_bytes=FIRST_VMEM_BYTES if streamed else VMEM_BYTES
        ),
        name="left",
    )(lesser, dipole)


def either_body(flag_ref, yes_ref, no_ref, out_ref):
    height = out_ref.shape[0]
    rows = height // 16

    def copied_from(ref):
        @pl.loop(0, height // rows)
        def _(i):
            at = pl.ds(pl.multiple_of(i * rows, rows), rows)
            out_ref[at] = ref[at]

    pl.when(flag_ref[0] != 0)(lambda: copied_from(yes_ref))
    pl.when(flag_ref[0] == 0)(lambda: copied_from(no_ref))


def either_of(flag, yes, no):
    return pl.pallas_call(
        either_body,
        in_specs=[
            pl.BlockSpec(memory_space=pltpu.SMEM),
            pl.BlockSpec(memory_space=pltpu.VMEM),
            pl.BlockSpec(memory_space=pltpu.VMEM),
        ],
        out_specs=pl.BlockSpec(memory_space=pltpu.VMEM),
        out_shape=jax.ShapeDtypeStruct(yes.shape, yes.dtype),
        compiler_params=pltpu.CompilerParams(vmem_limit_bytes=VMEM_BYTES),
        name="either",
    )(flag.astype(jnp.int32).reshape(1), yes, no)


def held_body(block_ref, out_ref):
    out_ref[...] = block_ref[...]


def held_of(block):
    return pl.pallas_call(
        held_body,
        in_specs=[pl.BlockSpec(memory_space=pltpu.VMEM)],
        out_specs=pl.BlockSpec(memory_space=pltpu.VMEM),
        out_shape=jax.ShapeDtypeStruct(block.shape, block.dtype),
        cost_estimate=pl.CostEstimate(flops=5000000000, bytes_accessed=0, transcendentals=0),
        compiler_params=pltpu.CompilerParams(vmem_limit_bytes=VMEM_BYTES),
        name="held",
    )(block)


def pieces_of(chunk):
    pieces, place = [], 0
    for part, first, eighths in chunk:
        for at in range(first, first + eighths, 2):
            size = min(2, first + eighths - at)
            pieces.append((part, at, place, size))
            place += size
    return pieces


def photon_body(chunk, skips, factors_ref, dipole_ref, phonon_ref, own_ref, *rest):
    sides, (out_ref, results, sent) = rest[: len(skips)], rest[-3:]
    width = own_ref.shape[0]
    unit = width // EIGHTHS
    factors = [factors_ref[n] for n in range(2 + len(skips))]
    copies = []
    for k, (part, at, place, size) in enumerate(pieces_of(chunk)):
        at, place, cols = at * unit, place * unit, size * unit

        def piece(ref, skip=0):
            return ref[:, skip * unit + place : skip * unit + place + cols].astype(jnp.float32)

        side = factors[2] * piece(sides[0], skips[0])
        for factor, ref, skip in zip(factors[3:], sides[1:], skips[1:]):
            side += factor * piece(ref, skip)
        mixed = (factors[0] * piece(own_ref) + factors[1] * side).astype(jnp.bfloat16)
        photon = jnp.dot(dipole_ref[0], mixed, preferred_element_type=jnp.float32)
        if part == 1:
            row = lax.broadcasted_iota(jnp.int32, photon.shape, 0)
            col = lax.broadcasted_iota(jnp.int32, photon.shape, 1) + at
            photon += jnp.where(row == col, phonon_ref[:, at : at + cols], 0.0)
        results[k, :, :cols] = photon.astype(results.dtype)
        copies.append(
            pltpu.make_async_copy(
                results.at[k, :, pl.ds(0, cols)],
                out_ref.at[0, 0, part, :, pl.ds(at, cols)],
                sent.at[k],
            )
        )
        copies[-1].start()
    for copy in copies:
        copy.wait()


def photon_of(chunk, factors, dipole, phonon, own, sides, out):
    width = own.shape[0]
    sides, skips = zip(*sides)
    n_pieces = len(pieces_of(chunk))
    operands = [factors, dipole, phonon, own, *sides]
    in_specs = [pl.BlockSpec(memory_space=pltpu.SMEM)]
    in_specs += [pl.BlockSpec(memory_space=pltpu.VMEM)] * (len(operands) - 1)
    aliases = {}
    if out is not None:
        aliases = {len(operands): 0}
        operands.append(out)
        in_specs.append(pl.BlockSpec(memory_space=pl.ANY))
    return pl.pallas_call(
        functools.partial(photon_body, chunk, skips),
        in_specs=in_specs,
        out_specs=pl.BlockSpec(memory_space=pl.ANY),
        out_shape=jax.ShapeDtypeStruct((1, 1, 2, width, width), jnp.bfloat16),
        scratch_shapes=[
            pltpu.VMEM((n_pieces, width, 2 * width // EIGHTHS), jnp.bfloat16),
            pltpu.SemaphoreType.DMA((n_pieces,)),
        ],
        input_output_aliases=aliases,
        compiler_params=pltpu.CompilerParams(vmem_limit_bytes=VMEM_BYTES),
        name="photon",
    )(*operands)


def on_device(
    lesser,
    greater_diag,
    dipole,
    photon_weights,
    sidebands,
    phonon_lags,
    phonon_strengths,
    slab_coupling,
):
    e_count = lesser.shape[0]
    width = lesser.shape[-1]
    count = lax.axis_size("energy")
    own = lax.axis_index("energy")
    everyone = doubled(diagonals_of(lesser, greater_diag), "energy", 1)
    left = [left_of(lesser, dipole, CHUNKS[0], streamed=True)]
    left += [left_of(lesser, dipole, chunk) for chunk in CHUNKS[1:]]
    everyone, left[0] = lax.optimization_barrier((everyone, left[0]))
    weight_0, weight_low, weight_high = photon_weights[0]
    flag = sidebands[0].astype(jnp.float32)
    if count == 8:
        first, second = {}, {}
        hops = tuple((source, by) for source, by, _ in DETOURS)
        second_hops = tuple((by, target) for _, by, target in DETOURS)
        first[0] = lax.ppermute(left[0], "energy", STRAIGHT + hops)
        first[1] = lax.ppermute(left[1], "energy", STRAIGHT)

        is_low = own < count // 2
        for route in (TO_HUBS, BETWEEN_HUBS):
            other = lax.ppermute(everyone, "energy", route)
            everyone = jnp.concatenate(
                [jnp.where(is_low, everyone, other), jnp.where(is_low, other, everyone)], axis=0
            )
        held = jnp.where(any_of(own, [hub for hub, _ in BETWEEN_HUBS]), everyone, 0.0)
        for route in FROM_HUBS:
            held += lax.ppermute(everyone, "energy", route)
        everyone = held

        middle = left_of(lesser, dipole, MIDDLE)
        first[0], everyone, *left, middle = lax.optimization_barrier(
            (first[0], everyone, *left, middle)
        )
        relays = any_of(own, [by for by, _ in second_hops])
        onward = either_of(relays, first[0], left[0])
        second[0] = lax.ppermute(onward, "energy", EDGES + second_hops)
        crossed = lax.ppermute(middle, "energy", CROSS)
        first[2] = lax.ppermute(left[2], "energy", STRAIGHT)
        first[1] = held_of(first[1])
        first[1], left[3] = lax.optimization_barrier((first[1], left[3]))
        second[3] = lax.ppermute(left[3], "energy", CROSS)
        first[3] = lax.ppermute(left[3], "energy", STRAIGHT)
        weights = [
            side_weight(own, STRAIGHT, weight_low, weight_high),
            side_weight(own, CROSS, weight_low, weight_high),
        ]
    else:
        step = 2
        while step < count:
            everyone = doubled(everyone, "energy", step)
            step *= 2
        first = [shifted(block, "energy", PHOT_BLOCKS) for block in left]
        second = [shifted(block, "energy", -PHOT_BLOCKS) for block in left]
        weights = [weight_low, weight_high]
    factors = jnp.stack([weight_0, flag, *weights])
    if count == 8:
        sides = [
            [(first[0], 0), (second[0], 0)],
            [(first[1], 0), (crossed, 0)],
            [(first[2], 0), (crossed, 1)],
            [(first[3], 0), (second[3], 0)],
        ]
    else:
        sides = [[(low, 0), (high, 0)] for low, high in zip(first, second)]

    own_rows = own * e_count + jnp.arange(e_count, dtype=jnp.int32)
    all_rows = jnp.arange(e_count * count, dtype=jnp.int32)
    k_less = lag_kernel(own_rows, all_rows, phonon_lags, phonon_strengths[0], phonon_strengths[1])
    k_great = lag_kernel(own_rows, all_rows, phonon_lags, phonon_strengths[1], phonon_strengths[0])
    corr_less = jnp.sum(k_less[0][:, None] * everyone[:, 0], axis=0)
    corr_great = jnp.sum(k_great[0][:, None] * everyone[:, 1], axis=0)
    correlated = jnp.stack([corr_less, corr_great])
    below = shifted(slab_coupling * correlated, "slab", 1)
    above = shifted(correlated, "slab", -1)
    phon_less, phon_great = correlated + below + slab_coupling * above

    out = None
    for n, chunk in enumerate(CHUNKS):
        out = photon_of(chunk, factors, dipole, phon_less[None], left[n], sides[n], out)
    return out, phon_great[None, None]


def solution(mesh):
    return jax.shard_map(
        on_device,
        mesh=mesh,
        in_specs=(
            P("energy", "slab", None, None, None),
            P("energy", "slab", None),
            P("slab", None, None),
            P("energy", None),
            P("energy"),
            P(),
            P(),
            P("slab", None),
        ),
        out_specs=(P("energy", "slab", None, None, None), P("energy", "slab", None)),
        check_vma=False,
    )
```

```python
import functools

import jax
import jax.numpy as jnp
from jax import lax
from jax.experimental import pallas as pl
from jax.experimental.pallas import tpu as pltpu
from jax.sharding import PartitionSpec as P

PHOT_BLOCKS = 3
CHUNKS = (((0, 0, 7),), ((1, 0, 2),), ((1, 2, 5),), ((1, 7, 1), (0, 7, 1)))
MIDDLE = ((1, 0, 7),)
EIGHTHS = 8
VMEM_BYTES = 20 * 1024 * 1024
EARLY_VMEM_BYTES = 53 * 1024 * 1024
FIRST_VMEM_BYTES = 48 * 1024 * 1024

STRAIGHT = ((0, 3), (2, 5), (3, 6), (4, 1), (5, 2), (7, 4))
CROSS = ((1, 4), (3, 0), (4, 7), (6, 3))
DETOURS = ((1, 0, 4), (6, 7, 3))
EDGES = ((3, 0), (4, 7))

TO_HUBS = ((3, 1), (4, 6))
BETWEEN_HUBS = ((1, 6), (6, 1))
FROM_HUBS = (((1, 3), (6, 4)), ((1, 5), (6, 2)), ((1, 7), (6, 0)))


def shifted(block, axis, distance):
    devices = range(lax.axis_size(axis))
    return lax.ppermute(
        block, axis, [(i - distance, i) for i in devices if i - distance in devices]
    )


def any_of(own, energies):
    return functools.reduce(jnp.logical_or, [own == energy for energy in energies])


def side_weight(own, route, low, high):
    from_low = any_of(own, [target for source, target in route if source < target])
    from_high = any_of(own, [target for source, target in route if source > target])
    return jnp.where(from_low, low, jnp.where(from_high, high, 0.0))


def doubled(block, axis, step):
    other = lax.ppermute(block, axis, [(i, i ^ step) for i in range(lax.axis_size(axis))])
    upper = (lax.axis_index(axis) & step) != 0
    return jnp.concatenate(
        [jnp.where(upper, other, block), jnp.where(upper, block, other)], axis=0
    )


def diagonals_body(tile, lesser_ref, greater_ref, out_ref, tiles, arrived):
    count = tiles.shape[0]
    copies = [
        pltpu.make_async_copy(
            lesser_ref.at[0, 0, 1, pl.ds(n * tile, tile), pl.ds(n * tile, tile)],
            tiles.at[n],
            arrived.at[n],
        )
        for n in range(count)
    ]
    for copy in copies:
        copy.start()
    row = lax.broadcasted_iota(jnp.int32, (tile, tile), 0)
    col = lax.broadcasted_iota(jnp.int32, (tile, tile), 1)
    out_ref[0, 1:2] = greater_ref[0]
    for n, copy in enumerate(copies):
        copy.wait()
        block = jnp.where(row == col, tiles[n].astype(jnp.float32), 0.0)
        out_ref[0, 0:1, n * tile : (n + 1) * tile] = jnp.sum(block, axis=0, keepdims=True)


def diagonals_of(lesser, greater_diag):
    width = lesser.shape[-1]
    tile = 128
    return pl.pallas_call(
        functools.partial(diagonals_body, tile),
        in_specs=[
            pl.BlockSpec(memory_space=pltpu.HBM),
            pl.BlockSpec(memory_space=pltpu.VMEM),
        ],
        out_specs=pl.BlockSpec(memory_space=pltpu.VMEM),
        out_shape=jax.ShapeDtypeStruct((1, 2, width), jnp.float32),
        scratch_shapes=[
            pltpu.VMEM((width // tile, tile, tile), lesser.dtype),
            pltpu.SemaphoreType.DMA((width // tile,)),
        ],
        compiler_params=pltpu.CompilerParams(vmem_limit_bytes=EARLY_VMEM_BYTES),
        name="diagonals",
    )(lesser, greater_diag)


def lag_kernel(rows, cols, phonon_lags, first, second):
    offset = cols[None, :] - rows[:, None]
    upward = (offset[None, :, :] == phonon_lags[:, None, None]).astype(jnp.float32)
    downward = (offset[None, :, :] == -phonon_lags[:, None, None]).astype(jnp.float32)
    return jnp.sum(first[:, None, None] * upward + second[:, None, None] * downward, axis=0)


def lag_sums(rows, everyone, phonon_lags, strengths):
    cols = jnp.arange(everyone.shape[0], dtype=jnp.int32)
    k_less = lag_kernel(rows, cols, phonon_lags, strengths[0], strengths[1])
    k_great = lag_kernel(rows, cols, phonon_lags, strengths[1], strengths[0])
    kernels = jnp.stack([k_less, k_great], axis=-1)
    return jnp.sum(kernels[..., None] * everyone[None], axis=1)


def left_body(chunk, streamed, lesser_ref, dipole_ref, left_ref, *scratch):
    width = left_ref.shape[0]
    unit, rows = width // EIGHTHS, width // 4
    starts = range(0, width, rows)
    if streamed:
        blocks, arrived = scratch
        copies = [
            pltpu.make_async_copy(
                lesser_ref.at[0, 0, chunk[0][0], pl.ds(i, rows)], blocks.at[pl.ds(i, rows)], sem
            )
            for i, sem in zip(starts, [arrived.at[n] for n in range(len(starts))])
        ]
        for copy in copies:
            copy.start()
    at = 0
    for part, first, eighths in chunk:
        cols = eighths * unit
        for n, i in enumerate(starts):
            if streamed:
                copies[n].wait()
                block = blocks[i : i + rows]
            else:
                block = lesser_ref[0, 0, part, i : i + rows]
            left_ref[i : i + rows, at : at + cols] = lax.dot_general(
                block,
                dipole_ref[0, first * unit : first * unit + cols],
                (((1,), (1,)), ((), ())),
                preferred_element_type=jnp.float32,
            ).astype(left_ref.dtype)
        at += cols


def left_of(lesser, dipole, chunk, streamed=False):
    width = lesser.shape[-1]
    cols = width // EIGHTHS * sum(eighths for _, _, eighths in chunk)
    scratch = [pltpu.VMEM((width, width), lesser.dtype), pltpu.SemaphoreType.DMA((4,))]
    return pl.pallas_call(
        functools.partial(left_body, chunk, streamed),
        in_specs=[
            pl.BlockSpec(memory_space=pl.ANY if streamed else pltpu.VMEM),
            pl.BlockSpec(memory_space=pltpu.VMEM),
        ],
        out_specs=pl.BlockSpec(memory_space=pltpu.VMEM),
        out_shape=jax.ShapeDtypeStruct((width, cols), lesser.dtype),
        scratch_shapes=scratch if streamed else [],
        compiler_params=pltpu.CompilerParams(
            vmem_limit_bytes=FIRST_VMEM_BYTES if streamed else VMEM_BYTES
        ),
        name="left",
    )(lesser, dipole)


def either_body(flag_ref, yes_ref, no_ref, out_ref):
    height = out_ref.shape[0]
    rows = height // 16

    def copied_from(ref):
        @pl.loop(0, height // rows)
        def _(i):
            at = pl.ds(pl.multiple_of(i * rows, rows), rows)
            out_ref[at] = ref[at]

    pl.when(flag_ref[0] != 0)(lambda: copied_from(yes_ref))
    pl.when(flag_ref[0] == 0)(lambda: copied_from(no_ref))


def either_of(flag, yes, no):
    return pl.pallas_call(
        either_body,
        in_specs=[
            pl.BlockSpec(memory_space=pltpu.SMEM),
            pl.BlockSpec(memory_space=pltpu.VMEM),
            pl.BlockSpec(memory_space=pltpu.VMEM),
        ],
        out_specs=pl.BlockSpec(memory_space=pltpu.VMEM),
        out_shape=jax.ShapeDtypeStruct(yes.shape, yes.dtype),
        compiler_params=pltpu.CompilerParams(vmem_limit_bytes=VMEM_BYTES),
        name="either",
    )(flag.astype(jnp.int32).reshape(1), yes, no)


def held_body(block_ref, out_ref):
    out_ref[...] = block_ref[...]


def held_of(block, flops):
    return pl.pallas_call(
        held_body,
        in_specs=[pl.BlockSpec(memory_space=pltpu.VMEM)],
        out_specs=pl.BlockSpec(memory_space=pltpu.VMEM),
        out_shape=jax.ShapeDtypeStruct(block.shape, block.dtype),
        cost_estimate=pl.CostEstimate(flops=flops, bytes_accessed=0, transcendentals=0),
        compiler_params=pltpu.CompilerParams(vmem_limit_bytes=VMEM_BYTES),
        name="held",
    )(block)


def pieces_of(chunk):
    pieces, place = [], 0
    for part, first, eighths in chunk:
        for at in range(first, first + eighths, 2):
            size = min(2, first + eighths - at)
            pieces.append((part, at, place, size))
            place += size
    return pieces


def photon_body(chunk, skips, factors_ref, dipole_ref, phonon_ref, own_ref, *rest):
    sides, (out_ref, results, sent) = rest[: len(skips)], rest[-3:]
    width = own_ref.shape[0]
    unit = width // EIGHTHS
    factors = [factors_ref[n] for n in range(2 + len(skips))]
    copies = []
    for k, (part, at, place, size) in enumerate(pieces_of(chunk)):
        at, place, cols = at * unit, place * unit, size * unit

        def piece(ref, skip=0):
            return ref[:, skip * unit + place : skip * unit + place + cols].astype(jnp.float32)

        side = factors[2] * piece(sides[0], skips[0])
        for factor, ref, skip in zip(factors[3:], sides[1:], skips[1:]):
            side += factor * piece(ref, skip)
        mixed = (factors[0] * piece(own_ref) + factors[1] * side).astype(jnp.bfloat16)
        photon = jnp.dot(dipole_ref[0], mixed, preferred_element_type=jnp.float32)
        if part == 1:
            row = lax.broadcasted_iota(jnp.int32, photon.shape, 0)
            col = lax.broadcasted_iota(jnp.int32, photon.shape, 1) + at
            photon += jnp.where(row == col, phonon_ref[:, at : at + cols], 0.0)
        results[k, :, :cols] = photon.astype(results.dtype)
        copies.append(
            pltpu.make_async_copy(
                results.at[k, :, pl.ds(0, cols)],
                out_ref.at[0, 0, part, :, pl.ds(at, cols)],
                sent.at[k],
            )
        )
        copies[-1].start()
    for copy in copies:
        copy.wait()


def photon_of(chunk, factors, dipole, phonon, own, sides, out):
    width = own.shape[0]
    sides, skips = zip(*sides)
    n_pieces = len(pieces_of(chunk))
    operands = [factors, dipole, phonon, own, *sides]
    in_specs = [pl.BlockSpec(memory_space=pltpu.SMEM)]
    in_specs += [pl.BlockSpec(memory_space=pltpu.VMEM)] * (len(operands) - 1)
    aliases = {}
    if out is not None:
        aliases = {len(operands): 0}
        operands.append(out)
        in_specs.append(pl.BlockSpec(memory_space=pl.ANY))
    return pl.pallas_call(
        functools.partial(photon_body, chunk, skips),
        in_specs=in_specs,
        out_specs=pl.BlockSpec(memory_space=pl.ANY),
        out_shape=jax.ShapeDtypeStruct((1, 1, 2, width, width), jnp.bfloat16),
        scratch_shapes=[
            pltpu.VMEM((n_pieces, width, 2 * width // EIGHTHS), jnp.bfloat16),
            pltpu.SemaphoreType.DMA((n_pieces,)),
        ],
        input_output_aliases=aliases,
        compiler_params=pltpu.CompilerParams(vmem_limit_bytes=VMEM_BYTES),
        name="photon",
    )(*operands)


def on_device(
    lesser,
    greater_diag,
    dipole,
    photon_weights,
    sidebands,
    phonon_lags,
    phonon_strengths,
    slab_coupling,
):
    e_count = lesser.shape[0]
    width = lesser.shape[-1]
    count = lax.axis_size("energy")
    own = lax.axis_index("energy")
    everyone = doubled(diagonals_of(lesser, greater_diag), "energy", 1)
    left = [left_of(lesser, dipole, CHUNKS[0], streamed=True)]
    left += [left_of(lesser, dipole, chunk) for chunk in CHUNKS[1:]]
    everyone, left[0] = lax.optimization_barrier((everyone, left[0]))
    weight_0, weight_low, weight_high = photon_weights[0]
    flag = sidebands[0].astype(jnp.float32)
    if count == 8:
        first, second = {}, {}
        hops = tuple((source, by) for source, by, _ in DETOURS)
        second_hops = tuple((by, target) for _, by, target in DETOURS)
        first[0] = lax.ppermute(left[0], "energy", STRAIGHT + hops)
        first[1] = lax.ppermute(left[1], "energy", STRAIGHT)

        is_low = own < count // 2
        for route in (TO_HUBS, BETWEEN_HUBS):
            other = lax.ppermute(everyone, "energy", route)
            everyone = jnp.concatenate(
                [jnp.where(is_low, everyone, other), jnp.where(is_low, other, everyone)], axis=0
            )
        hubs = [hub for hub, _ in BETWEEN_HUBS]
        to = [[own] + [dict(route)[hub] for route in FROM_HUBS] for hub in hubs]
        rows = [jnp.where(is_low, low, high) for low, high in zip(*to)]
        sums = lag_sums(jnp.stack(rows), everyone, phonon_lags, phonon_strengths)
        correlated = jnp.where(any_of(own, hubs), sums[0], 0.0)
        for n, route in enumerate(FROM_HUBS):
            correlated += lax.ppermute(sums[n + 1], "energy", route)

        middle = left_of(lesser, dipole, MIDDLE)
        first[0], correlated, *left, middle = lax.optimization_barrier(
            (first[0], correlated, *left, middle)
        )
        relays = any_of(own, [by for by, _ in second_hops])
        onward = either_of(relays, first[0], left[0])
        second[0] = lax.ppermute(onward, "energy", EDGES + second_hops)
        crossed = lax.ppermute(middle, "energy", CROSS)
        first[2] = lax.ppermute(left[2], "energy", STRAIGHT)
        first[1] = held_of(first[1], 4000000000)
        first[1], left[3] = lax.optimization_barrier((first[1], left[3]))
        second[3] = lax.ppermute(left[3], "energy", CROSS)
        first[3] = lax.ppermute(left[3], "energy", STRAIGHT)
        weights = [
            side_weight(own, STRAIGHT, weight_low, weight_high),
            side_weight(own, CROSS, weight_low, weight_high),
        ]
    else:
        step = 2
        while step < count:
            everyone = doubled(everyone, "energy", step)
            step *= 2
        correlated = lag_sums(own[None], everyone, phonon_lags, phonon_strengths)[0]
        first = [shifted(block, "energy", PHOT_BLOCKS) for block in left]
        second = [shifted(block, "energy", -PHOT_BLOCKS) for block in left]
        weights = [weight_low, weight_high]
    factors = jnp.stack([weight_0, flag, *weights])
    if count == 8:
        sides = [
            [(first[0], 0), (second[0], 0)],
            [(first[1], 0), (crossed, 0)],
            [(first[2], 0), (crossed, 2)],
            [(first[3], 0), (second[3], 0)],
        ]
    else:
        sides = [[(low, 0), (high, 0)] for low, high in zip(first, second)]

    correlated = held_of(correlated, 7000000000)
    below = shifted(slab_coupling * correlated, "slab", 1)
    above = shifted(correlated, "slab", -1)
    phon_less, phon_great = correlated + below + slab_coupling * above

    out = None
    for n, chunk in enumerate(CHUNKS):
        out = photon_of(chunk, factors, dipole, phon_less[None], left[n], sides[n], out)
    return out, phon_great[None, None]


def solution(mesh):
    return jax.shard_map(
        on_device,
        mesh=mesh,
        in_specs=(
            P("energy", "slab", None, None, None),
            P("energy", "slab", None),
            P("slab", None, None),
            P("energy", None),
            P("energy"),
            P(),
            P(),
            P("slab", None),
        ),
        out_specs=(P("energy", "slab", None, None, None), P("energy", "slab", None)),
        check_vma=False,
    )
```

```python
import functools

import jax
import jax.numpy as jnp
from jax import lax
from jax.experimental import pallas as pl
from jax.experimental.pallas import tpu as pltpu
from jax.sharding import PartitionSpec as P

PHOT_BLOCKS = 3
CHUNKS = (((0, 0, 7),), ((1, 0, 2),), ((1, 2, 5),), ((1, 7, 1), (0, 7, 1)))
MIDDLE = ((1, 0, 7),)
EIGHTHS = 8
VMEM_BYTES = 14 * 1024 * 1024
SMALL_VMEM_BYTES = 8 * 1024 * 1024
EARLY_VMEM_BYTES = 53 * 1024 * 1024
FIRST_VMEM_BYTES = 48 * 1024 * 1024

STRAIGHT = ((0, 3), (2, 5), (3, 6), (4, 1), (5, 2), (7, 4))
CROSS = ((1, 4), (3, 0), (4, 7), (6, 3))
DETOURS = ((1, 0, 4), (6, 7, 3))
EDGES = ((3, 0), (4, 7))

TO_HUBS = ((3, 1), (4, 6))
BETWEEN_HUBS = ((1, 6), (6, 1))
FROM_HUBS = (((1, 3), (6, 4)), ((1, 5), (6, 2)), ((1, 7), (6, 0)))


def shifted(block, axis, distance):
    devices = range(lax.axis_size(axis))
    return lax.ppermute(
        block, axis, [(i - distance, i) for i in devices if i - distance in devices]
    )


def any_of(own, energies):
    return functools.reduce(jnp.logical_or, [own == energy for energy in energies])


def side_weight(own, route, low, high):
    from_low = any_of(own, [target for source, target in route if source < target])
    from_high = any_of(own, [target for source, target in route if source > target])
    return jnp.where(from_low, low, jnp.where(from_high, high, 0.0))


def doubled(block, axis, step):
    other = lax.ppermute(block, axis, [(i, i ^ step) for i in range(lax.axis_size(axis))])
    upper = (lax.axis_index(axis) & step) != 0
    return jnp.concatenate(
        [jnp.where(upper, other, block), jnp.where(upper, block, other)], axis=0
    )


def diagonals_body(tile, lesser_ref, greater_ref, out_ref, tiles, arrived):
    count = tiles.shape[0]
    copies = [
        pltpu.make_async_copy(
            lesser_ref.at[0, 0, 1, pl.ds(n * tile, tile), pl.ds(n * tile, tile)],
            tiles.at[n],
            arrived.at[n],
        )
        for n in range(count)
    ]
    for copy in copies:
        copy.start()
    row = lax.broadcasted_iota(jnp.int32, (tile, tile), 0)
    col = lax.broadcasted_iota(jnp.int32, (tile, tile), 1)
    out_ref[0, 1:2] = greater_ref[0]
    for n, copy in enumerate(copies):
        copy.wait()
        block = jnp.where(row == col, tiles[n].astype(jnp.float32), 0.0)
        out_ref[0, 0:1, n * tile : (n + 1) * tile] = jnp.sum(block, axis=0, keepdims=True)


def diagonals_of(lesser, greater_diag):
    width = lesser.shape[-1]
    tile = 128
    return pl.pallas_call(
        functools.partial(diagonals_body, tile),
        in_specs=[
            pl.BlockSpec(memory_space=pltpu.HBM),
            pl.BlockSpec(memory_space=pltpu.VMEM),
        ],
        out_specs=pl.BlockSpec(memory_space=pltpu.VMEM),
        out_shape=jax.ShapeDtypeStruct((1, 2, width), jnp.float32),
        scratch_shapes=[
            pltpu.VMEM((width // tile, tile, tile), lesser.dtype),
            pltpu.SemaphoreType.DMA((width // tile,)),
        ],
        compiler_params=pltpu.CompilerParams(vmem_limit_bytes=EARLY_VMEM_BYTES),
        name="diagonals",
    )(lesser, greater_diag)


def lag_kernel(rows, cols, phonon_lags, first, second):
    offset = cols[None, :] - rows[:, None]
    upward = (offset[None, :, :] == phonon_lags[:, None, None]).astype(jnp.float32)
    downward = (offset[None, :, :] == -phonon_lags[:, None, None]).astype(jnp.float32)
    return jnp.sum(first[:, None, None] * upward + second[:, None, None] * downward, axis=0)


def lag_sums(rows, everyone, phonon_lags, strengths):
    cols = jnp.arange(everyone.shape[0], dtype=jnp.int32)
    k_less = lag_kernel(rows, cols, phonon_lags, strengths[0], strengths[1])
    k_great = lag_kernel(rows, cols, phonon_lags, strengths[1], strengths[0])
    kernels = jnp.stack([k_less, k_great], axis=-1)
    return jnp.sum(kernels[..., None] * everyone[None], axis=1)


def left_body(chunk, streamed, lesser_ref, dipole_ref, left_ref, *scratch):
    width = left_ref.shape[0]
    unit, rows = width // EIGHTHS, width // 4
    starts = range(0, width, rows)
    if streamed:
        blocks, arrived = scratch
        copies = [
            pltpu.make_async_copy(
                lesser_ref.at[0, 0, chunk[0][0], pl.ds(i, rows)], blocks.at[pl.ds(i, rows)], sem
            )
            for i, sem in zip(starts, [arrived.at[n] for n in range(len(starts))])
        ]
        for copy in copies:
            copy.start()
    at = 0
    for part, first, eighths in chunk:
        cols = eighths * unit
        for n, i in enumerate(starts):
            if streamed:
                copies[n].wait()
                block = blocks[i : i + rows]
            else:
                block = lesser_ref[0, 0, part, i : i + rows]
            left_ref[i : i + rows, at : at + cols] = lax.dot_general(
                block,
                dipole_ref[0, first * unit : first * unit + cols],
                (((1,), (1,)), ((), ())),
                preferred_element_type=jnp.float32,
            ).astype(left_ref.dtype)
        at += cols


def left_of(lesser, dipole, chunk, streamed=False):
    width = lesser.shape[-1]
    cols = width // EIGHTHS * sum(eighths for _, _, eighths in chunk)
    scratch = [pltpu.VMEM((width, width), lesser.dtype), pltpu.SemaphoreType.DMA((4,))]
    return pl.pallas_call(
        functools.partial(left_body, chunk, streamed),
        in_specs=[
            pl.BlockSpec(memory_space=pl.ANY if streamed else pltpu.VMEM),
            pl.BlockSpec(memory_space=pltpu.VMEM),
        ],
        out_specs=pl.BlockSpec(memory_space=pltpu.VMEM),
        out_shape=jax.ShapeDtypeStruct((width, cols), lesser.dtype),
        scratch_shapes=scratch if streamed else [],
        compiler_params=pltpu.CompilerParams(
            vmem_limit_bytes=FIRST_VMEM_BYTES if streamed else SMALL_VMEM_BYTES
        ),
        name="left",
    )(lesser, dipole)


def either_body(flag_ref, yes_ref, no_ref, out_ref):
    height = out_ref.shape[0]
    rows = height // 16

    def copied_from(ref):
        @pl.loop(0, height // rows)
        def _(i):
            at = pl.ds(pl.multiple_of(i * rows, rows), rows)
            out_ref[at] = ref[at]

    pl.when(flag_ref[0] != 0)(lambda: copied_from(yes_ref))
    pl.when(flag_ref[0] == 0)(lambda: copied_from(no_ref))


def either_of(flag, yes, no):
    return pl.pallas_call(
        either_body,
        in_specs=[
            pl.BlockSpec(memory_space=pltpu.SMEM),
            pl.BlockSpec(memory_space=pltpu.VMEM),
            pl.BlockSpec(memory_space=pltpu.VMEM),
        ],
        out_specs=pl.BlockSpec(memory_space=pltpu.VMEM),
        out_shape=jax.ShapeDtypeStruct(yes.shape, yes.dtype),
        compiler_params=pltpu.CompilerParams(vmem_limit_bytes=SMALL_VMEM_BYTES),
        name="either",
    )(flag.astype(jnp.int32).reshape(1), yes, no)


def held_body(block_ref, out_ref):
    out_ref[...] = block_ref[...]


def held_of(block, flops):
    return pl.pallas_call(
        held_body,
        in_specs=[pl.BlockSpec(memory_space=pltpu.VMEM)],
        out_specs=pl.BlockSpec(memory_space=pltpu.VMEM),
        out_shape=jax.ShapeDtypeStruct(block.shape, block.dtype),
        cost_estimate=pl.CostEstimate(flops=flops, bytes_accessed=0, transcendentals=0),
        compiler_params=pltpu.CompilerParams(vmem_limit_bytes=SMALL_VMEM_BYTES),
        name="held",
    )(block)


def pieces_of(chunk):
    pieces, place = [], 0
    for part, first, eighths in chunk:
        for at in range(first, first + eighths, 2):
            size = min(2, first + eighths - at)
            pieces.append((part, at, place, size))
            place += size
    return pieces


def photon_body(chunk, skips, factors_ref, dipole_ref, phonon_ref, own_ref, *rest):
    sides, (out_ref, results, sent) = rest[: len(skips)], rest[-3:]
    width = own_ref.shape[0]
    unit = width // EIGHTHS
    factors = [factors_ref[n] for n in range(2 + len(skips))]
    copies = []
    for k, (part, at, place, size) in enumerate(pieces_of(chunk)):
        at, place, cols = at * unit, place * unit, size * unit

        def piece(ref, skip=0):
            return ref[:, skip * unit + place : skip * unit + place + cols].astype(jnp.float32)

        side = factors[2] * piece(sides[0], skips[0])
        for factor, ref, skip in zip(factors[3:], sides[1:], skips[1:]):
            side += factor * piece(ref, skip)
        mixed = (factors[0] * piece(own_ref) + factors[1] * side).astype(jnp.bfloat16)
        photon = jnp.dot(dipole_ref[0], mixed, preferred_element_type=jnp.float32)
        if part == 1:
            row = lax.broadcasted_iota(jnp.int32, photon.shape, 0)
            col = lax.broadcasted_iota(jnp.int32, photon.shape, 1) + at
            photon += jnp.where(row == col, phonon_ref[:, at : at + cols], 0.0)
        results[k, :, :cols] = photon.astype(results.dtype)
        copies.append(
            pltpu.make_async_copy(
                results.at[k, :, pl.ds(0, cols)],
                out_ref.at[0, 0, part, :, pl.ds(at, cols)],
                sent.at[k],
            )
        )
        copies[-1].start()
    for copy in copies:
        copy.wait()


def photon_of(chunk, factors, dipole, phonon, own, sides, out):
    width = own.shape[0]
    sides, skips = zip(*sides)
    n_pieces = len(pieces_of(chunk))
    operands = [factors, dipole, phonon, own, *sides]
    in_specs = [pl.BlockSpec(memory_space=pltpu.SMEM)]
    in_specs += [pl.BlockSpec(memory_space=pltpu.VMEM)] * (len(operands) - 1)
    aliases = {}
    if out is not None:
        aliases = {len(operands): 0}
        operands.append(out)
        in_specs.append(pl.BlockSpec(memory_space=pl.ANY))
    return pl.pallas_call(
        functools.partial(photon_body, chunk, skips),
        in_specs=in_specs,
        out_specs=pl.BlockSpec(memory_space=pl.ANY),
        out_shape=jax.ShapeDtypeStruct((1, 1, 2, width, width), jnp.bfloat16),
        scratch_shapes=[
            pltpu.VMEM((n_pieces, width, 2 * width // EIGHTHS), jnp.bfloat16),
            pltpu.SemaphoreType.DMA((n_pieces,)),
        ],
        input_output_aliases=aliases,
        compiler_params=pltpu.CompilerParams(vmem_limit_bytes=VMEM_BYTES),
        name="photon",
    )(*operands)


def on_device(
    lesser,
    greater_diag,
    dipole,
    photon_weights,
    sidebands,
    phonon_lags,
    phonon_strengths,
    slab_coupling,
):
    width = lesser.shape[-1]
    count = lax.axis_size("energy")
    own = lax.axis_index("energy")
    everyone = doubled(diagonals_of(lesser, greater_diag), "energy", 1)
    left = [left_of(lesser, dipole, CHUNKS[0], streamed=True)]
    left += [left_of(lesser, dipole, chunk) for chunk in CHUNKS[1:]]
    everyone, left[0] = lax.optimization_barrier((everyone, left[0]))
    weight_0, weight_low, weight_high = photon_weights[0]
    flag = sidebands[0].astype(jnp.float32)
    if count == 8:
        first, second = {}, {}
        hops = tuple((source, by) for source, by, _ in DETOURS)
        second_hops = tuple((by, target) for _, by, target in DETOURS)
        first[0] = lax.ppermute(left[0], "energy", STRAIGHT + hops)
        first[1] = lax.ppermute(left[1], "energy", STRAIGHT)

        is_low = own < count // 2
        for route in (TO_HUBS, BETWEEN_HUBS):
            other = lax.ppermute(everyone, "energy", route)
            everyone = jnp.concatenate(
                [jnp.where(is_low, everyone, other), jnp.where(is_low, other, everyone)], axis=0
            )
        hubs = [hub for hub, _ in BETWEEN_HUBS]
        to = [[own] + [dict(route)[hub] for route in FROM_HUBS] for hub in hubs]
        rows = [jnp.where(is_low, low, high) for low, high in zip(*to)]
        sums = lag_sums(jnp.stack(rows), everyone, phonon_lags, phonon_strengths)
        correlated = jnp.where(any_of(own, hubs), sums[0], 0.0)
        for n, route in enumerate(FROM_HUBS):
            correlated += lax.ppermute(sums[n + 1], "energy", route)

        middle = left_of(lesser, dipole, MIDDLE)
        first[0], correlated, *left, middle = lax.optimization_barrier(
            (first[0], correlated, *left, middle)
        )
        relays = any_of(own, [by for by, _ in second_hops])
        onward = either_of(relays, first[0], left[0])
        second[0] = lax.ppermute(onward, "energy", EDGES + second_hops)
        crossed = lax.ppermute(middle, "energy", CROSS)
        first[2] = lax.ppermute(left[2], "energy", STRAIGHT)
        first[1] = held_of(first[1], 4000000000)
        first[1], left[3] = lax.optimization_barrier((first[1], left[3]))
        second[3] = lax.ppermute(left[3], "energy", CROSS)
        first[3] = lax.ppermute(left[3], "energy", STRAIGHT)
        weights = [
            side_weight(own, STRAIGHT, weight_low, weight_high),
            side_weight(own, CROSS, weight_low, weight_high),
        ]
    else:
        step = 2
        while step < count:
            everyone = doubled(everyone, "energy", step)
            step *= 2
        correlated = lag_sums(own[None], everyone, phonon_lags, phonon_strengths)[0]
        first = [shifted(block, "energy", PHOT_BLOCKS) for block in left]
        second = [shifted(block, "energy", -PHOT_BLOCKS) for block in left]
        weights = [weight_low, weight_high]
    factors = jnp.stack([weight_0, flag, *weights])
    if count == 8:
        sides = [
            [(first[0], 0), (second[0], 0)],
            [(first[1], 0), (crossed, 0)],
            [(first[2], 0), (crossed, 2)],
            [(first[3], 0), (second[3], 0)],
        ]
    else:
        sides = [[(low, 0), (high, 0)] for low, high in zip(first, second)]

    correlated = held_of(correlated, 7000000000)
    below = shifted(slab_coupling * correlated, "slab", 1)
    above = shifted(correlated, "slab", -1)
    phon_less, phon_great = correlated + below + slab_coupling * above

    out = None
    for n, chunk in enumerate(CHUNKS):
        out = photon_of(chunk, factors, dipole, phon_less[None], left[n], sides[n], out)
    return out, phon_great[None, None]


def solution(mesh):
    return jax.shard_map(
        on_device,
        mesh=mesh,
        in_specs=(
            P("energy", "slab", None, None, None),
            P("energy", "slab", None),
            P("slab", None, None),
            P("energy", None),
            P("energy"),
            P(),
            P(),
            P("slab", None),
        ),
        out_specs=(P("energy", "slab", None, None, None), P("energy", "slab", None)),
        check_vma=False,
    )
```

```python
import functools

import jax
import jax.numpy as jnp
from jax import lax
from jax.experimental import pallas as pl
from jax.experimental.pallas import tpu as pltpu
from jax.sharding import PartitionSpec as P

PHOT_BLOCKS = 3
CHUNKS = (((0, 0, 7),), ((1, 0, 2),), ((1, 2, 5),), ((1, 7, 1), (0, 7, 1)))
MIDDLE = ((1, 0, 7),)
EIGHTHS = 8
VMEM_BYTES = 14 * 1024 * 1024
SMALL_VMEM_BYTES = 8 * 1024 * 1024
EARLY_VMEM_BYTES = 53 * 1024 * 1024
FIRST_VMEM_BYTES = 48 * 1024 * 1024

STRAIGHT = ((0, 3), (2, 5), (3, 6), (4, 1), (5, 2), (7, 4))
CROSS = ((1, 4), (3, 0), (4, 7), (6, 3))
DETOURS = ((1, 0, 4), (6, 7, 3))
EDGES = ((3, 0), (4, 7))

TO_HUBS = ((3, 1), (4, 6))
BETWEEN_HUBS = ((1, 6), (6, 1))
FROM_HUBS = (((1, 3), (6, 4)), ((1, 5), (6, 2)), ((1, 7), (6, 0)))


def shifted(block, axis, distance):
    devices = range(lax.axis_size(axis))
    return lax.ppermute(
        block, axis, [(i - distance, i) for i in devices if i - distance in devices]
    )


def any_of(own, energies):
    return functools.reduce(jnp.logical_or, [own == energy for energy in energies])


def side_weight(own, route, low, high):
    from_low = any_of(own, [target for source, target in route if source < target])
    from_high = any_of(own, [target for source, target in route if source > target])
    return jnp.where(from_low, low, jnp.where(from_high, high, 0.0))


def doubled(block, axis, step):
    other = lax.ppermute(block, axis, [(i, i ^ step) for i in range(lax.axis_size(axis))])
    upper = (lax.axis_index(axis) & step) != 0
    return jnp.concatenate(
        [jnp.where(upper, other, block), jnp.where(upper, block, other)], axis=0
    )


def diagonals_body(tile, lesser_ref, greater_ref, out_ref, tiles, arrived):
    count = tiles.shape[0]
    copies = [
        pltpu.make_async_copy(
            lesser_ref.at[0, 0, 1, pl.ds(n * tile, tile), pl.ds(n * tile, tile)],
            tiles.at[n],
            arrived.at[n],
        )
        for n in range(count)
    ]
    for copy in copies:
        copy.start()
    row = lax.broadcasted_iota(jnp.int32, (tile, tile), 0)
    col = lax.broadcasted_iota(jnp.int32, (tile, tile), 1)
    out_ref[0, 1:2] = greater_ref[0]
    for n, copy in enumerate(copies):
        copy.wait()
        block = jnp.where(row == col, tiles[n].astype(jnp.float32), 0.0)
        out_ref[0, 0:1, n * tile : (n + 1) * tile] = jnp.sum(block, axis=0, keepdims=True)


def diagonals_of(lesser, greater_diag):
    width = lesser.shape[-1]
    tile = 128
    return pl.pallas_call(
        functools.partial(diagonals_body, tile),
        in_specs=[
            pl.BlockSpec(memory_space=pltpu.HBM),
            pl.BlockSpec(memory_space=pltpu.VMEM),
        ],
        out_specs=pl.BlockSpec(memory_space=pltpu.VMEM),
        out_shape=jax.ShapeDtypeStruct((1, 2, width), jnp.float32),
        scratch_shapes=[
            pltpu.VMEM((width // tile, tile, tile), lesser.dtype),
            pltpu.SemaphoreType.DMA((width // tile,)),
        ],
        compiler_params=pltpu.CompilerParams(vmem_limit_bytes=EARLY_VMEM_BYTES),
        name="diagonals",
    )(lesser, greater_diag)


def lag_kernel(rows, cols, phonon_lags, first, second):
    offset = cols[None, :] - rows[:, None]
    upward = (offset[None, :, :] == phonon_lags[:, None, None]).astype(jnp.float32)
    downward = (offset[None, :, :] == -phonon_lags[:, None, None]).astype(jnp.float32)
    return jnp.sum(first[:, None, None] * upward + second[:, None, None] * downward, axis=0)


def lag_sums(rows, everyone, phonon_lags, strengths):
    cols = jnp.arange(everyone.shape[0], dtype=jnp.int32)
    k_less = lag_kernel(rows, cols, phonon_lags, strengths[0], strengths[1])
    k_great = lag_kernel(rows, cols, phonon_lags, strengths[1], strengths[0])
    kernels = jnp.stack([k_less, k_great], axis=-1)
    return jnp.sum(kernels[..., None] * everyone[None], axis=1)


def left_body(chunk, streamed, lesser_ref, dipole_ref, left_ref, *rest):
    width = left_ref.shape[0]
    unit, rows = width // EIGHTHS, width // 4
    starts = range(0, width, rows)
    if streamed:
        again_ref, blocks, arrived = rest
        copies = [
            pltpu.make_async_copy(
                lesser_ref.at[0, 0, chunk[0][0], pl.ds(i, rows)], blocks.at[pl.ds(i, rows)], sem
            )
            for i, sem in zip(starts, [arrived.at[n] for n in range(len(starts))])
        ]
        for copy in copies:
            copy.start()
    at = 0
    for part, first, eighths in chunk:
        cols = eighths * unit
        for n, i in enumerate(starts):
            if streamed:
                copies[n].wait()
                block = blocks[i : i + rows]
            else:
                block = lesser_ref[0, 0, part, i : i + rows]
            product = lax.dot_general(
                block,
                dipole_ref[0, first * unit : first * unit + cols],
                (((1,), (1,)), ((), ())),
                preferred_element_type=jnp.float32,
            ).astype(left_ref.dtype)
            left_ref[i : i + rows, at : at + cols] = product
            if streamed:
                again_ref[i : i + rows, at : at + cols] = product
        at += cols


def left_of(lesser, dipole, chunk, streamed=False):
    width = lesser.shape[-1]
    cols = width // EIGHTHS * sum(eighths for _, _, eighths in chunk)
    scratch = [pltpu.VMEM((width, width), lesser.dtype), pltpu.SemaphoreType.DMA((4,))]
    return pl.pallas_call(
        functools.partial(left_body, chunk, streamed),
        in_specs=[
            pl.BlockSpec(memory_space=pl.ANY if streamed else pltpu.VMEM),
            pl.BlockSpec(memory_space=pltpu.VMEM),
        ],
        out_specs=[pl.BlockSpec(memory_space=pltpu.VMEM)] * (2 if streamed else 1),
        out_shape=[jax.ShapeDtypeStruct((width, cols), lesser.dtype)] * (2 if streamed else 1),
        scratch_shapes=scratch if streamed else [],
        compiler_params=pltpu.CompilerParams(
            vmem_limit_bytes=FIRST_VMEM_BYTES if streamed else SMALL_VMEM_BYTES
        ),
        name="left",
    )(lesser, dipole)


def either_body(flag_ref, yes_ref, no_ref, out_ref):
    height = out_ref.shape[0]
    rows = height // 16

    def copied_from(ref):
        @pl.loop(0, height // rows)
        def _(i):
            at = pl.ds(pl.multiple_of(i * rows, rows), rows)
            out_ref[at] = ref[at]

    pl.when(flag_ref[0] != 0)(lambda: copied_from(yes_ref))
    pl.when(flag_ref[0] == 0)(lambda: copied_from(no_ref))


def either_of(flag, yes, no):
    return pl.pallas_call(
        either_body,
        in_specs=[
            pl.BlockSpec(memory_space=pltpu.SMEM),
            pl.BlockSpec(memory_space=pltpu.VMEM),
            pl.BlockSpec(memory_space=pltpu.VMEM),
        ],
        out_specs=pl.BlockSpec(memory_space=pltpu.VMEM),
        out_shape=jax.ShapeDtypeStruct(yes.shape, yes.dtype),
        compiler_params=pltpu.CompilerParams(vmem_limit_bytes=SMALL_VMEM_BYTES),
        name="either",
    )(flag.astype(jnp.int32).reshape(1), yes, no)


def held_body(block_ref, out_ref):
    out_ref[...] = block_ref[...]


def held_of(block, flops):
    return pl.pallas_call(
        held_body,
        in_specs=[pl.BlockSpec(memory_space=pltpu.VMEM)],
        out_specs=pl.BlockSpec(memory_space=pltpu.VMEM),
        out_shape=jax.ShapeDtypeStruct(block.shape, block.dtype),
        cost_estimate=pl.CostEstimate(flops=flops, bytes_accessed=0, transcendentals=0),
        compiler_params=pltpu.CompilerParams(vmem_limit_bytes=SMALL_VMEM_BYTES),
        name="held",
    )(block)


def pieces_of(chunk):
    pieces, place = [], 0
    for part, first, eighths in chunk:
        for at in range(first, first + eighths, 2):
            size = min(2, first + eighths - at)
            pieces.append((part, at, place, size))
            place += size
    return pieces


def photon_body(chunk, skips, factors_ref, dipole_ref, phonon_ref, own_ref, *rest):
    sides, (out_ref, results, sent) = rest[: len(skips)], rest[-3:]
    width = own_ref.shape[0]
    unit = width // EIGHTHS
    factors = [factors_ref[n] for n in range(2 + len(skips))]
    copies = []
    for k, (part, at, place, size) in enumerate(pieces_of(chunk)):
        at, place, cols = at * unit, place * unit, size * unit

        def piece(ref, skip=0):
            return ref[:, skip * unit + place : skip * unit + place + cols].astype(jnp.float32)

        side = factors[2] * piece(sides[0], skips[0])
        for factor, ref, skip in zip(factors[3:], sides[1:], skips[1:]):
            side += factor * piece(ref, skip)
        mixed = (factors[0] * piece(own_ref) + factors[1] * side).astype(jnp.bfloat16)
        photon = jnp.dot(dipole_ref[0], mixed, preferred_element_type=jnp.float32)
        if part == 1:
            row = lax.broadcasted_iota(jnp.int32, photon.shape, 0)
            col = lax.broadcasted_iota(jnp.int32, photon.shape, 1) + at
            photon += jnp.where(row == col, phonon_ref[:, at : at + cols], 0.0)
        results[k, :, :cols] = photon.astype(results.dtype)
        copies.append(
            pltpu.make_async_copy(
                results.at[k, :, pl.ds(0, cols)],
                out_ref.at[0, 0, part, :, pl.ds(at, cols)],
                sent.at[k],
            )
        )
        copies[-1].start()
    for copy in copies:
        copy.wait()


def photon_of(chunk, factors, dipole, phonon, own, sides, out):
    width = own.shape[0]
    sides, skips = zip(*sides)
    n_pieces = len(pieces_of(chunk))
    operands = [factors, dipole, phonon, own, *sides]
    in_specs = [pl.BlockSpec(memory_space=pltpu.SMEM)]
    in_specs += [pl.BlockSpec(memory_space=pltpu.VMEM)] * (len(operands) - 1)
    aliases = {}
    if out is not None:
        aliases = {len(operands): 0}
        operands.append(out)
        in_specs.append(pl.BlockSpec(memory_space=pl.ANY))
    return pl.pallas_call(
        functools.partial(photon_body, chunk, skips),
        in_specs=in_specs,
        out_specs=pl.BlockSpec(memory_space=pl.ANY),
        out_shape=jax.ShapeDtypeStruct((1, 1, 2, width, width), jnp.bfloat16),
        scratch_shapes=[
            pltpu.VMEM((n_pieces, width, 2 * width // EIGHTHS), jnp.bfloat16),
            pltpu.SemaphoreType.DMA((n_pieces,)),
        ],
        input_output_aliases=aliases,
        compiler_params=pltpu.CompilerParams(vmem_limit_bytes=VMEM_BYTES),
        name="photon",
    )(*operands)


def on_device(
    lesser,
    greater_diag,
    dipole,
    photon_weights,
    sidebands,
    phonon_lags,
    phonon_strengths,
    slab_coupling,
):
    width = lesser.shape[-1]
    count = lax.axis_size("energy")
    own = lax.axis_index("energy")
    everyone = doubled(diagonals_of(lesser, greater_diag), "energy", 1)
    sent, kept = left_of(lesser, dipole, CHUNKS[0], streamed=True)
    left = [kept] + [left_of(lesser, dipole, chunk)[0] for chunk in CHUNKS[1:]]
    everyone, sent = lax.optimization_barrier((everyone, sent))
    weight_0, weight_low, weight_high = photon_weights[0]
    flag = sidebands[0].astype(jnp.float32)
    if count == 8:
        first, second = {}, {}
        hops = tuple((source, by) for source, by, _ in DETOURS)
        second_hops = tuple((by, target) for _, by, target in DETOURS)
        first[0] = lax.ppermute(sent, "energy", STRAIGHT + hops)
        first[1] = lax.ppermute(left[1], "energy", STRAIGHT)

        is_low = own < count // 2
        for route in (TO_HUBS, BETWEEN_HUBS):
            other = lax.ppermute(everyone, "energy", route)
            everyone = jnp.concatenate(
                [jnp.where(is_low, everyone, other), jnp.where(is_low, other, everyone)], axis=0
            )
        hubs = [hub for hub, _ in BETWEEN_HUBS]
        to = [[own] + [dict(route)[hub] for route in FROM_HUBS] for hub in hubs]
        rows = [jnp.where(is_low, low, high) for low, high in zip(*to)]
        sums = lag_sums(jnp.stack(rows), everyone, phonon_lags, phonon_strengths)
        correlated = jnp.where(any_of(own, hubs), sums[0], 0.0)
        for n, route in enumerate(FROM_HUBS):
            correlated += lax.ppermute(sums[n + 1], "energy", route)

        (middle,) = left_of(lesser, dipole, MIDDLE)
        first[0], correlated, *left, middle = lax.optimization_barrier(
            (first[0], correlated, *left, middle)
        )
        relays = any_of(own, [by for by, _ in second_hops])
        onward = either_of(relays, first[0], left[0])
        second[0] = lax.ppermute(onward, "energy", EDGES + second_hops)
        crossed = lax.ppermute(middle, "energy", CROSS)
        first[2] = lax.ppermute(left[2], "energy", STRAIGHT)
        first[1] = held_of(first[1], 4000000000)
        first[1], left[3] = lax.optimization_barrier((first[1], left[3]))
        second[3] = lax.ppermute(left[3], "energy", CROSS)
        first[3] = lax.ppermute(left[3], "energy", STRAIGHT)
        weights = [
            side_weight(own, STRAIGHT, weight_low, weight_high),
            side_weight(own, CROSS, weight_low, weight_high),
        ]
    else:
        step = 2
        while step < count:
            everyone = doubled(everyone, "energy", step)
            step *= 2
        correlated = lag_sums(own[None], everyone, phonon_lags, phonon_strengths)[0]
        first = [shifted(block, "energy", PHOT_BLOCKS) for block in left]
        second = [shifted(block, "energy", -PHOT_BLOCKS) for block in left]
        weights = [weight_low, weight_high]
    factors = jnp.stack([weight_0, flag, *weights])
    if count == 8:
        sides = [
            [(first[0], 0), (second[0], 0)],
            [(first[1], 0), (crossed, 0)],
            [(first[2], 0), (crossed, 2)],
            [(first[3], 0), (second[3], 0)],
        ]
    else:
        sides = [[(low, 0), (high, 0)] for low, high in zip(first, second)]

    correlated = held_of(correlated, 7000000000)
    below = shifted(slab_coupling * correlated, "slab", 1)
    above = shifted(correlated, "slab", -1)
    phon_less, phon_great = correlated + below + slab_coupling * above

    out = None
    for n, chunk in enumerate(CHUNKS):
        out = photon_of(chunk, factors, dipole, phon_less[None], left[n], sides[n], out)
    return out, phon_great[None, None]


def solution(mesh):
    return jax.shard_map(
        on_device,
        mesh=mesh,
        in_specs=(
            P("energy", "slab", None, None, None),
            P("energy", "slab", None),
            P("slab", None, None),
            P("energy", None),
            P("energy"),
            P(),
            P(),
            P("slab", None),
        ),
        out_specs=(P("energy", "slab", None, None, None), P("energy", "slab", None)),
        check_vma=False,
    )
```

```python
import functools

import jax
import jax.numpy as jnp
from jax import lax
from jax.experimental import pallas as pl
from jax.experimental.pallas import tpu as pltpu
from jax.sharding import PartitionSpec as P

PHOT_BLOCKS = 3
CHUNKS = (((0, 0, 8),), ((1, 0, 2),), ((1, 2, 5),), ((1, 7, 1),))
MIDDLE = ((1, 0, 7),)
EIGHTHS = 8
VMEM_BYTES = 20 * 1024 * 1024
EARLY_VMEM_BYTES = 53 * 1024 * 1024
FIRST_VMEM_BYTES = 48 * 1024 * 1024

STRAIGHT = ((0, 3), (2, 5), (3, 6), (4, 1), (5, 2), (7, 4))
CROSS = ((1, 4), (3, 0), (4, 7), (6, 3))
DETOURS = ((1, 0, 4), (6, 7, 3))
EDGES = ((3, 0), (4, 7))
OTHERS = ((1, 4), (6, 3))
EDGES_BY = ((3, 2), (4, 5))
EDGES_ON = ((2, 0), (5, 7))

TO_HUBS = ((3, 1), (4, 6))
BETWEEN_HUBS = ((1, 6), (6, 1))
FROM_HUBS = (((1, 3), (6, 4)), ((1, 5), (6, 2)), ((1, 7), (6, 0)))


def shifted(block, axis, distance):
    devices = range(lax.axis_size(axis))
    return lax.ppermute(
        block, axis, [(i - distance, i) for i in devices if i - distance in devices]
    )


def any_of(own, energies):
    return functools.reduce(jnp.logical_or, [own == energy for energy in energies])


def side_weight(own, route, low, high):
    from_low = any_of(own, [target for source, target in route if source < target])
    from_high = any_of(own, [target for source, target in route if source > target])
    return jnp.where(from_low, low, jnp.where(from_high, high, 0.0))


def doubled(block, axis, step):
    other = lax.ppermute(block, axis, [(i, i ^ step) for i in range(lax.axis_size(axis))])
    upper = (lax.axis_index(axis) & step) != 0
    return jnp.concatenate(
        [jnp.where(upper, other, block), jnp.where(upper, block, other)], axis=0
    )


def diagonals_body(tile, lesser_ref, greater_ref, out_ref, tiles, arrived):
    count = tiles.shape[0]
    copies = [
        pltpu.make_async_copy(
            lesser_ref.at[0, 0, 1, pl.ds(n * tile, tile), pl.ds(n * tile, tile)],
            tiles.at[n],
            arrived.at[n],
        )
        for n in range(count)
    ]
    for copy in copies:
        copy.start()
    row = lax.broadcasted_iota(jnp.int32, (tile, tile), 0)
    col = lax.broadcasted_iota(jnp.int32, (tile, tile), 1)
    out_ref[0, 1:2] = greater_ref[0]
    for n, copy in enumerate(copies):
        copy.wait()
        block = jnp.where(row == col, tiles[n].astype(jnp.float32), 0.0)
        out_ref[0, 0:1, n * tile : (n + 1) * tile] = jnp.sum(block, axis=0, keepdims=True)


def diagonals_of(lesser, greater_diag):
    width = lesser.shape[-1]
    tile = 128
    return pl.pallas_call(
        functools.partial(diagonals_body, tile),
        in_specs=[
            pl.BlockSpec(memory_space=pltpu.HBM),
            pl.BlockSpec(memory_space=pltpu.VMEM),
        ],
        out_specs=pl.BlockSpec(memory_space=pltpu.VMEM),
        out_shape=jax.ShapeDtypeStruct((1, 2, width), jnp.float32),
        scratch_shapes=[
            pltpu.VMEM((width // tile, tile, tile), lesser.dtype),
            pltpu.SemaphoreType.DMA((width // tile,)),
        ],
        compiler_params=pltpu.CompilerParams(vmem_limit_bytes=EARLY_VMEM_BYTES),
        name="diagonals",
    )(lesser, greater_diag)


def lag_kernel(rows, cols, phonon_lags, first, second):
    offset = cols[None, :] - rows[:, None]
    upward = (offset[None, :, :] == phonon_lags[:, None, None]).astype(jnp.float32)
    downward = (offset[None, :, :] == -phonon_lags[:, None, None]).astype(jnp.float32)
    return jnp.sum(first[:, None, None] * upward + second[:, None, None] * downward, axis=0)


def lag_sums(rows, everyone, phonon_lags, strengths):
    cols = jnp.arange(everyone.shape[0], dtype=jnp.int32)
    k_less = lag_kernel(rows, cols, phonon_lags, strengths[0], strengths[1])
    k_great = lag_kernel(rows, cols, phonon_lags, strengths[1], strengths[0])
    kernels = jnp.stack([k_less, k_great], axis=-1)
    return jnp.sum(kernels[..., None] * everyone[None], axis=1)


def left_body(chunk, streamed, lesser_ref, dipole_ref, left_ref, *scratch):
    width = left_ref.shape[0]
    unit, rows = width // EIGHTHS, width // 4
    starts = range(0, width, rows)
    if streamed:
        blocks, arrived = scratch
        copies = [
            pltpu.make_async_copy(
                lesser_ref.at[0, 0, chunk[0][0], pl.ds(i, rows)], blocks.at[pl.ds(i, rows)], sem
            )
            for i, sem in zip(starts, [arrived.at[n] for n in range(len(starts))])
        ]
        for copy in copies:
            copy.start()
    at = 0
    for part, first, eighths in chunk:
        cols = eighths * unit
        for n, i in enumerate(starts):
            if streamed:
                copies[n].wait()
                block = blocks[i : i + rows]
            else:
                block = lesser_ref[0, 0, part, i : i + rows]
            left_ref[i : i + rows, at : at + cols] = lax.dot_general(
                block,
                dipole_ref[0, first * unit : first * unit + cols],
                (((1,), (1,)), ((), ())),
                preferred_element_type=jnp.float32,
            ).astype(left_ref.dtype)
        at += cols


def left_of(lesser, dipole, chunk, streamed=False):
    width = lesser.shape[-1]
    cols = width // EIGHTHS * sum(eighths for _, _, eighths in chunk)
    scratch = [pltpu.VMEM((width, width), lesser.dtype), pltpu.SemaphoreType.DMA((4,))]
    return pl.pallas_call(
        functools.partial(left_body, chunk, streamed),
        in_specs=[
            pl.BlockSpec(memory_space=pl.ANY if streamed else pltpu.VMEM),
            pl.BlockSpec(memory_space=pltpu.VMEM),
        ],
        out_specs=pl.BlockSpec(memory_space=pltpu.VMEM),
        out_shape=jax.ShapeDtypeStruct((width, cols), lesser.dtype),
        scratch_shapes=scratch if streamed else [],
        compiler_params=pltpu.CompilerParams(
            vmem_limit_bytes=FIRST_VMEM_BYTES if streamed else VMEM_BYTES
        ),
        name="left",
    )(lesser, dipole)


def either_body(flag_ref, yes_ref, no_ref, out_ref):
    height = out_ref.shape[0]
    rows = height // 16

    def copied_from(ref):
        @pl.loop(0, height // rows)
        def _(i):
            at = pl.ds(pl.multiple_of(i * rows, rows), rows)
            out_ref[at] = ref[at]

    pl.when(flag_ref[0] != 0)(lambda: copied_from(yes_ref))
    pl.when(flag_ref[0] == 0)(lambda: copied_from(no_ref))


def either_of(flag, yes, no):
    return pl.pallas_call(
        either_body,
        in_specs=[
            pl.BlockSpec(memory_space=pltpu.SMEM),
            pl.BlockSpec(memory_space=pltpu.VMEM),
            pl.BlockSpec(memory_space=pltpu.VMEM),
        ],
        out_specs=pl.BlockSpec(memory_space=pltpu.VMEM),
        out_shape=jax.ShapeDtypeStruct(yes.shape, yes.dtype),
        compiler_params=pltpu.CompilerParams(vmem_limit_bytes=VMEM_BYTES),
        name="either",
    )(flag.astype(jnp.int32).reshape(1), yes, no)


def held_body(block_ref, out_ref):
    out_ref[...] = block_ref[...]


def held_of(block, flops):
    return pl.pallas_call(
        held_body,
        in_specs=[pl.BlockSpec(memory_space=pltpu.VMEM)],
        out_specs=pl.BlockSpec(memory_space=pltpu.VMEM),
        out_shape=jax.ShapeDtypeStruct(block.shape, block.dtype),
        cost_estimate=pl.CostEstimate(flops=flops, bytes_accessed=0, transcendentals=0),
        compiler_params=pltpu.CompilerParams(vmem_limit_bytes=VMEM_BYTES),
        name="held",
    )(block)


def pieces_of(chunk):
    pieces, place = [], 0
    for part, first, eighths in chunk:
        for at in range(first, first + eighths, 2):
            size = min(2, first + eighths - at)
            pieces.append((part, at, place, size))
            place += size
    return pieces


def photon_body(chunk, skips, factors_ref, dipole_ref, phonon_ref, own_ref, *rest):
    sides, (out_ref, results, sent) = rest[: len(skips)], rest[-3:]
    width = own_ref.shape[0]
    unit = width // EIGHTHS
    factors = [factors_ref[n] for n in range(2 + len(skips))]
    copies = []
    for k, (part, at, place, size) in enumerate(pieces_of(chunk)):
        at, place, cols = at * unit, place * unit, size * unit

        def piece(ref, skip=0):
            return ref[:, skip * unit + place : skip * unit + place + cols].astype(jnp.float32)

        side = factors[2] * piece(sides[0], skips[0])
        for factor, ref, skip in zip(factors[3:], sides[1:], skips[1:]):
            side += factor * piece(ref, skip)
        mixed = (factors[0] * piece(own_ref) + factors[1] * side).astype(jnp.bfloat16)
        photon = jnp.dot(dipole_ref[0], mixed, preferred_element_type=jnp.float32)
        if part == 1:
            row = lax.broadcasted_iota(jnp.int32, photon.shape, 0)
            col = lax.broadcasted_iota(jnp.int32, photon.shape, 1) + at
            photon += jnp.where(row == col, phonon_ref[:, at : at + cols], 0.0)
        results[k, :, :cols] = photon.astype(results.dtype)
        copies.append(
            pltpu.make_async_copy(
                results.at[k, :, pl.ds(0, cols)],
                out_ref.at[0, 0, part, :, pl.ds(at, cols)],
                sent.at[k],
            )
        )
        copies[-1].start()
    for copy in copies:
        copy.wait()


def photon_of(chunk, factors, dipole, phonon, own, sides, out):
    width = own.shape[0]
    sides, skips = zip(*sides)
    n_pieces = len(pieces_of(chunk))
    operands = [factors, dipole, phonon, own, *sides]
    in_specs = [pl.BlockSpec(memory_space=pltpu.SMEM)]
    in_specs += [pl.BlockSpec(memory_space=pltpu.VMEM)] * (len(operands) - 1)
    aliases = {}
    if out is not None:
        aliases = {len(operands): 0}
        operands.append(out)
        in_specs.append(pl.BlockSpec(memory_space=pl.ANY))
    return pl.pallas_call(
        functools.partial(photon_body, chunk, skips),
        in_specs=in_specs,
        out_specs=pl.BlockSpec(memory_space=pl.ANY),
        out_shape=jax.ShapeDtypeStruct((1, 1, 2, width, width), jnp.bfloat16),
        scratch_shapes=[
            pltpu.VMEM((n_pieces, width, 2 * width // EIGHTHS), jnp.bfloat16),
            pltpu.SemaphoreType.DMA((n_pieces,)),
        ],
        input_output_aliases=aliases,
        compiler_params=pltpu.CompilerParams(vmem_limit_bytes=VMEM_BYTES),
        name="photon",
    )(*operands)


def on_device(
    lesser,
    greater_diag,
    dipole,
    photon_weights,
    sidebands,
    phonon_lags,
    phonon_strengths,
    slab_coupling,
):
    width = lesser.shape[-1]
    count = lax.axis_size("energy")
    own = lax.axis_index("energy")
    everyone = doubled(diagonals_of(lesser, greater_diag), "energy", 1)
    left = [left_of(lesser, dipole, CHUNKS[0], streamed=True)]
    left += [left_of(lesser, dipole, chunk) for chunk in CHUNKS[1:]]
    everyone, left[0] = lax.optimization_barrier((everyone, left[0]))
    weight_0, weight_low, weight_high = photon_weights[0]
    flag = sidebands[0].astype(jnp.float32)
    if count == 8:
        first, second = {}, {}
        hops = tuple((source, by) for source, by, _ in DETOURS)
        second_hops = tuple((by, target) for _, by, target in DETOURS)
        first[0] = lax.ppermute(left[0], "energy", STRAIGHT + hops)

        is_low = own < count // 2
        for route in (TO_HUBS, BETWEEN_HUBS):
            other = lax.ppermute(everyone, "energy", route)
            everyone = jnp.concatenate(
                [jnp.where(is_low, everyone, other), jnp.where(is_low, other, everyone)], axis=0
            )
        hubs = [hub for hub, _ in BETWEEN_HUBS]
        to = [[own] + [dict(route)[hub] for route in FROM_HUBS] for hub in hubs]
        rows = [jnp.where(is_low, low, high) for low, high in zip(*to)]
        everyone, left[1] = lax.optimization_barrier((everyone, left[1]))
        first[1] = lax.ppermute(left[1], "energy", STRAIGHT)
        sums = lag_sums(jnp.stack(rows), everyone, phonon_lags, phonon_strengths)
        correlated = jnp.where(any_of(own, hubs), sums[0], 0.0)
        for n, route in enumerate(FROM_HUBS):
            correlated += lax.ppermute(sums[n + 1], "energy", route)

        middle = left_of(lesser, dipole, MIDDLE)
        first[0], correlated, *left, middle = lax.optimization_barrier(
            (first[0], correlated, *left, middle)
        )
        relays = any_of(own, [by for by, _ in second_hops])
        onward = either_of(relays, first[0], left[0])
        second[0] = lax.ppermute(onward, "energy", EDGES + second_hops)
        crossed = lax.ppermute(middle, "energy", CROSS)
        first[2] = lax.ppermute(left[2], "energy", STRAIGHT)
        by = lax.ppermute(left[3], "energy", EDGES_BY)
        first[1] = held_of(first[1], 4000000000)
        first[1], left[3], by = lax.optimization_barrier((first[1], left[3], by))
        edge = lax.ppermute(by, "energy", EDGES_ON)
        second[3] = lax.ppermute(left[3], "energy", OTHERS)
        first[3] = lax.ppermute(left[3], "energy", STRAIGHT)
        weights = [
            side_weight(own, STRAIGHT, weight_low, weight_high),
            side_weight(own, CROSS, weight_low, weight_high),
        ]
    else:
        step = 2
        while step < count:
            everyone = doubled(everyone, "energy", step)
            step *= 2
        correlated = lag_sums(own[None], everyone, phonon_lags, phonon_strengths)[0]
        first = [shifted(block, "energy", PHOT_BLOCKS) for block in left]
        second = [shifted(block, "energy", -PHOT_BLOCKS) for block in left]
        weights = [weight_low, weight_high]
    factors = jnp.stack([weight_0, flag, *weights, weights[1]])
    if count == 8:
        sides = [
            [(first[0], 0), (second[0], 0)],
            [(first[1], 0), (crossed, 0)],
            [(first[2], 0), (crossed, 2)],
            [(first[3], 0), (second[3], 0), (edge, 0)],
        ]
    else:
        sides = [[(low, 0), (high, 0)] for low, high in zip(first, second)]

    correlated = held_of(correlated, 17000000000)
    below = shifted(slab_coupling * correlated, "slab", 1)
    above = shifted(correlated, "slab", -1)
    phon_less, phon_great = correlated + below + slab_coupling * above

    out = None
    for n, chunk in enumerate(CHUNKS):
        out = photon_of(chunk, factors, dipole, phon_less[None], left[n], sides[n], out)
    return out, phon_great[None, None]


def solution(mesh):
    return jax.shard_map(
        on_device,
        mesh=mesh,
        in_specs=(
            P("energy", "slab", None, None, None),
            P("energy", "slab", None),
            P("slab", None, None),
            P("energy", None),
            P("energy"),
            P(),
            P(),
            P("slab", None),
        ),
        out_specs=(P("energy", "slab", None, None, None), P("energy", "slab", None)),
        check_vma=False,
    )
```

```python
import functools

import jax
import jax.numpy as jnp
from jax import lax
from jax.experimental import pallas as pl
from jax.experimental.pallas import tpu as pltpu
from jax.sharding import PartitionSpec as P

PHOT_BLOCKS = 3
CHUNKS = (((0, 0, 8),), ((1, 0, 2),), ((1, 2, 5),), ((1, 7, 1),))
MIDDLE = ((1, 0, 7),)
EIGHTHS = 8
VMEM_BYTES = 20 * 1024 * 1024
EARLY_VMEM_BYTES = 53 * 1024 * 1024
FIRST_VMEM_BYTES = 48 * 1024 * 1024

STRAIGHT = ((0, 3), (2, 5), (3, 6), (4, 1), (5, 2), (7, 4))
CROSS = ((1, 4), (3, 0), (4, 7), (6, 3))
DETOURS = ((1, 0, 4), (6, 7, 3))
EDGES = ((3, 0), (4, 7))
OTHERS = ((1, 4), (6, 3))
EDGES_BY = ((3, 2), (4, 5))
EDGES_ON = ((2, 0), (5, 7))

TO_HUBS = ((3, 1), (4, 6))
BETWEEN_HUBS = ((1, 6), (6, 1))
FROM_HUBS = (((1, 3), (6, 4)), ((1, 5), (6, 2)), ((1, 7), (6, 0)))


def shifted(block, axis, distance):
    devices = range(lax.axis_size(axis))
    return lax.ppermute(
        block, axis, [(i - distance, i) for i in devices if i - distance in devices]
    )


def any_of(own, energies):
    return functools.reduce(jnp.logical_or, [own == energy for energy in energies])


def side_weight(own, route, low, high):
    from_low = any_of(own, [target for source, target in route if source < target])
    from_high = any_of(own, [target for source, target in route if source > target])
    return jnp.where(from_low, low, jnp.where(from_high, high, 0.0))


def doubled(block, axis, step):
    other = lax.ppermute(block, axis, [(i, i ^ step) for i in range(lax.axis_size(axis))])
    upper = (lax.axis_index(axis) & step) != 0
    return jnp.concatenate(
        [jnp.where(upper, other, block), jnp.where(upper, block, other)], axis=0
    )


def diagonals_body(tile, lesser_ref, greater_ref, out_ref, tiles, arrived):
    count = tiles.shape[0]
    copies = [
        pltpu.make_async_copy(
            lesser_ref.at[0, 0, 1, pl.ds(n * tile, tile), pl.ds(n * tile, tile)],
            tiles.at[n],
            arrived.at[n],
        )
        for n in range(count)
    ]
    for copy in copies:
        copy.start()
    row = lax.broadcasted_iota(jnp.int32, (tile, tile), 0)
    col = lax.broadcasted_iota(jnp.int32, (tile, tile), 1)
    out_ref[0, 1:2] = greater_ref[0]
    for n, copy in enumerate(copies):
        copy.wait()
        block = jnp.where(row == col, tiles[n].astype(jnp.float32), 0.0)
        out_ref[0, 0:1, n * tile : (n + 1) * tile] = jnp.sum(block, axis=0, keepdims=True)


def diagonals_of(lesser, greater_diag):
    width = lesser.shape[-1]
    tile = 128
    return pl.pallas_call(
        functools.partial(diagonals_body, tile),
        in_specs=[
            pl.BlockSpec(memory_space=pltpu.HBM),
            pl.BlockSpec(memory_space=pltpu.VMEM),
        ],
        out_specs=pl.BlockSpec(memory_space=pltpu.VMEM),
        out_shape=jax.ShapeDtypeStruct((1, 2, width), jnp.float32),
        scratch_shapes=[
            pltpu.VMEM((width // tile, tile, tile), lesser.dtype),
            pltpu.SemaphoreType.DMA((width // tile,)),
        ],
        compiler_params=pltpu.CompilerParams(vmem_limit_bytes=EARLY_VMEM_BYTES),
        name="diagonals",
    )(lesser, greater_diag)


def lag_kernel(rows, cols, phonon_lags, first, second):
    offset = cols[None, :] - rows[:, None]
    upward = (offset[None, :, :] == phonon_lags[:, None, None]).astype(jnp.float32)
    downward = (offset[None, :, :] == -phonon_lags[:, None, None]).astype(jnp.float32)
    return jnp.sum(first[:, None, None] * upward + second[:, None, None] * downward, axis=0)


def lag_sums(rows, everyone, phonon_lags, strengths):
    cols = jnp.arange(everyone.shape[0], dtype=jnp.int32)
    k_less = lag_kernel(rows, cols, phonon_lags, strengths[0], strengths[1])
    k_great = lag_kernel(rows, cols, phonon_lags, strengths[1], strengths[0])
    kernels = jnp.stack([k_less, k_great], axis=-1)
    return jnp.sum(kernels[..., None] * everyone[None], axis=1)


def left_body(chunk, streamed, lesser_ref, dipole_ref, left_ref, *scratch):
    width = left_ref.shape[0]
    unit, rows = width // EIGHTHS, width // 4
    starts = range(0, width, rows)
    if streamed:
        blocks, arrived = scratch
        copies = [
            pltpu.make_async_copy(
                lesser_ref.at[0, 0, chunk[0][0], pl.ds(i, rows)], blocks.at[pl.ds(i, rows)], sem
            )
            for i, sem in zip(starts, [arrived.at[n] for n in range(len(starts))])
        ]
        for copy in copies:
            copy.start()
    at = 0
    for part, first, eighths in chunk:
        cols = eighths * unit
        for n, i in enumerate(starts):
            if streamed:
                copies[n].wait()
                block = blocks[i : i + rows]
            else:
                block = lesser_ref[0, 0, part, i : i + rows]
            left_ref[i : i + rows, at : at + cols] = lax.dot_general(
                block,
                dipole_ref[0, first * unit : first * unit + cols],
                (((1,), (1,)), ((), ())),
                preferred_element_type=jnp.float32,
            ).astype(left_ref.dtype)
        at += cols


def left_of(lesser, dipole, chunk, streamed=False):
    width = lesser.shape[-1]
    cols = width // EIGHTHS * sum(eighths for _, _, eighths in chunk)
    scratch = [pltpu.VMEM((width, width), lesser.dtype), pltpu.SemaphoreType.DMA((4,))]
    return pl.pallas_call(
        functools.partial(left_body, chunk, streamed),
        in_specs=[
            pl.BlockSpec(memory_space=pl.ANY if streamed else pltpu.VMEM),
            pl.BlockSpec(memory_space=pltpu.VMEM),
        ],
        out_specs=pl.BlockSpec(memory_space=pltpu.VMEM),
        out_shape=jax.ShapeDtypeStruct((width, cols), lesser.dtype),
        scratch_shapes=scratch if streamed else [],
        compiler_params=pltpu.CompilerParams(
            vmem_limit_bytes=FIRST_VMEM_BYTES if streamed else VMEM_BYTES
        ),
        name="left",
    )(lesser, dipole)


def either_body(flag_ref, yes_ref, no_ref, out_ref):
    height = out_ref.shape[0]
    rows = height // 16

    def copied_from(ref):
        @pl.loop(0, height // rows)
        def _(i):
            at = pl.ds(pl.multiple_of(i * rows, rows), rows)
            out_ref[at] = ref[at]

    pl.when(flag_ref[0] != 0)(lambda: copied_from(yes_ref))
    pl.when(flag_ref[0] == 0)(lambda: copied_from(no_ref))


def either_of(flag, yes, no):
    return pl.pallas_call(
        either_body,
        in_specs=[
            pl.BlockSpec(memory_space=pltpu.SMEM),
            pl.BlockSpec(memory_space=pltpu.VMEM),
            pl.BlockSpec(memory_space=pltpu.VMEM),
        ],
        out_specs=pl.BlockSpec(memory_space=pltpu.VMEM),
        out_shape=jax.ShapeDtypeStruct(yes.shape, yes.dtype),
        compiler_params=pltpu.CompilerParams(vmem_limit_bytes=VMEM_BYTES),
        name="either",
    )(flag.astype(jnp.int32).reshape(1), yes, no)


def held_body(block_ref, out_ref):
    out_ref[...] = block_ref[...]


def held_of(block, flops):
    return pl.pallas_call(
        held_body,
        in_specs=[pl.BlockSpec(memory_space=pltpu.VMEM)],
        out_specs=pl.BlockSpec(memory_space=pltpu.VMEM),
        out_shape=jax.ShapeDtypeStruct(block.shape, block.dtype),
        cost_estimate=pl.CostEstimate(flops=flops, bytes_accessed=0, transcendentals=0),
        compiler_params=pltpu.CompilerParams(vmem_limit_bytes=VMEM_BYTES),
        name="held",
    )(block)


def pieces_of(chunk):
    pieces, place = [], 0
    for part, first, eighths in chunk:
        for at in range(first, first + eighths, 2):
            size = min(2, first + eighths - at)
            pieces.append((part, at, place, size))
            place += size
    return pieces


def photon_body(segments, factors_ref, dipole_ref, phonon_ref, *refs):
    out_ref, results, sent = refs[-3:]
    copies = []
    for chunk, skips in segments:
        own_ref, *sides = refs[: 1 + len(skips)]
        refs = refs[1 + len(skips) :]
        width = own_ref.shape[0]
        unit = width // EIGHTHS
        factors = [factors_ref[n] for n in range(2 + len(skips))]
        for part, at, place, size in pieces_of(chunk):
            at, place, cols = at * unit, place * unit, size * unit

            def piece(ref, skip=0):
                start = skip * unit + place
                return ref[:, start : start + cols].astype(jnp.float32)

            side = factors[2] * piece(sides[0], skips[0])
            for factor, ref, skip in zip(factors[3:], sides[1:], skips[1:]):
                side += factor * piece(ref, skip)
            mixed = (factors[0] * piece(own_ref) + factors[1] * side).astype(jnp.bfloat16)
            photon = jnp.dot(dipole_ref[0], mixed, preferred_element_type=jnp.float32)
            if part == 1:
                row = lax.broadcasted_iota(jnp.int32, photon.shape, 0)
                col = lax.broadcasted_iota(jnp.int32, photon.shape, 1) + at
                photon += jnp.where(row == col, phonon_ref[:, at : at + cols], 0.0)
            k = len(copies)
            results[k, :, :cols] = photon.astype(results.dtype)
            copies.append(
                pltpu.make_async_copy(
                    results.at[k, :, pl.ds(0, cols)],
                    out_ref.at[0, 0, part, :, pl.ds(at, cols)],
                    sent.at[k],
                )
            )
            copies[-1].start()
    for copy in copies:
        copy.wait()


def photon_of(segments, factors, dipole, phonon, out):
    width = dipole.shape[-1]
    n_pieces = sum(len(pieces_of(chunk)) for chunk, _, _ in segments)
    operands = [factors, dipole, phonon]
    for _, own, sides in segments:
        operands += [own, *(block for block, _ in sides)]
    layout = [(chunk, [skip for _, skip in sides]) for chunk, _, sides in segments]
    in_specs = [pl.BlockSpec(memory_space=pltpu.SMEM)]
    in_specs += [pl.BlockSpec(memory_space=pltpu.VMEM)] * (len(operands) - 1)
    aliases = {}
    if out is not None:
        aliases = {len(operands): 0}
        operands.append(out)
        in_specs.append(pl.BlockSpec(memory_space=pl.ANY))
    return pl.pallas_call(
        functools.partial(photon_body, layout),
        in_specs=in_specs,
        out_specs=pl.BlockSpec(memory_space=pl.ANY),
        out_shape=jax.ShapeDtypeStruct((1, 1, 2, width, width), jnp.bfloat16),
        scratch_shapes=[
            pltpu.VMEM((n_pieces, width, 2 * width // EIGHTHS), jnp.bfloat16),
            pltpu.SemaphoreType.DMA((n_pieces,)),
        ],
        input_output_aliases=aliases,
        compiler_params=pltpu.CompilerParams(vmem_limit_bytes=VMEM_BYTES),
        name="photon",
    )(*operands)


def on_device(
    lesser,
    greater_diag,
    dipole,
    photon_weights,
    sidebands,
    phonon_lags,
    phonon_strengths,
    slab_coupling,
):
    width = lesser.shape[-1]
    count = lax.axis_size("energy")
    own = lax.axis_index("energy")
    everyone = doubled(diagonals_of(lesser, greater_diag), "energy", 1)
    left = [left_of(lesser, dipole, CHUNKS[0], streamed=True)]
    left += [left_of(lesser, dipole, chunk) for chunk in CHUNKS[1:]]
    everyone, left[0] = lax.optimization_barrier((everyone, left[0]))
    weight_0, weight_low, weight_high = photon_weights[0]
    flag = sidebands[0].astype(jnp.float32)
    if count == 8:
        first, second = {}, {}
        hops = tuple((source, by) for source, by, _ in DETOURS)
        second_hops = tuple((by, target) for _, by, target in DETOURS)
        first[0] = lax.ppermute(left[0], "energy", STRAIGHT + hops)

        is_low = own < count // 2
        for route in (TO_HUBS, BETWEEN_HUBS):
            other = lax.ppermute(everyone, "energy", route)
            everyone = jnp.concatenate(
                [jnp.where(is_low, everyone, other), jnp.where(is_low, other, everyone)], axis=0
            )
        hubs = [hub for hub, _ in BETWEEN_HUBS]
        to = [[own] + [dict(route)[hub] for route in FROM_HUBS] for hub in hubs]
        rows = [jnp.where(is_low, low, high) for low, high in zip(*to)]
        everyone, left[1] = lax.optimization_barrier((everyone, left[1]))
        first[1] = lax.ppermute(left[1], "energy", STRAIGHT)
        sums = lag_sums(jnp.stack(rows), everyone, phonon_lags, phonon_strengths)
        correlated = jnp.where(any_of(own, hubs), sums[0], 0.0)
        for n, route in enumerate(FROM_HUBS):
            correlated += lax.ppermute(sums[n + 1], "energy", route)

        middle = left_of(lesser, dipole, MIDDLE)
        first[0], correlated, *left, middle = lax.optimization_barrier(
            (first[0], correlated, *left, middle)
        )
        relays = any_of(own, [by for by, _ in second_hops])
        onward = either_of(relays, first[0], left[0])
        second[0] = lax.ppermute(onward, "energy", EDGES + second_hops)
        crossed = lax.ppermute(middle, "energy", CROSS)
        first[2] = lax.ppermute(left[2], "energy", STRAIGHT)
        by = lax.ppermute(left[3], "energy", EDGES_BY)
        first[1] = held_of(first[1], 4000000000)
        first[1], left[3], by = lax.optimization_barrier((first[1], left[3], by))
        edge = lax.ppermute(by, "energy", EDGES_ON)
        second[3] = lax.ppermute(left[3], "energy", OTHERS)
        first[3] = lax.ppermute(left[3], "energy", STRAIGHT)
        weights = [
            side_weight(own, STRAIGHT, weight_low, weight_high),
            side_weight(own, CROSS, weight_low, weight_high),
        ]
    else:
        step = 2
        while step < count:
            everyone = doubled(everyone, "energy", step)
            step *= 2
        correlated = lag_sums(own[None], everyone, phonon_lags, phonon_strengths)[0]
        first = [shifted(block, "energy", PHOT_BLOCKS) for block in left]
        second = [shifted(block, "energy", -PHOT_BLOCKS) for block in left]
        weights = [weight_low, weight_high]
    factors = jnp.stack([weight_0, flag, *weights, weights[1]])
    if count == 8:
        sides = [
            [(first[0], 0), (second[0], 0)],
            [(first[1], 0), (crossed, 0)],
            [(first[2], 0), (crossed, 2)],
            [(first[3], 0), (second[3], 0), (edge, 0)],
        ]
    else:
        sides = [[(low, 0), (high, 0)] for low, high in zip(first, second)]

    correlated = held_of(correlated, 17000000000)
    below = shifted(slab_coupling * correlated, "slab", 1)
    above = shifted(correlated, "slab", -1)
    phon_less, phon_great = correlated + below + slab_coupling * above

    out = None
    for together in ((0,), (1, 2), (3,)):
        segments = [(CHUNKS[n], left[n], sides[n]) for n in together]
        out = photon_of(segments, factors, dipole, phon_less[None], out)
    return out, phon_great[None, None]


def solution(mesh):
    return jax.shard_map(
        on_device,
        mesh=mesh,
        in_specs=(
            P("energy", "slab", None, None, None),
            P("energy", "slab", None),
            P("slab", None, None),
            P("energy", None),
            P("energy"),
            P(),
            P(),
            P("slab", None),
        ),
        out_specs=(P("energy", "slab", None, None, None), P("energy", "slab", None)),
        check_vma=False,
    )
```

```python
import functools

import jax
import jax.numpy as jnp
from jax import lax
from jax.experimental import pallas as pl
from jax.experimental.pallas import tpu as pltpu
from jax.sharding import PartitionSpec as P

PHOT_BLOCKS = 3
CHUNKS = (((0, 0, 8),), ((1, 0, 2),), ((1, 2, 5),), ((1, 7, 1),))
MIDDLE = ((1, 0, 7),)
EIGHTHS = 8
VMEM_BYTES = 20 * 1024 * 1024
EARLY_VMEM_BYTES = 53 * 1024 * 1024
FIRST_VMEM_BYTES = 48 * 1024 * 1024

STRAIGHT = ((0, 3), (2, 5), (3, 6), (4, 1), (5, 2), (7, 4))
CROSS = ((1, 4), (3, 0), (4, 7), (6, 3))
DETOURS = ((1, 0, 4), (6, 7, 3))
EDGES = ((3, 0), (4, 7))
OTHERS = ((1, 4), (6, 3))
EDGES_BY = ((3, 2), (4, 5))
EDGES_ON = ((2, 0), (5, 7))

TO_HUBS = ((3, 1), (4, 6))
BETWEEN_HUBS = ((1, 6), (6, 1))
FROM_HUBS = (((1, 3), (6, 4)), ((1, 5), (6, 2)), ((1, 7), (6, 0)))


def shifted(block, axis, distance):
    devices = range(lax.axis_size(axis))
    return lax.ppermute(
        block, axis, [(i - distance, i) for i in devices if i - distance in devices]
    )


def any_of(own, energies):
    return functools.reduce(jnp.logical_or, [own == energy for energy in energies])


def side_weight(own, route, low, high):
    from_low = any_of(own, [target for source, target in route if source < target])
    from_high = any_of(own, [target for source, target in route if source > target])
    return jnp.where(from_low, low, jnp.where(from_high, high, 0.0))


def doubled(block, axis, step):
    other = lax.ppermute(block, axis, [(i, i ^ step) for i in range(lax.axis_size(axis))])
    upper = (lax.axis_index(axis) & step) != 0
    return jnp.concatenate(
        [jnp.where(upper, other, block), jnp.where(upper, block, other)], axis=0
    )


def diagonals_body(tile, lesser_ref, greater_ref, out_ref, tiles, arrived):
    count = tiles.shape[0]
    copies = [
        pltpu.make_async_copy(
            lesser_ref.at[0, 0, 1, pl.ds(n * tile, tile), pl.ds(n * tile, tile)],
            tiles.at[n],
            arrived.at[n],
        )
        for n in range(count)
    ]
    for copy in copies:
        copy.start()
    row = lax.broadcasted_iota(jnp.int32, (tile, tile), 0)
    col = lax.broadcasted_iota(jnp.int32, (tile, tile), 1)
    out_ref[0, 1:2] = greater_ref[0]
    for n, copy in enumerate(copies):
        copy.wait()
        block = jnp.where(row == col, tiles[n].astype(jnp.float32), 0.0)
        out_ref[0, 0:1, n * tile : (n + 1) * tile] = jnp.sum(block, axis=0, keepdims=True)


def diagonals_of(lesser, greater_diag):
    width = lesser.shape[-1]
    tile = 128
    return pl.pallas_call(
        functools.partial(diagonals_body, tile),
        in_specs=[
            pl.BlockSpec(memory_space=pltpu.HBM),
            pl.BlockSpec(memory_space=pltpu.VMEM),
        ],
        out_specs=pl.BlockSpec(memory_space=pltpu.VMEM),
        out_shape=jax.ShapeDtypeStruct((1, 2, width), jnp.float32),
        scratch_shapes=[
            pltpu.VMEM((width // tile, tile, tile), lesser.dtype),
            pltpu.SemaphoreType.DMA((width // tile,)),
        ],
        compiler_params=pltpu.CompilerParams(vmem_limit_bytes=EARLY_VMEM_BYTES),
        name="diagonals",
    )(lesser, greater_diag)


def lag_kernel(rows, cols, phonon_lags, first, second):
    offset = cols[None, :] - rows[:, None]
    upward = (offset[None, :, :] == phonon_lags[:, None, None]).astype(jnp.float32)
    downward = (offset[None, :, :] == -phonon_lags[:, None, None]).astype(jnp.float32)
    return jnp.sum(first[:, None, None] * upward + second[:, None, None] * downward, axis=0)


def lag_sums(rows, everyone, phonon_lags, strengths):
    cols = jnp.arange(everyone.shape[0], dtype=jnp.int32)
    k_less = lag_kernel(rows, cols, phonon_lags, strengths[0], strengths[1])
    k_great = lag_kernel(rows, cols, phonon_lags, strengths[1], strengths[0])
    kernels = jnp.stack([k_less, k_great], axis=-1)
    return jnp.sum(kernels[..., None] * everyone[None], axis=1)


def left_body(chunk, streamed, lesser_ref, dipole_ref, left_ref, *scratch):
    width = left_ref.shape[0]
    unit, rows = width // EIGHTHS, width // 4
    starts = range(0, width, rows)
    if streamed:
        blocks, arrived = scratch
        copies = [
            pltpu.make_async_copy(
                lesser_ref.at[0, 0, chunk[0][0], pl.ds(i, rows)], blocks.at[pl.ds(i, rows)], sem
            )
            for i, sem in zip(starts, [arrived.at[n] for n in range(len(starts))])
        ]
        for copy in copies:
            copy.start()
    at = 0
    for part, first, eighths in chunk:
        cols = eighths * unit
        for n, i in enumerate(starts):
            if streamed:
                copies[n].wait()
                block = blocks[i : i + rows]
            else:
                block = lesser_ref[0, 0, part, i : i + rows]
            left_ref[i : i + rows, at : at + cols] = lax.dot_general(
                block,
                dipole_ref[0, first * unit : first * unit + cols],
                (((1,), (1,)), ((), ())),
                preferred_element_type=jnp.float32,
            ).astype(left_ref.dtype)
        at += cols


def left_of(lesser, dipole, chunk, streamed=False):
    width = lesser.shape[-1]
    cols = width // EIGHTHS * sum(eighths for _, _, eighths in chunk)
    scratch = [pltpu.VMEM((width, width), lesser.dtype), pltpu.SemaphoreType.DMA((4,))]
    return pl.pallas_call(
        functools.partial(left_body, chunk, streamed),
        in_specs=[
            pl.BlockSpec(memory_space=pl.ANY if streamed else pltpu.VMEM),
            pl.BlockSpec(memory_space=pltpu.VMEM),
        ],
        out_specs=pl.BlockSpec(memory_space=pltpu.VMEM),
        out_shape=jax.ShapeDtypeStruct((width, cols), lesser.dtype),
        scratch_shapes=scratch if streamed else [],
        compiler_params=pltpu.CompilerParams(
            vmem_limit_bytes=FIRST_VMEM_BYTES if streamed else VMEM_BYTES
        ),
        name="left",
    )(lesser, dipole)


def either_body(flag_ref, yes_ref, no_ref, out_ref):
    height = out_ref.shape[0]
    rows = height // 16

    def copied_from(ref):
        @pl.loop(0, height // rows)
        def _(i):
            at = pl.ds(pl.multiple_of(i * rows, rows), rows)
            out_ref[at] = ref[at]

    pl.when(flag_ref[0] != 0)(lambda: copied_from(yes_ref))
    pl.when(flag_ref[0] == 0)(lambda: copied_from(no_ref))


def either_of(flag, yes, no):
    return pl.pallas_call(
        either_body,
        in_specs=[
            pl.BlockSpec(memory_space=pltpu.SMEM),
            pl.BlockSpec(memory_space=pltpu.VMEM),
            pl.BlockSpec(memory_space=pltpu.VMEM),
        ],
        out_specs=pl.BlockSpec(memory_space=pltpu.VMEM),
        out_shape=jax.ShapeDtypeStruct(yes.shape, yes.dtype),
        compiler_params=pltpu.CompilerParams(vmem_limit_bytes=VMEM_BYTES),
        name="either",
    )(flag.astype(jnp.int32).reshape(1), yes, no)


def held_body(block_ref, out_ref):
    out_ref[...] = block_ref[...]


def held_of(block, flops):
    return pl.pallas_call(
        held_body,
        in_specs=[pl.BlockSpec(memory_space=pltpu.VMEM)],
        out_specs=pl.BlockSpec(memory_space=pltpu.VMEM),
        out_shape=jax.ShapeDtypeStruct(block.shape, block.dtype),
        cost_estimate=pl.CostEstimate(flops=flops, bytes_accessed=0, transcendentals=0),
        compiler_params=pltpu.CompilerParams(vmem_limit_bytes=VMEM_BYTES),
        name="held",
    )(block)


def pieces_of(chunk):
    pieces, place = [], 0
    for part, first, eighths in chunk:
        for at in range(first, first + eighths, 2):
            size = min(2, first + eighths - at)
            pieces.append((part, at, place, size))
            place += size
    return pieces


def photon_body(segments, factors_ref, dipole_ref, phonon_ref, *refs):
    out_ref, results, sent = refs[-3:]
    copies = []
    for chunk, skips in segments:
        own_ref, *sides = refs[: 1 + len(skips)]
        refs = refs[1 + len(skips) :]
        width = own_ref.shape[0]
        unit = width // EIGHTHS
        factors = [factors_ref[n] for n in range(2 + len(skips))]
        for part, at, place, size in pieces_of(chunk):
            at, place, cols = at * unit, place * unit, size * unit

            def piece(ref, skip=0):
                start = skip * unit + place
                return ref[:, start : start + cols].astype(jnp.float32)

            side = factors[2] * piece(sides[0], skips[0])
            for factor, ref, skip in zip(factors[3:], sides[1:], skips[1:]):
                side += factor * piece(ref, skip)
            mixed = (factors[0] * piece(own_ref) + factors[1] * side).astype(jnp.bfloat16)
            photon = jnp.dot(dipole_ref[0], mixed, preferred_element_type=jnp.float32)
            if part == 1:
                row = lax.broadcasted_iota(jnp.int32, photon.shape, 0)
                col = lax.broadcasted_iota(jnp.int32, photon.shape, 1) + at
                photon += jnp.where(row == col, phonon_ref[:, at : at + cols], 0.0)
            k = len(copies)
            results[k, :, :cols] = photon.astype(results.dtype)
            copies.append(
                pltpu.make_async_copy(
                    results.at[k, :, pl.ds(0, cols)],
                    out_ref.at[0, 0, part, :, pl.ds(at, cols)],
                    sent.at[k],
                )
            )
            copies[-1].start()
    for copy in copies:
        copy.wait()


def photon_of(segments, factors, dipole, phonon, out):
    width = dipole.shape[-1]
    n_pieces = sum(len(pieces_of(chunk)) for chunk, _, _ in segments)
    operands = [factors, dipole, phonon]
    for _, own, sides in segments:
        operands += [own, *(block for block, _ in sides)]
    layout = [(chunk, [skip for _, skip in sides]) for chunk, _, sides in segments]
    in_specs = [pl.BlockSpec(memory_space=pltpu.SMEM)]
    in_specs += [pl.BlockSpec(memory_space=pltpu.VMEM)] * (len(operands) - 1)
    aliases = {}
    if out is not None:
        aliases = {len(operands): 0}
        operands.append(out)
        in_specs.append(pl.BlockSpec(memory_space=pl.ANY))
    return pl.pallas_call(
        functools.partial(photon_body, layout),
        in_specs=in_specs,
        out_specs=pl.BlockSpec(memory_space=pl.ANY),
        out_shape=jax.ShapeDtypeStruct((1, 1, 2, width, width), jnp.bfloat16),
        scratch_shapes=[
            pltpu.VMEM((n_pieces, width, 2 * width // EIGHTHS), jnp.bfloat16),
            pltpu.SemaphoreType.DMA((n_pieces,)),
        ],
        input_output_aliases=aliases,
        compiler_params=pltpu.CompilerParams(vmem_limit_bytes=VMEM_BYTES),
        name="photon",
    )(*operands)


def on_device(
    lesser,
    greater_diag,
    dipole,
    photon_weights,
    sidebands,
    phonon_lags,
    phonon_strengths,
    slab_coupling,
):
    width = lesser.shape[-1]
    count = lax.axis_size("energy")
    own = lax.axis_index("energy")
    everyone = doubled(diagonals_of(lesser, greater_diag), "energy", 1)
    left = [left_of(lesser, dipole, CHUNKS[0], streamed=True)]
    left += [left_of(lesser, dipole, chunk) for chunk in CHUNKS[1:]]
    everyone, left[0] = lax.optimization_barrier((everyone, left[0]))
    weight_0, weight_low, weight_high = photon_weights[0]
    flag = sidebands[0].astype(jnp.float32)
    if count == 8:
        first, second = {}, {}
        hops = tuple((source, by) for source, by, _ in DETOURS)
        second_hops = tuple((by, target) for _, by, target in DETOURS)
        first[0] = lax.ppermute(left[0], "energy", STRAIGHT + hops)

        is_low = own < count // 2
        for route in (TO_HUBS, BETWEEN_HUBS):
            other = lax.ppermute(everyone, "energy", route)
            everyone = jnp.concatenate(
                [jnp.where(is_low, everyone, other), jnp.where(is_low, other, everyone)], axis=0
            )
        hubs = [hub for hub, _ in BETWEEN_HUBS]
        to = [[own] + [dict(route)[hub] for route in FROM_HUBS] for hub in hubs]
        rows = [jnp.where(is_low, low, high) for low, high in zip(*to)]
        everyone, left[1] = lax.optimization_barrier((everyone, left[1]))
        first[1] = lax.ppermute(left[1], "energy", STRAIGHT)
        sums = lag_sums(jnp.stack(rows), everyone, phonon_lags, phonon_strengths)
        correlated = jnp.where(any_of(own, hubs), sums[0], 0.0)
        for n, route in enumerate(FROM_HUBS):
            correlated += lax.ppermute(sums[n + 1], "energy", route)

        middle = left_of(lesser, dipole, MIDDLE)
        again = left_of(lesser, dipole, CHUNKS[0])
        first[0], correlated, *left, middle, again = lax.optimization_barrier(
            (first[0], correlated, *left, middle, again)
        )
        relays = any_of(own, [by for by, _ in second_hops])
        onward = either_of(relays, first[0], again)
        second[0] = lax.ppermute(onward, "energy", EDGES + second_hops)
        crossed = lax.ppermute(middle, "energy", CROSS)
        first[2] = lax.ppermute(left[2], "energy", STRAIGHT)
        by = lax.ppermute(left[3], "energy", EDGES_BY)
        first[1] = held_of(first[1], 4000000000)
        first[1], left[3], by = lax.optimization_barrier((first[1], left[3], by))
        edge = lax.ppermute(by, "energy", EDGES_ON)
        second[3] = lax.ppermute(left[3], "energy", OTHERS)
        first[3] = lax.ppermute(left[3], "energy", STRAIGHT)
        weights = [
            side_weight(own, STRAIGHT, weight_low, weight_high),
            side_weight(own, CROSS, weight_low, weight_high),
        ]
    else:
        step = 2
        while step < count:
            everyone = doubled(everyone, "energy", step)
            step *= 2
        correlated = lag_sums(own[None], everyone, phonon_lags, phonon_strengths)[0]
        first = [shifted(block, "energy", PHOT_BLOCKS) for block in left]
        second = [shifted(block, "energy", -PHOT_BLOCKS) for block in left]
        weights = [weight_low, weight_high]
    factors = jnp.stack([weight_0, flag, *weights, weights[1]])
    if count == 8:
        sides = [
            [(first[0], 0), (second[0], 0)],
            [(first[1], 0), (crossed, 0)],
            [(first[2], 0), (crossed, 2)],
            [(first[3], 0), (second[3], 0), (edge, 0)],
        ]
    else:
        sides = [[(low, 0), (high, 0)] for low, high in zip(first, second)]

    correlated = held_of(correlated, 17000000000)
    below = shifted(slab_coupling * correlated, "slab", 1)
    above = shifted(correlated, "slab", -1)
    phon_less, phon_great = correlated + below + slab_coupling * above

    out = None
    for together in ((0,), (1, 2), (3,)):
        segments = [(CHUNKS[n], left[n], sides[n]) for n in together]
        out = photon_of(segments, factors, dipole, phon_less[None], out)
    return out, phon_great[None, None]


def solution(mesh):
    return jax.shard_map(
        on_device,
        mesh=mesh,
        in_specs=(
            P("energy", "slab", None, None, None),
            P("energy", "slab", None),
            P("slab", None, None),
            P("energy", None),
            P("energy"),
            P(),
            P(),
            P("slab", None),
        ),
        out_specs=(P("energy", "slab", None, None, None), P("energy", "slab", None)),
        check_vma=False,
    )
```

```python
import functools

import jax
import jax.numpy as jnp
from jax import lax
from jax.experimental import pallas as pl
from jax.experimental.pallas import tpu as pltpu
from jax.sharding import PartitionSpec as P

PHOT_BLOCKS = 3
CHUNKS = (((0, 0, 8),), ((1, 0, 2),), ((1, 2, 5),), ((1, 7, 1),))
MIDDLE = ((1, 0, 7),)
EIGHTHS = 8
VMEM_BYTES = 20 * 1024 * 1024
EARLY_VMEM_BYTES = 53 * 1024 * 1024
FIRST_VMEM_BYTES = 48 * 1024 * 1024

STRAIGHT = ((0, 3), (2, 5), (3, 6), (4, 1), (5, 2), (7, 4))
CROSS = ((1, 4), (3, 0), (4, 7), (6, 3))
DETOURS = ((1, 0, 4), (6, 7, 3))
EDGES = ((3, 0), (4, 7))
OTHERS = ((1, 4), (6, 3))
EDGES_BY = ((3, 2), (4, 5))
EDGES_ON = ((2, 0), (5, 7))

TO_HUBS = ((3, 1), (4, 6))
BETWEEN_HUBS = ((1, 6), (6, 1))
FROM_HUBS = (((1, 3), (6, 4)), ((1, 5), (6, 2)), ((1, 7), (6, 0)))


def shifted(block, axis, distance):
    devices = range(lax.axis_size(axis))
    return lax.ppermute(
        block, axis, [(i - distance, i) for i in devices if i - distance in devices]
    )


def any_of(own, energies):
    return functools.reduce(jnp.logical_or, [own == energy for energy in energies])


def side_weight(own, route, low, high):
    from_low = any_of(own, [target for source, target in route if source < target])
    from_high = any_of(own, [target for source, target in route if source > target])
    return jnp.where(from_low, low, jnp.where(from_high, high, 0.0))


def doubled(block, axis, step):
    other = lax.ppermute(block, axis, [(i, i ^ step) for i in range(lax.axis_size(axis))])
    upper = (lax.axis_index(axis) & step) != 0
    return jnp.concatenate(
        [jnp.where(upper, other, block), jnp.where(upper, block, other)], axis=0
    )


def diagonals_body(tile, lesser_ref, greater_ref, out_ref, tiles, arrived):
    count = tiles.shape[0]
    copies = [
        pltpu.make_async_copy(
            lesser_ref.at[0, 0, 1, pl.ds(n * tile, tile), pl.ds(n * tile, tile)],
            tiles.at[n],
            arrived.at[n],
        )
        for n in range(count)
    ]
    for copy in copies:
        copy.start()
    row = lax.broadcasted_iota(jnp.int32, (tile, tile), 0)
    col = lax.broadcasted_iota(jnp.int32, (tile, tile), 1)
    out_ref[0, 1:2] = greater_ref[0]
    for n, copy in enumerate(copies):
        copy.wait()
        block = jnp.where(row == col, tiles[n].astype(jnp.float32), 0.0)
        out_ref[0, 0:1, n * tile : (n + 1) * tile] = jnp.sum(block, axis=0, keepdims=True)


def diagonals_of(lesser, greater_diag):
    width = lesser.shape[-1]
    tile = 128
    return pl.pallas_call(
        functools.partial(diagonals_body, tile),
        in_specs=[
            pl.BlockSpec(memory_space=pltpu.HBM),
            pl.BlockSpec(memory_space=pltpu.VMEM),
        ],
        out_specs=pl.BlockSpec(memory_space=pltpu.VMEM),
        out_shape=jax.ShapeDtypeStruct((1, 2, width), jnp.float32),
        scratch_shapes=[
            pltpu.VMEM((width // tile, tile, tile), lesser.dtype),
            pltpu.SemaphoreType.DMA((width // tile,)),
        ],
        compiler_params=pltpu.CompilerParams(vmem_limit_bytes=EARLY_VMEM_BYTES),
        name="diagonals",
    )(lesser, greater_diag)


def lag_kernel(rows, cols, phonon_lags, first, second):
    offset = cols[None, :] - rows[:, None]
    upward = (offset[None, :, :] == phonon_lags[:, None, None]).astype(jnp.float32)
    downward = (offset[None, :, :] == -phonon_lags[:, None, None]).astype(jnp.float32)
    return jnp.sum(first[:, None, None] * upward + second[:, None, None] * downward, axis=0)


def lag_sums(rows, everyone, phonon_lags, strengths):
    cols = jnp.arange(everyone.shape[0], dtype=jnp.int32)
    k_less = lag_kernel(rows, cols, phonon_lags, strengths[0], strengths[1])
    k_great = lag_kernel(rows, cols, phonon_lags, strengths[1], strengths[0])
    kernels = jnp.stack([k_less, k_great], axis=-1)
    return jnp.sum(kernels[..., None] * everyone[None], axis=1)


def left_body(chunk, streamed, lesser_ref, dipole_ref, left_ref, *scratch):
    width = left_ref.shape[0]
    unit, rows = width // EIGHTHS, width // 4
    starts = range(0, width, rows)
    if streamed:
        blocks, arrived = scratch
        copies = [
            pltpu.make_async_copy(
                lesser_ref.at[0, 0, chunk[0][0], pl.ds(i, rows)], blocks.at[pl.ds(i, rows)], sem
            )
            for i, sem in zip(starts, [arrived.at[n] for n in range(len(starts))])
        ]
        for copy in copies:
            copy.start()
    at = 0
    for part, first, eighths in chunk:
        cols = eighths * unit
        for n, i in enumerate(starts):
            if streamed:
                copies[n].wait()
                block = blocks[i : i + rows]
            else:
                block = lesser_ref[0, 0, part, i : i + rows]
            left_ref[i : i + rows, at : at + cols] = lax.dot_general(
                block,
                dipole_ref[0, first * unit : first * unit + cols],
                (((1,), (1,)), ((), ())),
                preferred_element_type=jnp.float32,
            ).astype(left_ref.dtype)
        at += cols


def left_of(lesser, dipole, chunk, streamed=False):
    width = lesser.shape[-1]
    cols = width // EIGHTHS * sum(eighths for _, _, eighths in chunk)
    scratch = [pltpu.VMEM((width, width), lesser.dtype), pltpu.SemaphoreType.DMA((4,))]
    return pl.pallas_call(
        functools.partial(left_body, chunk, streamed),
        in_specs=[
            pl.BlockSpec(memory_space=pl.ANY if streamed else pltpu.VMEM),
            pl.BlockSpec(memory_space=pltpu.VMEM),
        ],
        out_specs=pl.BlockSpec(memory_space=pltpu.VMEM),
        out_shape=jax.ShapeDtypeStruct((width, cols), lesser.dtype),
        scratch_shapes=scratch if streamed else [],
        compiler_params=pltpu.CompilerParams(
            vmem_limit_bytes=FIRST_VMEM_BYTES if streamed else VMEM_BYTES
        ),
        name="left",
    )(lesser, dipole)


def either_body(flag_ref, yes_ref, no_ref, out_ref, arrived):
    def copied_from(ref):
        copy = pltpu.make_async_copy(ref, out_ref, arrived)
        copy.start()
        copy.wait()

    pl.when(flag_ref[0] != 0)(lambda: copied_from(yes_ref))
    pl.when(flag_ref[0] == 0)(lambda: copied_from(no_ref))


def either_of(flag, yes, no):
    return pl.pallas_call(
        either_body,
        in_specs=[
            pl.BlockSpec(memory_space=pltpu.SMEM),
            pl.BlockSpec(memory_space=pl.ANY),
            pl.BlockSpec(memory_space=pl.ANY),
        ],
        out_specs=pl.BlockSpec(memory_space=pltpu.VMEM),
        out_shape=jax.ShapeDtypeStruct(yes.shape, yes.dtype),
        scratch_shapes=[pltpu.SemaphoreType.DMA],
        compiler_params=pltpu.CompilerParams(vmem_limit_bytes=VMEM_BYTES),
        name="either",
    )(flag.astype(jnp.int32).reshape(1), yes, no)


def held_body(block_ref, out_ref):
    out_ref[...] = block_ref[...]


def held_of(block, flops):
    return pl.pallas_call(
        held_body,
        in_specs=[pl.BlockSpec(memory_space=pltpu.VMEM)],
        out_specs=pl.BlockSpec(memory_space=pltpu.VMEM),
        out_shape=jax.ShapeDtypeStruct(block.shape, block.dtype),
        cost_estimate=pl.CostEstimate(flops=flops, bytes_accessed=0, transcendentals=0),
        compiler_params=pltpu.CompilerParams(vmem_limit_bytes=VMEM_BYTES),
        name="held",
    )(block)


def pieces_of(chunk):
    pieces, place = [], 0
    for part, first, eighths in chunk:
        for at in range(first, first + eighths, 2):
            size = min(2, first + eighths - at)
            pieces.append((part, at, place, size))
            place += size
    return pieces


def photon_body(segments, factors_ref, dipole_ref, phonon_ref, *refs):
    out_ref, results, sent = refs[-3:]
    copies = []
    for chunk, skips in segments:
        own_ref, *sides = refs[: 1 + len(skips)]
        refs = refs[1 + len(skips) :]
        width = own_ref.shape[0]
        unit = width // EIGHTHS
        factors = [factors_ref[n] for n in range(2 + len(skips))]
        for part, at, place, size in pieces_of(chunk):
            at, place, cols = at * unit, place * unit, size * unit

            def piece(ref, skip=0):
                start = skip * unit + place
                return ref[:, start : start + cols].astype(jnp.float32)

            side = factors[2] * piece(sides[0], skips[0])
            for factor, ref, skip in zip(factors[3:], sides[1:], skips[1:]):
                side += factor * piece(ref, skip)
            mixed = (factors[0] * piece(own_ref) + factors[1] * side).astype(jnp.bfloat16)
            photon = jnp.dot(dipole_ref[0], mixed, preferred_element_type=jnp.float32)
            if part == 1:
                row = lax.broadcasted_iota(jnp.int32, photon.shape, 0)
                col = lax.broadcasted_iota(jnp.int32, photon.shape, 1) + at
                photon += jnp.where(row == col, phonon_ref[:, at : at + cols], 0.0)
            k = len(copies)
            results[k, :, :cols] = photon.astype(results.dtype)
            copies.append(
                pltpu.make_async_copy(
                    results.at[k, :, pl.ds(0, cols)],
                    out_ref.at[0, 0, part, :, pl.ds(at, cols)],
                    sent.at[k],
                )
            )
            copies[-1].start()
    for copy in copies:
        copy.wait()


def photon_of(segments, factors, dipole, phonon, out):
    width = dipole.shape[-1]
    n_pieces = sum(len(pieces_of(chunk)) for chunk, _, _ in segments)
    operands = [factors, dipole, phonon]
    for _, own, sides in segments:
        operands += [own, *(block for block, _ in sides)]
    layout = [(chunk, [skip for _, skip in sides]) for chunk, _, sides in segments]
    in_specs = [pl.BlockSpec(memory_space=pltpu.SMEM)]
    in_specs += [pl.BlockSpec(memory_space=pltpu.VMEM)] * (len(operands) - 1)
    aliases = {}
    if out is not None:
        aliases = {len(operands): 0}
        operands.append(out)
        in_specs.append(pl.BlockSpec(memory_space=pl.ANY))
    return pl.pallas_call(
        functools.partial(photon_body, layout),
        in_specs=in_specs,
        out_specs=pl.BlockSpec(memory_space=pl.ANY),
        out_shape=jax.ShapeDtypeStruct((1, 1, 2, width, width), jnp.bfloat16),
        scratch_shapes=[
            pltpu.VMEM((n_pieces, width, 2 * width // EIGHTHS), jnp.bfloat16),
            pltpu.SemaphoreType.DMA((n_pieces,)),
        ],
        input_output_aliases=aliases,
        compiler_params=pltpu.CompilerParams(vmem_limit_bytes=VMEM_BYTES),
        name="photon",
    )(*operands)


def on_device(
    lesser,
    greater_diag,
    dipole,
    photon_weights,
    sidebands,
    phonon_lags,
    phonon_strengths,
    slab_coupling,
):
    width = lesser.shape[-1]
    count = lax.axis_size("energy")
    own = lax.axis_index("energy")
    everyone = doubled(diagonals_of(lesser, greater_diag), "energy", 1)
    left = [left_of(lesser, dipole, CHUNKS[0], streamed=True)]
    left += [left_of(lesser, dipole, chunk) for chunk in CHUNKS[1:]]
    everyone, left[0] = lax.optimization_barrier((everyone, left[0]))
    weight_0, weight_low, weight_high = photon_weights[0]
    flag = sidebands[0].astype(jnp.float32)
    if count == 8:
        first, second = {}, {}
        hops = tuple((source, by) for source, by, _ in DETOURS)
        second_hops = tuple((by, target) for _, by, target in DETOURS)
        first[0] = lax.ppermute(left[0], "energy", STRAIGHT + hops)

        is_low = own < count // 2
        for route in (TO_HUBS, BETWEEN_HUBS):
            other = lax.ppermute(everyone, "energy", route)
            everyone = jnp.concatenate(
                [jnp.where(is_low, everyone, other), jnp.where(is_low, other, everyone)], axis=0
            )
        hubs = [hub for hub, _ in BETWEEN_HUBS]
        to = [[own] + [dict(route)[hub] for route in FROM_HUBS] for hub in hubs]
        rows = [jnp.where(is_low, low, high) for low, high in zip(*to)]
        everyone, left[1] = lax.optimization_barrier((everyone, left[1]))
        first[1] = lax.ppermute(left[1], "energy", STRAIGHT)
        sums = lag_sums(jnp.stack(rows), everyone, phonon_lags, phonon_strengths)
        correlated = jnp.where(any_of(own, hubs), sums[0], 0.0)
        for n, route in enumerate(FROM_HUBS):
            correlated += lax.ppermute(sums[n + 1], "energy", route)

        middle = left_of(lesser, dipole, MIDDLE)
        first[0], correlated, *left, middle = lax.optimization_barrier(
            (first[0], correlated, *left, middle)
        )
        relays = any_of(own, [by for by, _ in second_hops])
        onward = either_of(relays, first[0], left[0])
        second[0] = lax.ppermute(onward, "energy", EDGES + second_hops)
        crossed = lax.ppermute(middle, "energy", CROSS)
        first[2] = lax.ppermute(left[2], "energy", STRAIGHT)
        by = lax.ppermute(left[3], "energy", EDGES_BY)
        first[1] = held_of(first[1], 4000000000)
        first[1], left[3], by = lax.optimization_barrier((first[1], left[3], by))
        edge = lax.ppermute(by, "energy", EDGES_ON)
        second[3] = lax.ppermute(left[3], "energy", OTHERS)
        first[3] = lax.ppermute(left[3], "energy", STRAIGHT)
        weights = [
            side_weight(own, STRAIGHT, weight_low, weight_high),
            side_weight(own, CROSS, weight_low, weight_high),
        ]
    else:
        step = 2
        while step < count:
            everyone = doubled(everyone, "energy", step)
            step *= 2
        correlated = lag_sums(own[None], everyone, phonon_lags, phonon_strengths)[0]
        first = [shifted(block, "energy", PHOT_BLOCKS) for block in left]
        second = [shifted(block, "energy", -PHOT_BLOCKS) for block in left]
        weights = [weight_low, weight_high]
    factors = jnp.stack([weight_0, flag, *weights, weights[1]])
    if count == 8:
        sides = [
            [(first[0], 0), (second[0], 0)],
            [(first[1], 0), (crossed, 0)],
            [(first[2], 0), (crossed, 2)],
            [(first[3], 0), (second[3], 0), (edge, 0)],
        ]
    else:
        sides = [[(low, 0), (high, 0)] for low, high in zip(first, second)]

    correlated = held_of(correlated, 17000000000)
    below = shifted(slab_coupling * correlated, "slab", 1)
    above = shifted(correlated, "slab", -1)
    phon_less, phon_great = correlated + below + slab_coupling * above

    out = None
    for together in ((0,), (1, 2), (3,)):
        segments = [(CHUNKS[n], left[n], sides[n]) for n in together]
        out = photon_of(segments, factors, dipole, phon_less[None], out)
    return out, phon_great[None, None]


def solution(mesh):
    return jax.shard_map(
        on_device,
        mesh=mesh,
        in_specs=(
            P("energy", "slab", None, None, None),
            P("energy", "slab", None),
            P("slab", None, None),
            P("energy", None),
            P("energy"),
            P(),
            P(),
            P("slab", None),
        ),
        out_specs=(P("energy", "slab", None, None, None), P("energy", "slab", None)),
        check_vma=False,
    )
```
